32 devices in a mesh: outer: 4 (over z), inner: 8 (over y, x, core).
Axes of the slice: x: 2, y: 2, z: 4, core: 2. Of those that a mesh axis runs over, the one named last changes fastest.
Arguments:
- target: bfloat16 [32768, 1024], P(('outer', 'inner')), may hold values from -6 to 6
- memory: bfloat16 [16384, 1024], P(('outer', 'inner')), may hold values from -6 to 6
- cotangent: bfloat16 [32768, 1024], P(('outer', 'inner')), may hold values from -6 to 6
- segment_ids: int32 [32, 1024], P(('outer', 'inner')), may hold values from 0 to 7, never falling along the last dimension, each value on 1 to 256 neighbouring positions
- memory_segments: int32 [32, 512], P(('outer', 'inner')), may hold values from 0 to 7, never falling along the last dimension, each value on 1 to 128 neighbouring positions
- directions: int32 [32, 8], P(('outer', 'inner')), may hold values from 0 to 15
- lang_table: bfloat16 [1024, 16], P(('outer', 'inner')), may hold values from -3 to 3
- self_qkv: bfloat16 [1024, 3072], P('inner', 'outer'), may hold values from -0.1875 to 0.1875
- self_out: bfloat16 [1024, 1024], P('inner', 'outer'), may hold values from -1.5 to 1.5
- cross_q: bfloat16 [1024, 1024], P('inner', 'outer'), may hold values from -0.1875 to 0.1875
- cross_kv: bfloat16 [1024, 2048], P('inner', 'outer'), may hold values from -0.1875 to 0.1875
- cross_out: bfloat16 [1024, 1024], P('inner', 'outer'), may hold values from -1.5 to 1.5
- ffn_in: bfloat16 [1024, 4096], P('inner', 'outer'), may hold values from -0.1875 to 0.1875
- ffn_in_bias: bfloat16 [4096], P(('outer', 'inner')), may hold values from -2 to 2
- ffn_out: bfloat16 [4096, 1024], P(('outer', 'inner')), may hold values from -0.09375 to 0.09375
- ffn_out_bias: bfloat16 [1024], P(('outer', 'inner')), may hold values from -2 to 2
- norm_gains: bfloat16 [1024, 3], P(('outer', 'inner')), may hold values from 0.5 to 1.5
- norm_biases: bfloat16 [1024, 3], P(('outer', 'inner')), may hold values from -2 to 2
Outputs:
- layer_output: bfloat16 [32768, 1024], P(('outer', 'inner'))
- target_grad: float32 [32768, 1024], P(('outer', 'inner'))
- memory_grad: float32 [16384, 1024], P(('outer', 'inner'))
- lang_table_grad: float32 [1024, 16], P(('outer', 'inner'))
- self_qkv_grad: float32 [1024, 3072], P('inner', 'outer')
- self_out_grad: float32 [1024, 1024], P('inner', 'outer')
- cross_q_grad: float32 [1024, 1024], P('inner', 'outer')
- cross_kv_grad: float32 [1024, 2048], P('inner', 'outer')
- cross_out_grad: float32 [1024, 1024], P('inner', 'outer')
- ffn_in_grad: float32 [1024, 4096], P('inner', 'outer')
- ffn_in_bias_grad: float32 [4096], P(('outer', 'inner'))
- ffn_out_grad: float32 [4096, 1024], P(('outer', 'inner'))
- ffn_out_bias_grad: float32 [1024], P(('outer', 'inner'))
- norm_gains_grad: float32 [1024, 3], P(('outer', 'inner'))
- norm_biases_grad: float32 [1024, 3], P(('outer', 'inner'))
The draws below stay inside these ranges and needn't reach their ends.
Inputs may be any that keep to these rules, and one draw needn't show every extreme that they name: `segment_ids`: along each row the ids never fall and every id of 0 to 7 occurs, at most 1024 / 4 times, exactly that often for one of them. `memory_segments`: along each row the ids never fall and every id of 0 to 7 occurs, at most 512 / 4 times, exactly that often for one of them.
All inputs are finite; a program needn't handle non-finite values.
Results may differ from the reference program's by a relative error of at most 0.017.
The reference program's roundings to bfloat16 on the way count: a program that leaves them out, or rounds other values in their place, can miss the bound.
Values may be sent and summed in bfloat16 or wider, within the bound.
No kernel may reach another device: no remote copies, remote signals or barrier semaphores. Data moves between devices by JAX's collectives and lax.ppermute only.
A program may use at most 256 MiB of HBM per device.

```python
import math
import jax
import jax.numpy as jnp
import numpy as np
from jax import lax

D = 1024
FF = 4096
HEADS = 16
HEAD_DIM = 64
LANGS = 16
SEGS = 8
ROW_LEN = 1024
MEM_LEN = 512
ROWS = 32
TOKENS = 32768
MEM_TOKENS = 16384


def place_ends(values, own_key, smallest, top_value):
    spot = [jax.random.randint(jax.random.fold_in(own_key, axis), (), 0, length) for axis, length in enumerate(values.shape)]
    longest = values.shape.index(max(values.shape))
    next_to = spot[:longest] + [(spot[longest] + 1) % values.shape[longest]] + spot[longest + 1:]
    return values.at[tuple(spot)].set(smallest).at[tuple(next_to)].set(top_value)


def steps_of(key, extent, shards, smallest, top_value):
    def one(axis_at, blocks):
        heights = jax.random.uniform(jax.random.fold_in(jax.random.fold_in(key, 6), axis_at), (blocks,), jnp.float32, smallest / len(shards), top_value / len(shards))
        return jnp.repeat(jnp.exp(heights), extent[axis_at] // blocks).reshape((-1,) + (1,) * (len(extent) - axis_at - 1))

    factor_of = one(*shards[0])
    for cut in shards[1:]:
        factor_of = factor_of * one(*cut)
    return factor_of


def split_up(count, total, reach, slope):
    portions = [(1 << 20) // math.isqrt(standing ** slope) + 1 for standing in range(2, count + 1)]
    spare, given = total - reach - (count - 1), [1] * (count - 1)
    while spare > 0:
        movable = [i for i in range(count - 1) if given[i] < reach]
        whole, budget = sum([portions[i] for i in movable]), spare
        for i in movable:
            more = min(reach - given[i], max(1, budget * portions[i] // whole), spare)
            given[i] = given[i] + more
            spare = spare - more
    return np.array([reach] + given)


def uneven(rng, amount, total, reach, lean):
    if amount == 2:
        one = jax.random.randint(rng, (), max(1, total - reach), min(reach, total - 1) + 1)
        return jnp.stack([one, total - one])
    sizes = jnp.asarray(split_up(amount, total, reach, lean), jnp.int32)
    couples = (amount - 1) // 2
    source_of, sink = sizes[1:1 + 2 * couples:2], sizes[2:2 + 2 * couples:2]
    margin = jnp.minimum(source_of - 1, reach - sink)
    shifted = jax.random.randint(jax.random.fold_in(rng, 1), (couples,), 0, 1 << 20) % (margin + 1)
    sizes = sizes.at[1:1 + 2 * couples:2].set(source_of - shifted).at[2:2 + 2 * couples:2].set(sink + shifted)
    return sizes[jax.random.permutation(jax.random.fold_in(rng, 2), amount)]


def noise(rng, shape, scale, most, pieces=(), held_as=jnp.bfloat16):
    loudness = steps_of(rng, shape, pieces, -0.22, 0.18) if pieces else 1.0
    values = jax.random.normal(rng, shape, jnp.float32) * scale * loudness
    return jnp.minimum(jnp.maximum(values, -most), most).astype(held_as)


def setup_inputs(seed: int = 0) -> dict:
    keys = jax.random.split(jax.random.key(seed), 19)
    target = noise(keys[0], (TOKENS, D), 1.0, 6.0, ((0, 32),))
    memory = noise(keys[1], (MEM_TOKENS, D), 1.0, 6.0, ((0, 32),))
    cotangent = noise(keys[2], (TOKENS, D), 1.0, 6.0, ((0, 32),))
    segment_ids = jax.vmap(lambda own: jnp.searchsorted(jnp.cumsum(uneven(own, SEGS, ROW_LEN, ROW_LEN // 4, 1)), jnp.arange(ROW_LEN), side="right"))(jax.random.split(keys[3], ROWS)).reshape((ROWS, ROW_LEN)).astype(jnp.int32)
    memory_segments = jax.vmap(lambda own: jnp.searchsorted(jnp.cumsum(uneven(own, SEGS, MEM_LEN, MEM_LEN // 4, 1)), jnp.arange(MEM_LEN), side="right"))(jax.random.split(keys[4], ROWS)).reshape((ROWS, MEM_LEN)).astype(jnp.int32)
    directions = place_ends(jax.random.randint(keys[5], (ROWS, SEGS), 0, LANGS), jax.random.fold_in(keys[5], 1), 0, LANGS - 1).astype(jnp.int32)
    lang_table = noise(keys[6], (D, LANGS), 0.5, 3.0, ((0, 32),))
    self_qkv = noise(keys[7], (D, 3 * D), D ** -0.5, 0.1875, ((0, 8), (1, 4)))
    self_out = noise(keys[8], (D, D), (D // 64) ** -0.5, 1.5, ((0, 8), (1, 4)))
    cross_q = noise(keys[9], (D, D), D ** -0.5, 0.1875, ((0, 8), (1, 4)))
    cross_kv = noise(keys[10], (D, 2 * D), D ** -0.5, 0.1875, ((0, 8), (1, 4)))
    cross_out = noise(keys[11], (D, D), (D // 64) ** -0.5, 1.5, ((0, 8), (1, 4)))
    ffn_in = noise(keys[12], (D, FF), D ** -0.5, 0.1875, ((0, 8), (1, 4)))
    ffn_in_bias = noise(keys[13], (FF,), 0.3, 2.0, ((0, 32),))
    ffn_out = noise(keys[14], (FF, D), FF ** -0.5, 0.09375, ((0, 32),))
    ffn_out_bias = noise(keys[15], (D,), 0.3, 2.0, ((0, 32),))
    norm_gains = jnp.clip(1.0 + 0.1 * jax.random.normal(keys[16], (D, 3), jnp.float32), 0.5, 1.5).astype(jnp.bfloat16)
    norm_biases = noise(keys[17], (D, 3), 0.3, 2.0, ((0, 32),))
    return {"target": target, "memory": memory, "cotangent": cotangent, "segment_ids": segment_ids, "memory_segments": memory_segments, "directions": directions, "lang_table": lang_table, "self_qkv": self_qkv, "self_out": self_out, "cross_q": cross_q, "cross_kv": cross_kv, "cross_out": cross_out, "ffn_in": ffn_in, "ffn_in_bias": ffn_in_bias, "ffn_out": ffn_out, "ffn_out_bias": ffn_out_bias, "norm_gains": norm_gains, "norm_biases": norm_biases}


epsilon = 1e-05
residual_scale = 2.0
masked_score = -1000000000.0

@jax.custom_vjp
def low(v):
    return lax.optimization_barrier(v.astype(jnp.bfloat16)).astype(jnp.float32)

@jax.custom_vjp
def low_back(v):
    return v

def low_keep(v):
    return (low(v), None)

def low_pass(kept, grad):
    return (grad,)

def back_keep(v):
    return (v, None)

def back_low(kept, grad):
    return (low(grad),)
low.defvjp(low_keep, low_pass)
low_back.defvjp(back_keep, back_low)

def layer_norm(matrix, gain_vec, shift_vec):
    row_mean = lax.optimization_barrier(jnp.mean(matrix, axis=-1, keepdims=True))
    centred = matrix - row_mean
    row_var = lax.optimization_barrier(jnp.mean(centred * centred, axis=-1, keepdims=True))
    return centred * lax.rsqrt(row_var + epsilon) * gain_vec + shift_vec

def product(left_side, right_side):
    return jnp.dot(left_side, right_side, precision=lax.Precision.HIGHEST)

def attend(queries, keys_all, values_all, allowed):
    length = queries.shape[0]
    memory_length = keys_all.shape[0]
    query_heads = queries.reshape(length, HEADS, HEAD_DIM)
    key_heads = keys_all.reshape(memory_length, HEADS, HEAD_DIM)
    value_heads = values_all.reshape(memory_length, HEADS, HEAD_DIM)
    scores = jnp.einsum('qhd,khd->hqk', query_heads, key_heads, precision=lax.Precision.HIGHEST) * HEAD_DIM ** (-0.5)
    scores = low_back(jnp.where(allowed[None], scores, masked_score))
    probs_low = low(jax.nn.softmax(scores, axis=-1))
    mixed_heads = jnp.einsum('hqk,khd->qhd', probs_low, value_heads, precision=lax.Precision.HIGHEST)
    return low(low_back(mixed_heads.reshape(length, HEADS * HEAD_DIM)))

def decoder_layer(target_row, memory_row, params, segment_row, memory_seg_row, direction_row):
    lang_table, self_qkv, self_out, cross_q, cross_kv, cross_out, ffn_in, ffn_in_bias, ffn_out, ffn_out_bias, norm_gains, norm_biases = params
    length = target_row.shape[0]
    model_width = target_row.shape[1]
    positions = jnp.arange(length)
    own_causal = (positions[:, None] >= positions[None, :]) & (segment_row[:, None] == segment_row[None, :])
    across = segment_row[:, None] == memory_seg_row[None, :]
    token_dir = direction_row[segment_row]
    start = target_row + jnp.take(lang_table, token_dir, axis=1).T
    self_entry = low(start)
    triple = low(low_back(product(self_entry, self_qkv)))
    self_mix = attend(triple[:, :model_width], triple[:, model_width:2 * model_width], triple[:, 2 * model_width:], own_causal)
    first = layer_norm(residual_scale * start + low_back(product(self_mix, self_out)), norm_gains[:, 0], norm_biases[:, 0])
    cross_entry = low(first)
    cross_queries = low(low_back(product(cross_entry, cross_q)))
    cross_pairs = low(low_back(product(memory_row, cross_kv)))
    cross_mix = attend(cross_queries, cross_pairs[:, :model_width], cross_pairs[:, model_width:], across)
    second = layer_norm(residual_scale * first + low_back(product(cross_mix, cross_out)), norm_gains[:, 1], norm_biases[:, 1])
    ffn_entry = low(second)
    hidden_pre = low_back(product(ffn_entry, ffn_in) + ffn_in_bias)
    hidden_act = low(jax.nn.gelu(hidden_pre, approximate=False))
    ffn_branch = low_back(product(hidden_act, ffn_out) + ffn_out_bias)
    return layer_norm(residual_scale * second + ffn_branch, norm_gains[:, 2], norm_biases[:, 2])

def reference(target, memory, cotangent, segment_ids, memory_segments, directions, lang_table, self_qkv, self_out, cross_q, cross_kv, cross_out, ffn_in, ffn_in_bias, ffn_out, ffn_out_bias, norm_gains, norm_biases):
    weights = tuple((weight_arg.astype(jnp.float32) for weight_arg in (lang_table, self_qkv, self_out, cross_q, cross_kv, cross_out, ffn_in, ffn_in_bias, ffn_out, ffn_out_bias, norm_gains, norm_biases)))
    model_width = target.shape[1]
    target_rows = target.astype(jnp.float32).reshape(segment_ids.shape[0], segment_ids.shape[1], model_width)
    memory_rows = memory.astype(jnp.float32).reshape(memory_segments.shape[0], memory_segments.shape[1], model_width)
    cotangent_rows = cotangent.astype(jnp.float32).reshape(target_rows.shape)

    def one_row(totals, row_items):
        target_row, memory_row, cot_row, segment_row, memory_seg_row, direction_row = row_items

        def apply_layer(target_in, memory_in, params):
            return decoder_layer(target_in, memory_in, params, segment_row, memory_seg_row, direction_row)
        layer_out, pull_back = jax.vjp(apply_layer, target_row, memory_row, weights)
        grad_target, grad_memory, grad_weights = pull_back(cot_row)
        totals = jax.tree.map(jnp.add, totals, grad_weights)
        return (totals, (layer_out.astype(jnp.bfloat16), grad_target, grad_memory))
    zeros_init = jax.tree.map(jnp.zeros_like, weights)
    totals, row_results = lax.scan(one_row, zeros_init, (target_rows, memory_rows, cotangent_rows, segment_ids, memory_segments, directions))
    outputs, grad_targets, grad_memories = row_results
    return (outputs.reshape(target.shape), grad_targets.reshape(target.shape), grad_memories.reshape(memory.shape), totals[0], totals[1], totals[2], totals[3], totals[4], totals[5], totals[6], totals[7], totals[8], totals[9], totals[10], totals[11])
```

```python
import functools

import jax
import jax.numpy as jnp
from jax import lax
from jax.experimental import pallas as pl
from jax.experimental.pallas import tpu as pltpu
from jax.sharding import PartitionSpec as P

HEADS = 16
HEAD_DIM = 64
GROUP = 4
BLOCK = 256
WINDOW = 512

epsilon = 1e-05
masked_score = -1000000000.0
bf16 = jnp.bfloat16
f32 = jnp.float32
both = ("outer", "inner")
MIB = 1 << 20


def mm(left, right):
    return lax.dot_general(left, right, (((1,), (0,)), ((), ())), preferred_element_type=f32)


def mm_nt(left, right):
    return lax.dot_general(left, right, (((1,), (1,)), ((), ())), preferred_element_type=f32)


def params():
    return pltpu.CompilerParams(vmem_limit_bytes=60 * MIB)


def cost(flops, moved, trans=0):
    share = 64
    return pl.CostEstimate(
        flops=int(flops) // share, bytes_accessed=int(moved) // share, transcendentals=int(trans) // share
    )


def whole(shape):
    return pl.BlockSpec(shape, lambda *_: (0,) * len(shape), pipeline_mode=pl.Buffered(1))


def weight_step(model, width, at):
    return pl.BlockSpec((1, model, width), lambda o, *_: (o, 0, at))


def weight_block(packed, width, at):
    outer, model, _ = packed.shape
    return pl.BlockSpec(
        (outer, model, width), lambda *_: (0, 0, at), pipeline_mode=pl.Buffered(1)
    )


def normalise(matrix):
    centred = matrix - jnp.mean(matrix, axis=-1, keepdims=True)
    rstd = lax.rsqrt(jnp.mean(centred * centred, axis=-1, keepdims=True) + epsilon)
    return centred * rstd, rstd


def norm_back(grad, gain, normed, rstd):
    scaled = grad * gain
    mean_scaled = jnp.mean(scaled, axis=-1, keepdims=True)
    mean_product = jnp.mean(scaled * normed, axis=-1, keepdims=True)
    return (scaled - mean_scaled - normed * mean_product) * rstd


def column_sum(matrix):
    return jnp.sum(matrix, axis=0, keepdims=True)


def triple_kernel(target_ref, token_ref, lang_ref, weight_ref, out_ref):
    start = target_ref[...].astype(f32) + mm(token_ref[...], lang_ref[...])
    out_ref[...] = mm(start.astype(bf16), weight_ref[0]).astype(bf16)


def triple_call(target, token_hot, lang_rows, packed, width, at):
    tokens, model = target.shape
    outer = packed.shape[0]
    step = tokens // 2
    return pl.pallas_call(
        triple_kernel,
        grid=(outer, 2),
        in_specs=[
            pl.BlockSpec((step, model), lambda o, r: (r, 0)),
            pl.BlockSpec((step, 128), lambda o, r: (r, 0)),
            pl.BlockSpec((128, model), lambda o, r: (0, 0)),
            weight_step(model, width, at),
        ],
        out_specs=pl.BlockSpec((step, width), lambda o, r: (r, o)),
        out_shape=jax.ShapeDtypeStruct((tokens, outer * width), bf16),
        compiler_params=params(),
        cost_estimate=cost(2 * tokens * model * outer * width, 16 * MIB),
        name="triple",
    )(target, token_hot, lang_rows, packed)


def pairs_kernel(memory_ref, weight_ref, out_ref):
    out_ref[...] = mm(memory_ref[...], weight_ref[0]).astype(bf16)


def pairs_call(memory, packed, width, at):
    tokens, model = memory.shape
    outer = packed.shape[0]
    return pl.pallas_call(
        pairs_kernel,
        grid=(outer,),
        in_specs=[
            pl.BlockSpec((tokens, model), lambda o: (0, 0)),
            weight_step(model, width, at),
        ],
        out_specs=pl.BlockSpec((tokens, width), lambda o: (0, o)),
        out_shape=jax.ShapeDtypeStruct((tokens, outer * width), bf16),
        compiler_params=params(),
        cost_estimate=cost(2 * tokens * model * outer * width, 8 * MIB),
        name="pairs",
    )(memory, packed)


def mask_bias(own_ref, other_ref, start, window, causal):
    block = own_ref.shape[0]
    allowed = own_ref[...] == other_ref[:, pl.ds(start, window)]
    if causal:
        own_at = pl.program_id(0) * block + lax.broadcasted_iota(jnp.int32, (block, window), 0)
        other_at = start + lax.broadcasted_iota(jnp.int32, (block, window), 1)
        allowed = allowed & (own_at >= other_at)
    return jnp.where(allowed, 0.0, masked_score).astype(f32)


def window_start(block_index, causal):
    if not causal:
        return 0
    return pl.multiple_of(jnp.maximum(block_index - 1, 0) * BLOCK, BLOCK)


def attend_kernel(causal, window, q_ref, k_ref, v_ref, own_ref, other_ref, mix_ref, level_ref, bias_ref):
    start = window_start(pl.program_id(0), causal)
    group = pl.program_id(1)

    @pl.when(group == 0)
    def _():
        bias_ref[...] = mask_bias(own_ref, other_ref, start, window, causal)
        level_ref[...] = jnp.zeros_like(level_ref)

    width = q_ref.shape[1]
    owner = lax.broadcasted_iota(jnp.int32, (1, width), 1) // HEAD_DIM
    lane = lax.broadcasted_iota(jnp.int32, (1, 128), 1)
    queries = q_ref[...] * bf16(HEAD_DIM ** -0.5)
    keys = k_ref[pl.ds(start, window), :]
    values = v_ref[pl.ds(start, window), :]
    mix = jnp.zeros(q_ref.shape, f32)
    levels = level_ref[...]
    for head in range(GROUP):
        chosen = owner == head
        scores = mm_nt(queries * chosen.astype(bf16), keys) + bias_ref[...]
        row_max = jnp.max(scores, axis=-1, keepdims=True)
        exps = jnp.exp(scores - row_max)
        total = jnp.sum(exps, axis=-1, keepdims=True)
        probs = (exps * (1.0 / total)).astype(bf16)
        mix = jnp.where(chosen, mm(probs, values), mix)
        levels = jnp.where(lane == group * GROUP + head, row_max + jnp.log(total), levels)
    mix_ref[...] = mix.astype(bf16)
    level_ref[...] = levels


def attend_call(q_array, q_at, k_array, k_at, v_array, v_at, own_column, other_row, causal):
    tokens, others = q_array.shape[0], k_array.shape[0]
    width = GROUP * HEAD_DIM
    model = HEADS * HEAD_DIM
    return pl.pallas_call(
        functools.partial(attend_kernel, causal, WINDOW),
        grid=(tokens // BLOCK, HEADS // GROUP),
        in_specs=[
            pl.BlockSpec((BLOCK, width), lambda b, g: (b, q_at + g)),
            pl.BlockSpec((others, width), lambda b, g: (0, k_at + g)),
            pl.BlockSpec((others, width), lambda b, g: (0, v_at + g)),
            pl.BlockSpec((BLOCK, 1), lambda b, g: (b, 0)),
            pl.BlockSpec((1, others), lambda b, g: (0, 0)),
        ],
        out_specs=[
            pl.BlockSpec((BLOCK, width), lambda b, g: (b, g)),
            pl.BlockSpec((BLOCK, 128), lambda b, g: (b, 0)),
        ],
        out_shape=[
            jax.ShapeDtypeStruct((tokens, model), bf16),
            jax.ShapeDtypeStruct((tokens, 128), f32),
        ],
        scratch_shapes=[pltpu.VMEM((BLOCK, WINDOW), f32)],
        compiler_params=params(),
        cost_estimate=cost(16e9, 12 * MIB, HEADS * tokens * WINDOW),
        name="attend",
    )(q_array, k_array, v_array, own_column, other_row)


def attend_back_kernel(
    causal, joined, q_ref, k_ref, v_ref, grad_ref, level_ref, own_ref, other_ref, *rest
):
    if joined:
        out_ref, keys_t, values_t = rest
    else:
        out_ref, pair_ref, keys_t, values_t = rest
    block_index = pl.program_id(0)
    group = pl.program_id(1)
    blocks = pl.num_programs(0)
    start = window_start(block_index, causal)
    window = WINDOW
    width = q_ref.shape[1]
    model = HEADS * HEAD_DIM
    rows = pl.ds(pl.multiple_of(group * width, width), width)

    @pl.when(block_index == 0)
    def _():
        keys_t[rows, :] = jnp.zeros((width, keys_t.shape[1]), f32)
        values_t[rows, :] = jnp.zeros((width, keys_t.shape[1]), f32)

    bias = mask_bias(own_ref, other_ref, start, window, causal)
    owner = lax.broadcasted_iota(jnp.int32, (1, width), 1) // HEAD_DIM
    lane = lax.broadcasted_iota(jnp.int32, (1, 128), 1)
    queries = q_ref[...] * bf16(HEAD_DIM ** -0.5)
    grads = grad_ref[...]
    queries_t = queries.T
    grads_t = grads.T
    keys = k_ref[pl.ds(start, window), :]
    values = v_ref[pl.ds(start, window), :]
    levels = level_ref[...]
    grad_q = jnp.zeros(q_ref.shape, f32)
    spot = pl.ds(start, window)
    for head in range(GROUP):
        chosen = owner == head
        picked = chosen.astype(bf16)
        scores = mm_nt(queries * picked, keys) + bias
        level = jnp.sum(
            jnp.where(lane == group * GROUP + head, levels, 0.0), axis=-1, keepdims=True
        )
        probs = jnp.exp(scores - level)
        grad_probs = mm_nt(grads * picked, values)
        inner = jnp.sum(probs * grad_probs, axis=-1, keepdims=True)
        grad_scores = (probs * (grad_probs - inner)).astype(bf16)
        band = slice(head * HEAD_DIM, (head + 1) * HEAD_DIM)
        target_rows = pl.ds(pl.multiple_of(group * width + head * HEAD_DIM, HEAD_DIM), HEAD_DIM)
        values_t[target_rows, spot] += mm(grads_t[band, :], probs.astype(bf16))
        keys_t[target_rows, spot] += mm(queries_t[band, :], grad_scores)
        grad_q = jnp.where(chosen, mm(grad_scores, keys), grad_q)
    grad_q = (grad_q * HEAD_DIM ** -0.5).astype(bf16)
    own_rows = pl.ds(pl.multiple_of(block_index * BLOCK, BLOCK), BLOCK)
    columns = pl.multiple_of(group * width, width)
    out_ref[own_rows, pl.ds(columns, width)] = grad_q
    other_ref_out, shift = (out_ref, model) if joined else (pair_ref, 0)

    @pl.when(block_index == blocks - 1)
    def _():
        other_ref_out[:, pl.ds(columns + shift, width)] = keys_t[rows, :].T.astype(bf16)
        other_ref_out[:, pl.ds(columns + shift + model, width)] = values_t[rows, :].T.astype(bf16)


def attend_back_call(
    q_array, q_at, k_array, k_at, v_array, v_at, grad_mix, levels, own_column, other_row, causal
):
    tokens, others = q_array.shape[0], k_array.shape[0]
    width = GROUP * HEAD_DIM
    model = HEADS * HEAD_DIM
    if causal:
        out_shape = [jax.ShapeDtypeStruct((tokens, 3 * model), bf16)]
    else:
        out_shape = [
            jax.ShapeDtypeStruct((tokens, model), bf16),
            jax.ShapeDtypeStruct((others, 2 * model), bf16),
        ]
    return pl.pallas_call(
        functools.partial(attend_back_kernel, causal, causal),
        grid=(tokens // BLOCK, HEADS // GROUP),
        in_specs=[
            pl.BlockSpec((BLOCK, width), lambda b, g: (b, q_at + g)),
            pl.BlockSpec((others, width), lambda b, g: (0, k_at + g)),
            pl.BlockSpec((others, width), lambda b, g: (0, v_at + g)),
            pl.BlockSpec((BLOCK, width), lambda b, g: (b, g)),
            pl.BlockSpec((BLOCK, 128), lambda b, g: (b, 0)),
            pl.BlockSpec((BLOCK, 1), lambda b, g: (b, 0)),
            pl.BlockSpec((1, others), lambda b, g: (0, 0)),
        ],
        out_specs=[whole(item.shape) for item in out_shape],
        out_shape=out_shape,
        scratch_shapes=[pltpu.VMEM((model, others), f32), pltpu.VMEM((model, others), f32)],
        compiler_params=params(),
        cost_estimate=cost(40e9, 16 * MIB, HEADS * tokens * WINDOW),
        name="attend_back",
    )(q_array, k_array, v_array, grad_mix, levels, own_column, other_row)


def middle_kernel(
    mix_ref, target_ref, token_ref, lang_ref, vec_ref, out_weight_ref, query_weight_ref,
    normed_ref, rstd_ref, entry_ref, queries_ref,
):
    outer, _, width = out_weight_ref.shape
    start = target_ref[...].astype(f32) + mm(token_ref[...], lang_ref[...])
    mix = mix_ref[...]
    branch = jnp.concatenate([mm(mix, out_weight_ref[o]) for o in range(outer)], axis=1)
    normed, rstd = normalise(2.0 * start + branch)
    normed_ref[...] = normed
    rstd_ref[...] = rstd
    entry = (normed * vec_ref[0:1, :] + vec_ref[3:4, :]).astype(bf16)
    entry_ref[...] = entry
    for o in range(outer):
        queries_ref[:, o * width:(o + 1) * width] = mm(entry, query_weight_ref[o]).astype(bf16)


def middle_call(mix, target, token_hot, lang_rows, vec, packed, at_self, at_cross, width):
    tokens, model = target.shape
    row = lambda r: (r, 0)
    return pl.pallas_call(
        middle_kernel,
        grid=(tokens // BLOCK,),
        in_specs=[
            pl.BlockSpec((BLOCK, model), row),
            pl.BlockSpec((BLOCK, model), row),
            pl.BlockSpec((BLOCK, 128), row),
            whole(lang_rows.shape),
            whole(vec.shape),
            weight_block(packed, width, at_self),
            weight_block(packed, width, at_cross),
        ],
        out_specs=[
            pl.BlockSpec((BLOCK, model), row),
            pl.BlockSpec((BLOCK, 1), row),
            pl.BlockSpec((BLOCK, model), row),
            pl.BlockSpec((BLOCK, model), row),
        ],
        out_shape=[
            jax.ShapeDtypeStruct((tokens, model), f32),
            jax.ShapeDtypeStruct((tokens, 1), f32),
            jax.ShapeDtypeStruct((tokens, model), bf16),
            jax.ShapeDtypeStruct((tokens, model), bf16),
        ],
        compiler_params=params(),
        cost_estimate=cost(4 * tokens * model * model, 16 * MIB),
        name="middle",
    )(mix, target, token_hot, lang_rows, vec, packed, packed)


def feed_kernel(
    at_cross, at_in, at_out,
    mix_ref, normed_ref, cot_ref, vec_ref, bias_ref, cross_hbm, in_hbm, out_hbm,
    layer_ref, entry_ref, act_ref, branch_grad_ref, pre_grad_ref, residual_ref, cross_grad_ref,
    mix_grad_ref, sums_ref, bias_sum_ref,
    cross_weight, in_weight, out_weight, slope, sems,
):
    outer, _, width = cross_weight.shape
    chunk = in_weight.shape[2]
    step = pl.program_id(0)

    def cross_copy():
        return pltpu.make_async_copy(
            cross_hbm.at[:, :, pl.ds(at_cross, width)], cross_weight, sems.at[0]
        )

    def in_copy(o):
        return pltpu.make_async_copy(
            in_hbm.at[o, :, pl.ds(at_in, chunk)], in_weight.at[o], sems.at[1 + o]
        )

    def out_copy(o):
        return pltpu.make_async_copy(
            out_hbm.at[o, :, pl.ds(at_out, out_weight.shape[2])], out_weight.at[o],
            sems.at[1 + outer + o],
        )


    @pl.when(step == 0)
    def _():
        cross_copy().start()
        for o in range(outer):
            in_copy(o).start()
            out_copy(o).start()
        sums_ref[...] = jnp.zeros_like(sums_ref)
        bias_sum_ref[...] = jnp.zeros_like(bias_sum_ref)
        cross_copy().wait()

    gain0, gain1, gain2 = vec_ref[0:1, :], vec_ref[1:2, :], vec_ref[2:3, :]
    shift0, shift1, shift2 = vec_ref[3:4, :], vec_ref[4:5, :], vec_ref[5:6, :]
    first = normed_ref[...] * gain0 + shift0
    mix = mix_ref[...]
    branch = jnp.concatenate([mm(mix, cross_weight[o]) for o in range(outer)], axis=1)
    normed1, rstd1 = normalise(2.0 * first + branch)
    second = normed1 * gain1 + shift1
    entry = second.astype(bf16)
    entry_ref[...] = entry
    total = 2.0 * second + vec_ref[6:7, :]
    for o in range(outer):
        @pl.when(step == 0)
        def _():
            in_copy(o).wait()
            out_copy(o).wait()

        span = slice(o * chunk, (o + 1) * chunk)
        pre = mm(entry, in_weight[o]) + bias_ref[:, span]
        half = 0.5 + 0.5 * lax.erf(pre * (0.5 ** 0.5))
        slope[:, span] = half + pre * (jnp.exp(-0.5 * pre * pre) * 0.3989422804014327)
        act = (pre * half).astype(bf16)
        act_ref[:, span] = act
        total = total + mm(act, out_weight[o])
    normed2, rstd2 = normalise(total)
    layer_ref[...] = (normed2 * gain2 + shift2).astype(bf16)
    cot = cot_ref[...].astype(f32)
    sums_ref[0:1, :] += column_sum(cot * normed2)
    sums_ref[1:2, :] += column_sum(cot)
    back2 = norm_back(cot, gain2, normed2, rstd2)
    branch_grad = back2.astype(bf16)
    branch_grad_ref[...] = branch_grad
    sums_ref[2:3, :] += column_sum(branch_grad.astype(f32))
    grad_second = 2.0 * back2
    for o in range(outer):
        span = slice(o * chunk, (o + 1) * chunk)
        pre_grad = (mm_nt(branch_grad, out_weight[o]) * slope[:, span]).astype(bf16)
        pre_grad_ref[:, span] = pre_grad
        bias_sum_ref[:, span] += column_sum(pre_grad.astype(f32))
        grad_second = grad_second + mm_nt(pre_grad, in_weight[o])
    sums_ref[3:4, :] += column_sum(grad_second * normed1)
    sums_ref[4:5, :] += column_sum(grad_second)
    back1 = norm_back(grad_second, gain1, normed1, rstd1)
    residual_ref[...] = back1
    cross_grad = back1.astype(bf16)
    cross_grad_ref[...] = cross_grad
    mix_grad = mm_nt(cross_grad[:, 0:width], cross_weight[0])
    for o in range(1, outer):
        mix_grad = mix_grad + mm_nt(
            cross_grad[:, o * width:(o + 1) * width], cross_weight[o]
        )
    mix_grad_ref[...] = mix_grad.astype(bf16)


def feed_call(mix, normed, cot, vec, bias, packed_cross, at_cross, packed_in, at_in, packed_out, at_out, width):
    tokens, model = mix.shape
    hidden = bias.shape[1]
    outer = packed_cross.shape[0]
    chunk = hidden // outer
    row = lambda r: (r, 0)
    blocked = lambda cols: pl.BlockSpec((BLOCK, cols), row)
    anywhere = pl.BlockSpec(memory_space=pl.ANY)
    out = lambda cols, kind: jax.ShapeDtypeStruct((tokens, cols), kind)
    return pl.pallas_call(
        functools.partial(feed_kernel, at_cross, at_in, at_out),
        grid=(tokens // BLOCK,),
        in_specs=[
            blocked(model), blocked(model), blocked(model),
            whole(vec.shape), whole(bias.shape), anywhere, anywhere, anywhere,
        ],
        out_specs=[
            blocked(model), blocked(model), blocked(hidden), blocked(model), blocked(hidden),
            blocked(model), blocked(model), blocked(model),
            pl.BlockSpec((8, model), lambda r: (0, 0)),
            pl.BlockSpec((1, hidden), lambda r: (0, 0)),
        ],
        out_shape=[
            out(model, bf16), out(model, bf16), out(hidden, bf16), out(model, bf16),
            out(hidden, bf16), out(model, f32), out(model, bf16), out(model, bf16),
            jax.ShapeDtypeStruct((8, model), f32),
            jax.ShapeDtypeStruct((1, hidden), f32),
        ],
        scratch_shapes=[
            pltpu.VMEM((outer, model, width), bf16),
            pltpu.VMEM((outer, model, chunk), bf16),
            pltpu.VMEM((outer, chunk, model), bf16),
            pltpu.VMEM((BLOCK, hidden), f32),
            pltpu.SemaphoreType.DMA((1 + 2 * outer,)),
        ],
        compiler_params=params(),
        cost_estimate=cost(36 * tokens * model * model, 60 * MIB, tokens * hidden * 2),
        name="feed",
    )(mix, normed, cot, vec, bias, packed_cross, packed_in, packed_out)


def middle_back_kernel(
    residual_ref, queries_grad_ref, normed_ref, rstd_ref, vec_ref, query_weight_ref, out_weight_ref,
    start_ref, branch_grad_ref, mix_grad_ref, sums_ref,
):
    outer, _, width = out_weight_ref.shape

    @pl.when(pl.program_id(0) == 0)
    def _():
        sums_ref[...] = jnp.zeros_like(sums_ref)

    grad_first = 2.0 * residual_ref[...]
    for o in range(outer):
        grad_first = grad_first + mm_nt(
            queries_grad_ref[:, o * width:(o + 1) * width], query_weight_ref[o]
        )
    normed = normed_ref[...]
    sums_ref[0:1, :] += column_sum(grad_first * normed)
    sums_ref[1:2, :] += column_sum(grad_first)
    back = norm_back(grad_first, vec_ref[0:1, :], normed, rstd_ref[...])
    start_ref[...] = back
    branch_grad = back.astype(bf16)
    branch_grad_ref[...] = branch_grad
    mix_grad = mm_nt(branch_grad[:, 0:width], out_weight_ref[0])
    for o in range(1, outer):
        mix_grad = mix_grad + mm_nt(
            branch_grad[:, o * width:(o + 1) * width], out_weight_ref[o]
        )
    mix_grad_ref[...] = mix_grad.astype(bf16)


def middle_back_call(residual, queries_grad, normed, rstd, vec, packed, at_cross, at_self, width):
    tokens, model = residual.shape
    row = lambda r: (r, 0)
    blocked = pl.BlockSpec((BLOCK, model), row)
    return pl.pallas_call(
        middle_back_kernel,
        grid=(tokens // BLOCK,),
        in_specs=[
            blocked, blocked, blocked,
            pl.BlockSpec((BLOCK, 1), row),
            whole(vec.shape),
            weight_block(packed, width, at_cross),
            weight_block(packed, width, at_self),
        ],
        out_specs=[blocked, blocked, blocked, pl.BlockSpec((8, model), lambda r: (0, 0))],
        out_shape=[
            jax.ShapeDtypeStruct((tokens, model), f32),
            jax.ShapeDtypeStruct((tokens, model), bf16),
            jax.ShapeDtypeStruct((tokens, model), bf16),
            jax.ShapeDtypeStruct((8, model), f32),
        ],
        compiler_params=params(),
        cost_estimate=cost(4 * tokens * model * model, 22 * MIB),
        name="middle_back",
    )(residual, queries_grad, normed, rstd, vec, packed, packed)


def fill_product(table_ref, left_t, right_ref, lo, hi, out_refs):
    piece, width = out_refs[0].shape[2:]
    inner = left_t.shape[0] // piece
    part = inner // len(out_refs)
    count = min(BLOCK // piece, part)
    for at, out_ref in enumerate(out_refs):
        @pl.loop(0, part // count)
        def _(m):
            blocks = [
                left_t[pl.ds(pl.multiple_of(table_ref[at * part + m * count + k] * piece, piece), piece), :]
                for k in range(count)
            ]
            product = mm(jnp.concatenate(blocks, axis=0), right_ref[:, lo:hi]).astype(bf16)
            out_ref[pl.ds(m * count, count), 0] = product.reshape(count, piece, width)


def split_refs(rest, outputs):
    return rest[-outputs - 1:-1], rest[-1]


def weight_kernel(outputs, lo, hi, table_ref, left_ref, right_ref, *rest):
    out_refs, left_t = split_refs(rest, outputs)

    @pl.when(pl.program_id(0) == 0)
    def _():
        left_t[...] = left_ref[...].T

    fill_product(table_ref, left_t, right_ref, lo, hi, out_refs)


def entry_weight_kernel(outputs, lo, hi, table_ref, target_ref, token_ref, lang_ref, right_ref, *rest):
    out_refs, left_t = split_refs(rest, outputs)

    @pl.when(pl.program_id(0) == 0)
    def _():
        start = target_ref[...].astype(f32) + mm(token_ref[...], lang_ref[...])
        left_t[...] = start.astype(bf16).T

    fill_product(table_ref, left_t, right_ref, lo, hi, out_refs)


def rows_weight_kernel(outputs, lo, hi, table_ref, left_ref, right_ref, *rest):
    out_refs, left_t = split_refs(rest, outputs)
    left_t[...] = left_ref[...].T
    fill_product(table_ref, left_t, right_ref, lo, hi, out_refs)


def weight_call(
    kernel, table, lefts, left_specs, right, right_spec, inner, model, lo, hi, at, total, outputs, held
):
    tokens = right.shape[0]
    outer = table.shape[0] - inner
    width = hi - lo
    operands = list(lefts) + [right]
    specs = list(left_specs) + [right_spec]
    aliases = {}
    for index, item in enumerate(held or ()):
        aliases[1 + len(operands)] = index
        operands.append(item)
        specs.append(pl.BlockSpec(memory_space=pl.ANY))
    part = inner // outputs
    return pl.pallas_call(
        functools.partial(kernel, outputs, lo, hi),
        grid_spec=pltpu.PrefetchScalarGridSpec(
            num_scalar_prefetch=1,
            grid=(outer,),
            in_specs=specs,
            out_specs=[
                pl.BlockSpec(
                    (part, 1, model // inner, width), lambda o, table: (0, table[inner + o], 0, at)
                )
            ] * outputs,
            scratch_shapes=[pltpu.VMEM((model, tokens), bf16)],
        ),
        out_shape=[jax.ShapeDtypeStruct((part, outer, model // inner, total), bf16)] * outputs,
        input_output_aliases=aliases,
        compiler_params=params(),
        cost_estimate=cost(2 * tokens * model * outer * width, 4 * MIB + 4 * model * outer * width),
        name="weight_grad",
    )(table, *operands)


def column_weight_grad(table, left, right, inner, width, at, total, outputs, held=None):
    tokens, model = left.shape
    return weight_call(
        weight_kernel, table, [left], [whole(left.shape)], right,
        pl.BlockSpec((tokens, width), lambda o, table: (0, o)), inner, model, 0, width, at, total,
        outputs, held,
    )


def row_weight_grad(table, left, right, inner, at, total, held=None):
    tokens, width = right.shape
    rows = left.shape[1] // (table.shape[0] - inner)
    return weight_call(
        rows_weight_kernel, table, [left], [pl.BlockSpec((tokens, rows), lambda o, table: (0, o))],
        right, whole(right.shape), inner, rows, 0, width, at, total, 1, held,
    )


def target_back_kernel(start_ref, triple_ref, weight_ref, token_t_ref, out_ref, lang_ref):
    outer, _, width = weight_ref.shape

    @pl.when(pl.program_id(0) == 0)
    def _():
        lang_ref[...] = jnp.zeros_like(lang_ref)

    grad = 2.0 * start_ref[...]
    for o in range(outer):
        grad = grad + mm_nt(
            triple_ref[:, o * width:(o + 1) * width], weight_ref[o]
        )
    out_ref[...] = grad
    high = grad.astype(bf16)
    rest = grad - high.astype(f32)
    mid = rest.astype(bf16)
    low = (rest - mid.astype(f32)).astype(bf16)
    token_t = token_t_ref[...]
    lang_ref[...] += mm(token_t, high) + mm(token_t, mid) + mm(token_t, low)


def target_back_call(start_grad, triple_grad, packed, width, at, token_t):
    tokens, model = start_grad.shape
    outer = packed.shape[0]
    row = lambda r: (r, 0)
    return pl.pallas_call(
        target_back_kernel,
        grid=(tokens // BLOCK,),
        in_specs=[
            pl.BlockSpec((BLOCK, model), row),
            pl.BlockSpec((BLOCK, outer * width), row),
            weight_block(packed, width, at),
            pl.BlockSpec((token_t.shape[0], BLOCK), lambda r: (0, r)),
        ],
        out_specs=[
            pl.BlockSpec((BLOCK, model), row),
            pl.BlockSpec((token_t.shape[0], model), lambda r: (0, 0)),
        ],
        out_shape=[
            jax.ShapeDtypeStruct((tokens, model), f32),
            jax.ShapeDtypeStruct((token_t.shape[0], model), f32),
        ],
        compiler_params=params(),
        cost_estimate=cost(2 * tokens * model * outer * width, 20 * MIB),
        name="target_back",
    )(start_grad, triple_grad, packed, token_t)


def memory_back_kernel(pairs_ref, weight_ref, out_ref):
    outer, _, width = weight_ref.shape
    grad = mm_nt(pairs_ref[:, 0:width], weight_ref[0])
    for o in range(1, outer):
        grad = grad + mm_nt(
            pairs_ref[:, o * width:(o + 1) * width], weight_ref[o]
        )
    out_ref[...] = grad


def memory_back_call(pairs_grad, packed, width, at):
    tokens = pairs_grad.shape[0]
    outer, model, _ = packed.shape
    row = lambda r: (r, 0)
    return pl.pallas_call(
        memory_back_kernel,
        grid=(tokens // BLOCK,),
        in_specs=[
            pl.BlockSpec((BLOCK, outer * width), row),
            weight_block(packed, width, at),
        ],
        out_specs=pl.BlockSpec((BLOCK, model), row),
        out_shape=jax.ShapeDtypeStruct((tokens, model), f32),
        compiler_params=params(),
        cost_estimate=cost(2 * tokens * model * outer * width, 8 * MIB),
        name="memory_back",
    )(pairs_grad, packed)


def gather(shard, outer):
    full = lax.all_gather(shard, both, axis=0, tiled=True)
    return full.reshape(outer, full.shape[0] // outer, full.shape[1])


def bits_of(count):
    return count.bit_length() - 1


def reverse_bits(number, order):
    last = len(order) - 1
    return sum(((number >> bit) & 1) << (last - at) for at, bit in enumerate(order))


def place_orders(outer, inner, swapped):
    inner_order = list(range(bits_of(inner)))
    if swapped and len(inner_order) > 2:
        inner_order[1], inner_order[2] = inner_order[2], inner_order[1]
    return inner_order, list(range(bits_of(outer)))


def inner_places(inner, order):
    places = [0] * inner
    for number in range(inner):
        places[reverse_bits(number, order)] = number
    return jnp.array(places, jnp.int32)


def together_with(value, *others):
    return lax.optimization_barrier((value,) + others)


def chain_step(state, devices):
    keep, send, bits = state
    moved = lax.ppermute(send, both, [(d, d ^ (1 << bits[0])) for d in range(devices)])
    if len(bits) == 1:
        return (keep.astype(f32) + moved.astype(f32))[0], None, ()
    half = keep.shape[0] // 2
    send = (keep[half:].astype(f32) + moved[half:].astype(f32)).astype(send.dtype)
    keep = (keep[:half].astype(f32) + moved[:half].astype(f32)).astype(send.dtype)
    return keep, send, bits[1:]


def chain_start(halves, orders, inner):
    inner_order, outer_order = orders
    keep, send = [item.reshape((-1,) + item.shape[2:]) for item in halves]
    return keep, send, tuple(inner_order + [bits_of(inner) + bit for bit in outer_order])


def chain_end(state, devices):
    while state[2]:
        state = chain_step(state, devices)
    return state[0]


def hold(value, *states):
    value, parts = lax.optimization_barrier((value, [state[:2] for state in states]))
    return value, *[(*part, state[2]) for part, state in zip(parts, states)]


def inner_scatter(packed):
    inner, outer, rows, columns = packed.shape
    flat = packed.reshape(inner * outer * rows, columns)
    part = lax.psum_scatter(flat, "inner", scatter_dimension=0, tiled=True)
    part = part.reshape(outer, rows, columns)
    bits = tuple(bits_of(inner) + bit for bit in range(bits_of(outer)))
    return part[:outer // 2], part[outer // 2:], bits


def per_device(
    target, memory, cotangent, segment_ids, memory_segments, directions, lang_table,
    self_qkv, self_out, cross_q, cross_kv, cross_out, ffn_in, ffn_in_bias, ffn_out, ffn_out_bias,
    norm_gains, norm_biases,
):
    outer = lax.axis_size("outer")
    inner = lax.axis_size("inner")
    devices = outer * inner
    tokens, model = target.shape
    hidden = devices * ffn_in_bias.shape[0]
    langs = lang_table.shape[1]
    piece = model // devices
    rows = model // inner
    w3, w1, w2, w4 = 3 * model // outer, model // outer, 2 * model // outer, hidden // outer
    ratio = hidden // model
    together = ffn_out.shape[0] == rows and model == w4

    small = jnp.concatenate(
        [
            lang_table.T, norm_gains.T, norm_biases.T,
            ffn_out_bias.reshape(1, piece), ffn_in_bias.reshape(ratio, piece),
        ],
        axis=0,
    )
    n_small = small.shape[0]
    small = jnp.pad(small, ((0, rows - n_small), (0, 128 - piece)))
    shards = [self_qkv, self_out, cross_kv, cross_q, cross_out, small]
    weights = gather(jnp.concatenate(shards, axis=1), outer)
    at_small = w3 + 2 * w1 + w2 + w1
    if together:
        shard, weights = lax.optimization_barrier((jnp.concatenate([ffn_in, ffn_out], axis=1), weights))
        g_in = gather(shard, outer)
        g_out, at_out = g_in, w4
    else:
        g_in = gather(ffn_in, outer)
        g_out, at_out = gather(ffn_out, outer), 0

    my_inner, my_outer = lax.axis_index("inner"), lax.axis_index("outer")
    straight = place_orders(outer, inner, False)
    crossed = place_orders(outer, inner, True)
    outer_order = straight[1]
    outer_places = jnp.array([reverse_bits(o, outer_order) for o in range(outer)], jnp.int32)
    outer_places = outer_places ^ reverse_bits(my_outer, outer_order)
    table_plain = jnp.concatenate([jnp.arange(inner, dtype=jnp.int32), outer_places])
    table_a = jnp.concatenate([inner_places(inner, straight[0]) ^ my_inner, outer_places])
    table_b = jnp.concatenate([inner_places(inner, crossed[0]) ^ my_inner, outer_places])

    seg = segment_ids.reshape(-1)
    hot_seg = seg[:, None] == jnp.arange(directions.shape[1])[None, :]
    token_dir = jnp.sum(jnp.where(hot_seg, directions.reshape(1, -1), 0), axis=-1)
    token_hot = (token_dir[:, None] == jnp.arange(128)[None, :]).astype(bf16)
    token_t = (jnp.arange(langs)[:, None] == token_dir[None, :]).astype(bf16)
    own_column = seg[:, None]

    smalls = weights[:, :, at_small:at_small + piece].reshape(devices, rows, piece)[:, :n_small]
    smalls = smalls.transpose(1, 0, 2)
    lang_rows = jnp.pad(smalls[:langs].reshape(langs, model), ((0, 128 - langs), (0, 0)))
    vec = jnp.pad(smalls[langs:langs + 7].reshape(7, model).astype(f32), ((0, 1), (0, 0)))
    in_bias = smalls[langs + 7:].transpose(1, 0, 2).reshape(1, hidden).astype(f32)

    triple = triple_call(target, token_hot, lang_rows, weights, w3, 0)
    hg = HEADS // GROUP
    self_mix, self_levels = attend_call(
        triple, 0, triple, hg, triple, 2 * hg, own_column, segment_ids, True
    )
    pairs = pairs_call(memory, weights, w2, 2)
    normed0, rstd0, cross_entry, queries = middle_call(
        self_mix, target, token_hot, lang_rows, vec, weights, 3, 6, w1
    )
    cross_mix, cross_levels = attend_call(
        queries, 0, pairs, 0, pairs, hg, own_column, memory_segments, False
    )
    (
        layer_output, ffn_entry, act, branch_grad, pre_grad, residual1, cross_grad, cross_mix_grad,
        sums, bias_sum,
    ) = feed_call(
        cross_mix, normed0, cotangent, vec, in_bias, weights, w3 + 2 * w1 + w2, g_in, 0, g_out, at_out, w1
    )

    if together:
        ffn_grads = row_weight_grad(table_plain, act, branch_grad, inner, 1, 2 * w4)
        ffn_grads = column_weight_grad(
            table_plain, ffn_entry, pre_grad, inner, w4, 0, 2 * w4, 1, ffn_grads
        )
        ffn_states = [inner_scatter(ffn_grads[0])]
    else:
        ffn_grads = column_weight_grad(table_plain, ffn_entry, pre_grad, inner, w4, 0, w4, 1)
        ffn_grads += row_weight_grad(table_plain, act, branch_grad, inner, 0, model)
        ffn_states = [inner_scatter(item) for item in ffn_grads]

    cross_mix_grad, _ = lax.optimization_barrier((cross_mix_grad, ffn_grads))
    queries_grad, pairs_grad = attend_back_call(
        queries, 0, pairs, 0, pairs, hg, cross_mix_grad, cross_levels, own_column, memory_segments, False
    )
    start_grad, self_grad, self_mix_grad, sums0 = middle_back_call(
        residual1, queries_grad, normed0, rstd0, vec, weights, 6, 3, w1
    )
    grads_a = column_weight_grad(table_a, memory, pairs_grad, inner, w2, 0, w2 + w1, 2)
    grads_a = column_weight_grad(table_a, self_mix, self_grad, inner, w1, 2, w2 + w1, 2, grads_a)
    state_a = chain_start(grads_a, straight, inner)
    queries_grad, state_a = hold(queries_grad, state_a)
    grads_b = column_weight_grad(table_b, cross_entry, queries_grad, inner, w1, 0, 2 * w1, 2)
    grads_b = column_weight_grad(table_b, cross_mix, cross_grad, inner, w1, 1, 2 * w1, 2, grads_b)
    state_b = chain_start(grads_b, crossed, inner)
    state_a = chain_step(state_a, devices)
    self_mix_grad, state_a, state_b = hold(self_mix_grad, state_a, state_b)
    (triple_grad,) = attend_back_call(
        triple, 0, triple, hg, triple, 2 * hg, self_mix_grad, self_levels, own_column, segment_ids, True
    )
    state_a, state_b = chain_step(state_a, devices), chain_step(state_b, devices)
    triple_grad, state_a, state_b, *ffn_states = hold(triple_grad, state_a, state_b, *ffn_states)
    middle = (w3 + 255) // 256 * 128

    def triple_weight_grad(table, right, lo, hi):
        return weight_call(
            entry_weight_kernel, table, [target, token_hot, lang_rows],
            [whole(target.shape), whole(token_hot.shape), whole(lang_rows.shape)],
            right, pl.BlockSpec((tokens, w3), lambda o, table: (0, o)), inner, model, lo, hi, 0,
            hi - lo, 2, None,
        )

    state_c = chain_start(triple_weight_grad(table_a, triple_grad, 0, middle), straight, inner)
    triple_grad, state_c = hold(triple_grad, state_c)
    state_d = chain_start(triple_weight_grad(table_b, triple_grad, middle, w3), crossed, inner)
    state_a, state_b = chain_step(state_a, devices), chain_step(state_b, devices)
    state_c = chain_step(state_c, devices)
    triple_grad, state_a, state_b, state_c, state_d = hold(
        triple_grad, state_a, state_b, state_c, state_d
    )
    target_grad, lang_sum = target_back_call(start_grad, triple_grad, weights, w3, 0, token_t)
    state_c, state_d = chain_step(state_c, devices), chain_step(state_d, devices)
    lang_sum, state_c, state_d = hold(lang_sum, state_c, state_d)

    stacked = jnp.concatenate(
        [lang_sum, sums0[0:1], sums[3:4], sums[0:1], sums0[1:2], sums[4:5], sums[1:2], sums[2:3]], axis=0
    )
    stacked = stacked.reshape(langs + 7, devices, piece).transpose(1, 0, 2)
    stacked = jnp.concatenate([stacked, bias_sum.reshape(devices, ratio, piece)], axis=1)
    order = table_a[:inner, None] + inner * (inner_places(outer, outer_order) ^ my_outer)[None, :]
    stacked = jnp.take(stacked, order.reshape(-1), axis=0, mode="clip")
    half = devices // 2
    state_e = chain_start(
        [stacked[:half].reshape(inner // 2, outer, n_small, piece),
         stacked[half:].reshape(inner // 2, outer, n_small, piece)], straight, inner,
    )
    pairs_grad, state_e = hold(pairs_grad, state_e)
    memory_grad = memory_back_call(pairs_grad, weights, w2, 2)

    done_a, done_b, done_c, done_d, extra = [
        chain_end(state, devices) for state in (state_a, state_b, state_c, state_d, state_e)
    ]
    ffn_done = [chain_end(state, devices) for state in ffn_states]
    if together:
        ffn_in_grad, ffn_out_grad = ffn_done[0][:, :w4], ffn_done[0][:, w4:]
    else:
        ffn_in_grad, ffn_out_grad = ffn_done
    return (
        layer_output,
        target_grad,
        memory_grad,
        extra[:langs].T,
        jnp.concatenate([done_c, done_d], axis=1),
        done_a[:, w2:],
        done_b[:, :w1],
        done_a[:, :w2],
        done_b[:, w1:],
        ffn_in_grad,
        extra[langs + 7:].reshape(-1),
        ffn_out_grad,
        extra[langs + 6],
        extra[langs:langs + 3].T,
        extra[langs + 3:langs + 6].T,
    )


def solution(mesh):
    rows, cols, line = P(both, None), P("inner", "outer"), P(both)
    return jax.shard_map(
        per_device,
        mesh=mesh,
        in_specs=(
            rows, rows, rows, rows, rows, rows, rows, cols, cols, cols, cols, cols, cols, line, rows,
            line, rows, rows,
        ),
        out_specs=(
            rows, rows, rows, rows, cols, cols, cols, cols, cols, cols, line, rows, line, rows, rows,
        ),
        check_vma=False,
    )
```

```python
import functools

import jax
import jax.numpy as jnp
from jax import lax
from jax.experimental import pallas as pl
from jax.experimental.pallas import tpu as pltpu
from jax.sharding import PartitionSpec as P

HEADS = 16
HEAD_DIM = 64
GROUP = 4
BLOCK = 256
WINDOW = 512

epsilon = 1e-05
masked_score = -1000000000.0
bf16 = jnp.bfloat16
f32 = jnp.float32
both = ("outer", "inner")
MIB = 1 << 20


def mm(left, right):
    return lax.dot_general(left, right, (((1,), (0,)), ((), ())), preferred_element_type=f32)


def mm_nt(left, right):
    return lax.dot_general(left, right, (((1,), (1,)), ((), ())), preferred_element_type=f32)


def params():
    return pltpu.CompilerParams(vmem_limit_bytes=60 * MIB)


def cost(flops, moved, trans=0):
    share = 64
    return pl.CostEstimate(
        flops=int(flops) // share, bytes_accessed=int(moved) // share, transcendentals=int(trans) // share
    )


def whole(shape):
    return pl.BlockSpec(shape, lambda *_: (0,) * len(shape), pipeline_mode=pl.Buffered(1))


def weight_step(model, width, at):
    return pl.BlockSpec((1, model, width), lambda o, *_: (o, 0, at))


def weight_block(packed, width, at):
    outer, model, _ = packed.shape
    return pl.BlockSpec(
        (outer, model, width), lambda *_: (0, 0, at), pipeline_mode=pl.Buffered(1)
    )


def normalise(matrix):
    centred = matrix - jnp.mean(matrix, axis=-1, keepdims=True)
    rstd = lax.rsqrt(jnp.mean(centred * centred, axis=-1, keepdims=True) + epsilon)
    return centred * rstd, rstd


def norm_back(grad, gain, normed, rstd):
    scaled = grad * gain
    mean_scaled = jnp.mean(scaled, axis=-1, keepdims=True)
    mean_product = jnp.mean(scaled * normed, axis=-1, keepdims=True)
    return (scaled - mean_scaled - normed * mean_product) * rstd


def column_sum(matrix):
    return jnp.sum(matrix, axis=0, keepdims=True)


def triple_kernel(target_ref, token_ref, lang_ref, weight_ref, out_ref, entry_t_ref, entry_ref):
    @pl.when(pl.program_id(0) == 0)
    def _():
        start = target_ref[...].astype(f32) + mm(token_ref[...], lang_ref[...])
        entry_ref[...] = start.astype(bf16)
        entry_t_ref[...] = entry_ref[...].T

    out_ref[...] = mm(entry_ref[...], weight_ref[0]).astype(bf16)


def triple_call(target, token_hot, lang_rows, packed, width, at):
    tokens, model = target.shape
    outer = packed.shape[0]
    return pl.pallas_call(
        triple_kernel,
        grid=(outer,),
        in_specs=[
            whole(target.shape), whole(token_hot.shape), whole(lang_rows.shape),
            weight_step(model, width, at),
        ],
        out_specs=[pl.BlockSpec((tokens, width), lambda o: (0, o)), whole((model, tokens))],
        out_shape=[
            jax.ShapeDtypeStruct((tokens, outer * width), bf16),
            jax.ShapeDtypeStruct((model, tokens), bf16),
        ],
        scratch_shapes=[pltpu.VMEM((tokens, model), bf16)],
        compiler_params=params(),
        cost_estimate=cost(2 * tokens * model * outer * width, 16 * MIB),
        name="triple",
    )(target, token_hot, lang_rows, packed)


def pairs_kernel(memory_ref, weight_ref, out_ref, memory_t_ref):
    @pl.when(pl.program_id(0) == 0)
    def _():
        memory_t_ref[...] = memory_ref[...].T

    out_ref[...] = mm(memory_ref[...], weight_ref[0]).astype(bf16)


def pairs_call(memory, packed, width, at):
    tokens, model = memory.shape
    outer = packed.shape[0]
    return pl.pallas_call(
        pairs_kernel,
        grid=(outer,),
        in_specs=[whole(memory.shape), weight_step(model, width, at)],
        out_specs=[pl.BlockSpec((tokens, width), lambda o: (0, o)), whole((model, tokens))],
        out_shape=[
            jax.ShapeDtypeStruct((tokens, outer * width), bf16),
            jax.ShapeDtypeStruct((model, tokens), bf16),
        ],
        compiler_params=params(),
        cost_estimate=cost(2 * tokens * model * outer * width, 8 * MIB),
        name="pairs",
    )(memory, packed)


def mask_bias(own_ref, other_ref, start, window, causal):
    block = own_ref.shape[0]
    allowed = own_ref[...] == other_ref[:, pl.ds(start, window)]
    if causal:
        own_at = pl.program_id(0) * block + lax.broadcasted_iota(jnp.int32, (block, window), 0)
        other_at = start + lax.broadcasted_iota(jnp.int32, (block, window), 1)
        allowed = allowed & (own_at >= other_at)
    return jnp.where(allowed, 0.0, masked_score).astype(f32)


def window_start(block_index, causal):
    if not causal:
        return 0
    return pl.multiple_of(jnp.maximum(block_index - 1, 0) * BLOCK, BLOCK)


def attend_kernel(causal, window, q_ref, k_ref, v_ref, own_ref, other_ref, mix_ref, mix_t_ref, level_ref, bias_ref):
    start = window_start(pl.program_id(0), causal)
    group = pl.program_id(1)

    @pl.when(group == 0)
    def _():
        bias_ref[...] = mask_bias(own_ref, other_ref, start, window, causal)
        level_ref[...] = jnp.zeros_like(level_ref)

    width = q_ref.shape[1]
    owner = lax.broadcasted_iota(jnp.int32, (1, width), 1) // HEAD_DIM
    lane = lax.broadcasted_iota(jnp.int32, (1, 128), 1)
    queries = q_ref[...] * bf16(HEAD_DIM ** -0.5)
    keys = k_ref[pl.ds(start, window), :]
    values = v_ref[pl.ds(start, window), :]
    mix = jnp.zeros(q_ref.shape, f32)
    levels = level_ref[...]
    for head in range(GROUP):
        chosen = owner == head
        scores = mm_nt(queries * chosen.astype(bf16), keys) + bias_ref[...]
        row_max = jnp.max(scores, axis=-1, keepdims=True)
        exps = jnp.exp(scores - row_max)
        total = jnp.sum(exps, axis=-1, keepdims=True)
        probs = (exps * (1.0 / total)).astype(bf16)
        mix = jnp.where(chosen, mm(probs, values), mix)
        levels = jnp.where(lane == group * GROUP + head, row_max + jnp.log(total), levels)
    mix = mix.astype(bf16)
    mix_ref[...] = mix
    mix_t_ref[...] = mix.T
    level_ref[...] = levels


def attend_call(q_array, q_at, k_array, k_at, v_array, v_at, own_column, other_row, causal):
    tokens, others = q_array.shape[0], k_array.shape[0]
    width = GROUP * HEAD_DIM
    model = HEADS * HEAD_DIM
    return pl.pallas_call(
        functools.partial(attend_kernel, causal, WINDOW),
        grid=(tokens // BLOCK, HEADS // GROUP),
        in_specs=[
            pl.BlockSpec((BLOCK, width), lambda b, g: (b, q_at + g)),
            pl.BlockSpec((others, width), lambda b, g: (0, k_at + g)),
            pl.BlockSpec((others, width), lambda b, g: (0, v_at + g)),
            pl.BlockSpec((BLOCK, 1), lambda b, g: (b, 0)),
            pl.BlockSpec((1, others), lambda b, g: (0, 0)),
        ],
        out_specs=[
            pl.BlockSpec((BLOCK, width), lambda b, g: (b, g)),
            pl.BlockSpec((width, BLOCK), lambda b, g: (g, b)),
            pl.BlockSpec((BLOCK, 128), lambda b, g: (b, 0)),
        ],
        out_shape=[
            jax.ShapeDtypeStruct((tokens, model), bf16),
            jax.ShapeDtypeStruct((model, tokens), bf16),
            jax.ShapeDtypeStruct((tokens, 128), f32),
        ],
        scratch_shapes=[pltpu.VMEM((BLOCK, WINDOW), f32)],
        compiler_params=params(),
        cost_estimate=cost(16e9, 12 * MIB, HEADS * tokens * WINDOW),
        name="attend",
    )(q_array, k_array, v_array, own_column, other_row)


def attend_back_kernel(
    causal, joined, q_ref, k_ref, v_ref, grad_ref, level_ref, own_ref, other_ref, *rest
):
    if joined:
        out_ref, keys_t, values_t = rest
    else:
        out_ref, pair_ref, keys_t, values_t = rest
    block_index = pl.program_id(0)
    group = pl.program_id(1)
    blocks = pl.num_programs(0)
    start = window_start(block_index, causal)
    window = WINDOW
    width = q_ref.shape[1]
    model = HEADS * HEAD_DIM
    rows = pl.ds(pl.multiple_of(group * width, width), width)

    @pl.when(block_index == 0)
    def _():
        keys_t[rows, :] = jnp.zeros((width, keys_t.shape[1]), f32)
        values_t[rows, :] = jnp.zeros((width, keys_t.shape[1]), f32)

    bias = mask_bias(own_ref, other_ref, start, window, causal)
    owner = lax.broadcasted_iota(jnp.int32, (1, width), 1) // HEAD_DIM
    lane = lax.broadcasted_iota(jnp.int32, (1, 128), 1)
    queries = q_ref[...] * bf16(HEAD_DIM ** -0.5)
    grads = grad_ref[...]
    queries_t = queries.T
    grads_t = grads.T
    keys = k_ref[pl.ds(start, window), :]
    values = v_ref[pl.ds(start, window), :]
    levels = level_ref[...]
    grad_q = jnp.zeros(q_ref.shape, f32)
    spot = pl.ds(start, window)
    for head in range(GROUP):
        chosen = owner == head
        picked = chosen.astype(bf16)
        scores = mm_nt(queries * picked, keys) + bias
        level = jnp.sum(
            jnp.where(lane == group * GROUP + head, levels, 0.0), axis=-1, keepdims=True
        )
        probs = jnp.exp(scores - level)
        grad_probs = mm_nt(grads * picked, values)
        inner = jnp.sum(probs * grad_probs, axis=-1, keepdims=True)
        grad_scores = (probs * (grad_probs - inner)).astype(bf16)
        band = slice(head * HEAD_DIM, (head + 1) * HEAD_DIM)
        target_rows = pl.ds(pl.multiple_of(group * width + head * HEAD_DIM, HEAD_DIM), HEAD_DIM)
        values_t[target_rows, spot] += mm(grads_t[band, :], probs.astype(bf16))
        keys_t[target_rows, spot] += mm(queries_t[band, :], grad_scores)
        grad_q = jnp.where(chosen, mm(grad_scores, keys), grad_q)
    grad_q = (grad_q * HEAD_DIM ** -0.5).astype(bf16)
    own_rows = pl.ds(pl.multiple_of(block_index * BLOCK, BLOCK), BLOCK)
    columns = pl.multiple_of(group * width, width)
    out_ref[own_rows, pl.ds(columns, width)] = grad_q
    other_ref_out, shift = (out_ref, model) if joined else (pair_ref, 0)

    @pl.when(block_index == blocks - 1)
    def _():
        other_ref_out[:, pl.ds(columns + shift, width)] = keys_t[rows, :].astype(bf16).T
        other_ref_out[:, pl.ds(columns + shift + model, width)] = values_t[rows, :].astype(bf16).T


def attend_back_call(
    q_array, q_at, k_array, k_at, v_array, v_at, grad_mix, levels, own_column, other_row, causal
):
    tokens, others = q_array.shape[0], k_array.shape[0]
    width = GROUP * HEAD_DIM
    model = HEADS * HEAD_DIM
    if causal:
        out_shape = [jax.ShapeDtypeStruct((tokens, 3 * model), bf16)]
    else:
        out_shape = [
            jax.ShapeDtypeStruct((tokens, model), bf16),
            jax.ShapeDtypeStruct((others, 2 * model), bf16),
        ]
    return pl.pallas_call(
        functools.partial(attend_back_kernel, causal, causal),
        grid=(tokens // BLOCK, HEADS // GROUP),
        in_specs=[
            pl.BlockSpec((BLOCK, width), lambda b, g: (b, q_at + g)),
            pl.BlockSpec((others, width), lambda b, g: (0, k_at + g)),
            pl.BlockSpec((others, width), lambda b, g: (0, v_at + g)),
            pl.BlockSpec((BLOCK, width), lambda b, g: (b, g)),
            pl.BlockSpec((BLOCK, 128), lambda b, g: (b, 0)),
            pl.BlockSpec((BLOCK, 1), lambda b, g: (b, 0)),
            pl.BlockSpec((1, others), lambda b, g: (0, 0)),
        ],
        out_specs=[whole(item.shape) for item in out_shape],
        out_shape=out_shape,
        scratch_shapes=[pltpu.VMEM((model, others), f32), pltpu.VMEM((model, others), f32)],
        compiler_params=params(),
        cost_estimate=cost(40e9, 16 * MIB, HEADS * tokens * WINDOW),
        name="attend_back",
    )(q_array, k_array, v_array, grad_mix, levels, own_column, other_row)


def middle_kernel(
    mix_ref, target_ref, token_ref, lang_ref, vec_ref, out_weight_ref, query_weight_ref,
    normed_ref, rstd_ref, entry_t_ref, queries_ref,
):
    outer, _, width = out_weight_ref.shape
    start = target_ref[...].astype(f32) + mm(token_ref[...], lang_ref[...])
    mix = mix_ref[...]
    branch = jnp.concatenate([mm(mix, out_weight_ref[o]) for o in range(outer)], axis=1)
    normed, rstd = normalise(2.0 * start + branch)
    normed_ref[...] = normed
    rstd_ref[...] = rstd
    entry = (normed * vec_ref[0:1, :] + vec_ref[3:4, :]).astype(bf16)
    entry_t_ref[...] = entry.T
    for o in range(outer):
        queries_ref[:, o * width:(o + 1) * width] = mm(entry, query_weight_ref[o]).astype(bf16)


def middle_call(mix, target, token_hot, lang_rows, vec, packed, at_self, at_cross, width):
    tokens, model = target.shape
    row = lambda r: (r, 0)
    return pl.pallas_call(
        middle_kernel,
        grid=(tokens // BLOCK,),
        in_specs=[
            pl.BlockSpec((BLOCK, model), row),
            pl.BlockSpec((BLOCK, model), row),
            pl.BlockSpec((BLOCK, 128), row),
            whole(lang_rows.shape),
            whole(vec.shape),
            weight_block(packed, width, at_self),
            weight_block(packed, width, at_cross),
        ],
        out_specs=[
            pl.BlockSpec((BLOCK, model), row),
            pl.BlockSpec((BLOCK, 1), row),
            pl.BlockSpec((model, BLOCK), lambda r: (0, r)),
            pl.BlockSpec((BLOCK, model), row),
        ],
        out_shape=[
            jax.ShapeDtypeStruct((tokens, model), f32),
            jax.ShapeDtypeStruct((tokens, 1), f32),
            jax.ShapeDtypeStruct((model, tokens), bf16),
            jax.ShapeDtypeStruct((tokens, model), bf16),
        ],
        compiler_params=params(),
        cost_estimate=cost(4 * tokens * model * model, 16 * MIB),
        name="middle",
    )(mix, target, token_hot, lang_rows, vec, packed, packed)


def feed_kernel(
    at_cross, at_in, at_out,
    mix_ref, normed_ref, cot_ref, vec_ref, bias_ref, cross_hbm, in_hbm, out_hbm,
    layer_ref, entry_t_ref, act_ref, branch_grad_t_ref, pre_grad_ref, residual_ref, cross_grad_ref,
    mix_grad_ref, sums_ref, bias_sum_ref,
    cross_weight, in_weight, out_weight, slope, sems,
):
    outer, _, width = cross_weight.shape
    chunk = in_weight.shape[2]
    step = pl.program_id(0)

    def cross_copy():
        return pltpu.make_async_copy(
            cross_hbm.at[:, :, pl.ds(at_cross, width)], cross_weight, sems.at[0]
        )

    def in_copy(o):
        return pltpu.make_async_copy(
            in_hbm.at[o, :, pl.ds(at_in, chunk)], in_weight.at[o], sems.at[1 + o]
        )

    def out_copy(o):
        return pltpu.make_async_copy(
            out_hbm.at[o, :, pl.ds(at_out, out_weight.shape[2])], out_weight.at[o],
            sems.at[1 + outer + o],
        )


    @pl.when(step == 0)
    def _():
        cross_copy().start()
        for o in range(outer):
            in_copy(o).start()
            out_copy(o).start()
        sums_ref[...] = jnp.zeros_like(sums_ref)
        bias_sum_ref[...] = jnp.zeros_like(bias_sum_ref)
        cross_copy().wait()

    gain0, gain1, gain2 = vec_ref[0:1, :], vec_ref[1:2, :], vec_ref[2:3, :]
    shift0, shift1, shift2 = vec_ref[3:4, :], vec_ref[4:5, :], vec_ref[5:6, :]
    first = normed_ref[...] * gain0 + shift0
    mix = mix_ref[...]
    branch = jnp.concatenate([mm(mix, cross_weight[o]) for o in range(outer)], axis=1)
    normed1, rstd1 = normalise(2.0 * first + branch)
    second = normed1 * gain1 + shift1
    entry = second.astype(bf16)
    entry_t_ref[...] = entry.T
    total = 2.0 * second + vec_ref[6:7, :]
    for o in range(outer):
        @pl.when(step == 0)
        def _():
            in_copy(o).wait()
            out_copy(o).wait()

        span = slice(o * chunk, (o + 1) * chunk)
        pre = mm(entry, in_weight[o]) + bias_ref[:, span]
        half = 0.5 + 0.5 * lax.erf(pre * (0.5 ** 0.5))
        slope[:, span] = half + pre * (jnp.exp(-0.5 * pre * pre) * 0.3989422804014327)
        act = (pre * half).astype(bf16)
        act_ref[:, span] = act
        total = total + mm(act, out_weight[o])
    normed2, rstd2 = normalise(total)
    layer_ref[...] = (normed2 * gain2 + shift2).astype(bf16)
    cot = cot_ref[...].astype(f32)
    sums_ref[0:1, :] += column_sum(cot * normed2)
    sums_ref[1:2, :] += column_sum(cot)
    back2 = norm_back(cot, gain2, normed2, rstd2)
    branch_grad = back2.astype(bf16)
    branch_grad_t_ref[...] = branch_grad.T
    sums_ref[2:3, :] += column_sum(branch_grad.astype(f32))
    grad_second = 2.0 * back2
    for o in range(outer):
        span = slice(o * chunk, (o + 1) * chunk)
        pre_grad = (mm_nt(branch_grad, out_weight[o]) * slope[:, span]).astype(bf16)
        pre_grad_ref[:, span] = pre_grad
        bias_sum_ref[:, span] += column_sum(pre_grad.astype(f32))
        grad_second = grad_second + mm_nt(pre_grad, in_weight[o])
    sums_ref[3:4, :] += column_sum(grad_second * normed1)
    sums_ref[4:5, :] += column_sum(grad_second)
    back1 = norm_back(grad_second, gain1, normed1, rstd1)
    residual_ref[...] = back1
    cross_grad = back1.astype(bf16)
    cross_grad_ref[...] = cross_grad
    mix_grad = mm_nt(cross_grad[:, 0:width], cross_weight[0])
    for o in range(1, outer):
        mix_grad = mix_grad + mm_nt(
            cross_grad[:, o * width:(o + 1) * width], cross_weight[o]
        )
    mix_grad_ref[...] = mix_grad.astype(bf16)


def feed_call(mix, normed, cot, vec, bias, packed_cross, at_cross, packed_in, at_in, packed_out, at_out, width):
    tokens, model = mix.shape
    hidden = bias.shape[1]
    outer = packed_cross.shape[0]
    chunk = hidden // outer
    row = lambda r: (r, 0)
    blocked = lambda cols: pl.BlockSpec((BLOCK, cols), row)
    anywhere = pl.BlockSpec(memory_space=pl.ANY)
    turned = pl.BlockSpec((model, BLOCK), lambda r: (0, r))
    turned_shape = jax.ShapeDtypeStruct((model, tokens), bf16)
    out = lambda cols, kind: jax.ShapeDtypeStruct((tokens, cols), kind)
    return pl.pallas_call(
        functools.partial(feed_kernel, at_cross, at_in, at_out),
        grid=(tokens // BLOCK,),
        in_specs=[
            blocked(model), blocked(model), blocked(model),
            whole(vec.shape), whole(bias.shape), anywhere, anywhere, anywhere,
        ],
        out_specs=[
            blocked(model), turned, blocked(hidden), turned, blocked(hidden),
            blocked(model), blocked(model), blocked(model),
            pl.BlockSpec((8, model), lambda r: (0, 0)),
            pl.BlockSpec((1, hidden), lambda r: (0, 0)),
        ],
        out_shape=[
            out(model, bf16), turned_shape, out(hidden, bf16), turned_shape,
            out(hidden, bf16), out(model, f32), out(model, bf16), out(model, bf16),
            jax.ShapeDtypeStruct((8, model), f32),
            jax.ShapeDtypeStruct((1, hidden), f32),
        ],
        scratch_shapes=[
            pltpu.VMEM((outer, model, width), bf16),
            pltpu.VMEM((outer, model, chunk), bf16),
            pltpu.VMEM((outer, chunk, model), bf16),
            pltpu.VMEM((BLOCK, hidden), f32),
            pltpu.SemaphoreType.DMA((1 + 2 * outer,)),
        ],
        compiler_params=params(),
        cost_estimate=cost(36 * tokens * model * model, 60 * MIB, tokens * hidden * 2),
        name="feed",
    )(mix, normed, cot, vec, bias, packed_cross, packed_in, packed_out)


def middle_back_kernel(
    residual_ref, queries_grad_ref, normed_ref, rstd_ref, vec_ref, query_weight_ref, out_weight_ref,
    start_ref, branch_grad_ref, mix_grad_ref, sums_ref,
):
    outer, _, width = out_weight_ref.shape

    @pl.when(pl.program_id(0) == 0)
    def _():
        sums_ref[...] = jnp.zeros_like(sums_ref)

    grad_first = 2.0 * residual_ref[...]
    for o in range(outer):
        grad_first = grad_first + mm_nt(
            queries_grad_ref[:, o * width:(o + 1) * width], query_weight_ref[o]
        )
    normed = normed_ref[...]
    sums_ref[0:1, :] += column_sum(grad_first * normed)
    sums_ref[1:2, :] += column_sum(grad_first)
    back = norm_back(grad_first, vec_ref[0:1, :], normed, rstd_ref[...])
    start_ref[...] = back
    branch_grad = back.astype(bf16)
    branch_grad_ref[...] = branch_grad
    mix_grad = mm_nt(branch_grad[:, 0:width], out_weight_ref[0])
    for o in range(1, outer):
        mix_grad = mix_grad + mm_nt(
            branch_grad[:, o * width:(o + 1) * width], out_weight_ref[o]
        )
    mix_grad_ref[...] = mix_grad.astype(bf16)


def middle_back_call(residual, queries_grad, normed, rstd, vec, packed, at_cross, at_self, width):
    tokens, model = residual.shape
    row = lambda r: (r, 0)
    blocked = pl.BlockSpec((BLOCK, model), row)
    return pl.pallas_call(
        middle_back_kernel,
        grid=(tokens // BLOCK,),
        in_specs=[
            blocked, blocked, blocked,
            pl.BlockSpec((BLOCK, 1), row),
            whole(vec.shape),
            weight_block(packed, width, at_cross),
            weight_block(packed, width, at_self),
        ],
        out_specs=[blocked, blocked, blocked, pl.BlockSpec((8, model), lambda r: (0, 0))],
        out_shape=[
            jax.ShapeDtypeStruct((tokens, model), f32),
            jax.ShapeDtypeStruct((tokens, model), bf16),
            jax.ShapeDtypeStruct((tokens, model), bf16),
            jax.ShapeDtypeStruct((8, model), f32),
        ],
        compiler_params=params(),
        cost_estimate=cost(4 * tokens * model * model, 22 * MIB),
        name="middle_back",
    )(residual, queries_grad, normed, rstd, vec, packed, packed)


def half_kernel(count, first, table_ref, *refs):
    lefts, rights = refs[:count], refs[count:2 * count]
    out_ref, held, sems = refs[2 * count], refs[2 * count + 1:-1], refs[-1]
    part, _, piece, _ = out_ref.shape
    step = pl.program_id(0)

    def copy(at, row):
        source = pl.multiple_of(table_ref[first + row] * piece, piece)
        return pltpu.make_async_copy(
            lefts[at].at[pl.ds(source, piece), :], held[at].at[pl.ds(row * piece, piece), :],
            sems.at[at, row],
        )

    @pl.when(step == 0)
    def _():
        for at in range(count):
            for row in range(part):
                copy(at, row).start()

    lo = 0
    for at in range(count):
        @pl.when(step == 0)
        def _():
            for row in range(part):
                copy(at, row).wait()

        width = rights[at].shape[1]
        product = mm(held[at][...], rights[at][...]).astype(bf16)
        out_ref[:, 0, :, lo:lo + width] = product.reshape(part, piece, width)
        lo += width


def half_weight_grads(table, lefts, rights, inner, first):
    outer = table.shape[0] - inner
    part, piece = inner // 2, lefts[0].shape[0] // inner
    widths = [right.shape[1] // outer for right in rights]
    flops = sum(right.size for right in rights) * part * piece * 2
    return pl.pallas_call(
        functools.partial(half_kernel, len(lefts), first),
        grid_spec=pltpu.PrefetchScalarGridSpec(
            num_scalar_prefetch=1,
            grid=(outer,),
            in_specs=[pl.BlockSpec(memory_space=pl.ANY)] * len(lefts) + [
                pl.BlockSpec((right.shape[0], width), lambda o, table: (0, o))
                for right, width in zip(rights, widths)
            ],
            out_specs=pl.BlockSpec(
                (part, 1, piece, sum(widths)), lambda o, table: (0, table[inner + o], 0, 0)
            ),
            scratch_shapes=[pltpu.VMEM((part * piece, left.shape[1]), bf16) for left in lefts]
            + [pltpu.SemaphoreType.DMA((len(lefts), part))],
        ),
        out_shape=jax.ShapeDtypeStruct((part, outer, piece, sum(widths)), bf16),
        compiler_params=params(),
        cost_estimate=cost(flops, 12 * MIB),
        name="half_weight_grads",
    )(table, *lefts, *rights)


def feed_in_kernel(table_ref, left_ref, right_ref, *rest):
    out_ref = rest[-1]
    inner, _, piece, width = out_ref.shape
    product = mm(left_ref[...], right_ref[...]).astype(bf16)
    out_ref[:, 0] = product.reshape(inner, piece, width)


def feed_out_kernel(table_ref, left_ref, right_ref, out_ref):
    inner, _, piece, width = out_ref.shape
    product = mm(left_ref[...], right_ref[...]).astype(bf16)
    for i in range(inner):
        for b in range(width // piece):
            out_ref[i, 0, :, b * piece:(b + 1) * piece] = product[
                b * piece:(b + 1) * piece, i * piece:(i + 1) * piece
            ]


def feed_rows_kernel(table_ref, left_ref, right_ref, out_ref):
    inner, _, piece, width = out_ref.shape
    product = mm(left_ref[...].T, right_ref[...]).astype(bf16)
    out_ref[:, 0] = product.reshape(inner, piece, width)


def feed_weight_grad(kernel, table, left, left_spec, right, right_spec, inner, piece, width, at, total, held=None):
    outer = table.shape[0] - inner
    operands, specs = [left, right], [left_spec, right_spec]
    if held is not None:
        operands.append(held)
        specs.append(pl.BlockSpec(memory_space=pl.ANY))
    return pl.pallas_call(
        kernel,
        grid_spec=pltpu.PrefetchScalarGridSpec(
            num_scalar_prefetch=1,
            grid=(outer,),
            in_specs=specs,
            out_specs=pl.BlockSpec(
                (inner, 1, piece, width), lambda o, table: (0, table[inner + o], 0, at)
            ),
        ),
        out_shape=jax.ShapeDtypeStruct((inner, outer, piece, total), bf16),
        input_output_aliases={} if held is None else {3: 0},
        compiler_params=params(),
        cost_estimate=cost(8 * left.shape[1] * 1024 * 1024, 24 * MIB),
        name="feed_weight_grad",
    )(table, *operands)


def entry_back_kernel(
    start_ref, triple_ref, pairs_ref, weight_ref, pairs_weight_ref, token_t_ref,
    out_ref, memory_ref, lang_ref,
):
    outer, _, width = weight_ref.shape
    pair_width = pairs_weight_ref.shape[2]

    @pl.when(pl.program_id(0) == 0)
    def _():
        lang_ref[...] = jnp.zeros_like(lang_ref)

    grad = 2.0 * start_ref[...]
    for o in range(outer):
        grad = grad + mm_nt(triple_ref[:, o * width:(o + 1) * width], weight_ref[o])
    out_ref[...] = grad
    high = grad.astype(bf16)
    rest = grad - high.astype(f32)
    mid = rest.astype(bf16)
    low = (rest - mid.astype(f32)).astype(bf16)
    token_t = token_t_ref[...]
    lang_ref[...] += mm(token_t, high) + mm(token_t, mid) + mm(token_t, low)
    memory_grad = mm_nt(pairs_ref[:, 0:pair_width], pairs_weight_ref[0])
    for o in range(1, outer):
        memory_grad = memory_grad + mm_nt(
            pairs_ref[:, o * pair_width:(o + 1) * pair_width], pairs_weight_ref[o]
        )
    memory_ref[...] = memory_grad


def entry_back_call(start_grad, triple_grad, pairs_grad, packed, width, pairs_packed, pairs_width, at, token_t):
    tokens, model = start_grad.shape
    outer = packed.shape[0]
    steps = tokens // BLOCK
    memory_block = pairs_grad.shape[0] // steps
    row = lambda r: (r, 0)
    return pl.pallas_call(
        entry_back_kernel,
        grid=(steps,),
        in_specs=[
            pl.BlockSpec((BLOCK, model), row),
            pl.BlockSpec((BLOCK, outer * width), row),
            pl.BlockSpec((memory_block, outer * pairs_width), row),
            weight_block(packed, width, 0),
            weight_block(pairs_packed, pairs_width, at),
            pl.BlockSpec((token_t.shape[0], BLOCK), lambda r: (0, r)),
        ],
        out_specs=[
            pl.BlockSpec((BLOCK, model), row),
            pl.BlockSpec((memory_block, model), row),
            pl.BlockSpec((token_t.shape[0], model), lambda r: (0, 0)),
        ],
        out_shape=[
            jax.ShapeDtypeStruct((tokens, model), f32),
            jax.ShapeDtypeStruct(pairs_grad.shape[:1] + (model,), f32),
            jax.ShapeDtypeStruct((token_t.shape[0], model), f32),
        ],
        compiler_params=params(),
        cost_estimate=cost(2 * tokens * model * outer * (width + pairs_width // 2), 40 * MIB),
        name="entry_back",
    )(start_grad, triple_grad, pairs_grad, packed, pairs_packed, token_t)


def gather(shard, outer):
    full = lax.all_gather(shard, both, axis=0, tiled=True)
    return full.reshape(outer, full.shape[0] // outer, full.shape[1])


def swap(value, distance, devices):
    return lax.ppermute(value, both, [(d, d ^ distance) for d in range(devices)])


def total_of(pieces, kind):
    total = pieces[0].astype(f32)
    for item in pieces[1:]:
        total = total + item.astype(f32)
    return total.astype(kind)


def hold(*values):
    return lax.optimization_barrier(values)


def core_stage(keep, send, devices):
    moved = swap(send, 1, devices)
    return [total_of((keep[k], moved[k]), keep.dtype) for k in range(keep.shape[0])]


def plane_stage(parts, devices):
    moved = [parts[0]] + [swap(parts[k], 2 * k, devices) for k in range(1, len(parts))]
    return [total_of([item[o] for item in moved], parts[0].dtype) for o in range(parts[0].shape[0])]


def outer_stage(parts, inner, devices):
    moved = [parts[0]] + [swap(parts[k], inner * k, devices) for k in range(1, len(parts))]
    return total_of(moved, f32)


def outer_half(part, inner, devices):
    half = part.shape[0] // 2
    moved = swap(part[half:], inner * half, devices)
    return (part[:half].astype(f32) + moved.astype(f32)).astype(f32 if half == 1 else part.dtype)


def inner_scatter(packed):
    inner, outer, rows, columns = packed.shape
    flat = packed.reshape(inner * outer * rows, columns)
    part = lax.psum_scatter(flat, "inner", scatter_dimension=0, tiled=True)
    return part.reshape(outer, rows, columns)


def permuted_column(shard, outer, inner, devices):
    own = lax.axis_index("outer")
    column = jnp.zeros((outer,) + shard.shape, shard.dtype)
    for k in range(outer):
        moved = swap(shard, inner * k, devices) if k else shard
        column = lax.dynamic_update_slice(column, moved[None], (own ^ k, 0, 0))
    return column


def plane_moves(column, inner, devices):
    return [column] + [swap(column, 2 * k, devices) for k in range(1, inner // 2)]


def plane_place(moves):
    chip = lax.axis_index("inner") // 2
    outer, rows, columns = moves[0].shape
    plane = jnp.zeros((outer, len(moves), rows, columns), moves[0].dtype)
    for k, item in enumerate(moves):
        plane = lax.dynamic_update_slice(plane, item[:, None], (0, chip ^ k, 0, 0))
    return plane


def core_place(plane, moved):
    core = lax.rem(lax.axis_index("inner"), 2)
    mine = jnp.arange(2)[None, None, :, None, None] == core
    full = jnp.where(mine, plane[:, :, None], moved[:, :, None])
    outer, chips, _, rows, columns = full.shape
    return full.reshape(outer, chips * 2 * rows, columns)


def per_device(
    target, memory, cotangent, segment_ids, memory_segments, directions, lang_table,
    self_qkv, self_out, cross_q, cross_kv, cross_out, ffn_in, ffn_in_bias, ffn_out, ffn_out_bias,
    norm_gains, norm_biases,
):
    outer = lax.axis_size("outer")
    inner = lax.axis_size("inner")
    devices = outer * inner
    tokens, model = target.shape
    hidden = devices * ffn_in_bias.shape[0]
    langs = lang_table.shape[1]
    piece = model // devices
    rows = model // inner
    w3, w1, w2, w4 = 3 * model // outer, model // outer, 2 * model // outer, hidden // outer
    ratio = hidden // model
    together = ffn_out.shape[0] == rows and model == w4

    small = jnp.concatenate(
        [
            lang_table.T, norm_gains.T, norm_biases.T,
            ffn_out_bias.reshape(1, piece), ffn_in_bias.reshape(ratio, piece),
        ],
        axis=0,
    )
    n_small = small.shape[0]
    small = jnp.pad(small, ((0, rows - n_small), (0, 128 - piece)))
    first_weights = gather(jnp.concatenate([self_qkv, small], axis=1), outer)
    at_small = w3
    column = permuted_column(
        jnp.concatenate([self_out, cross_q, cross_kv, cross_out], axis=1), outer, inner, devices
    )
    moves = plane_moves(column, inner, devices)
    if together:
        shard, _ = hold(jnp.concatenate([ffn_in, ffn_out], axis=1), column)
        g_in = gather(shard, outer)
        g_out, at_out = g_in, w4
    else:
        g_in = gather(ffn_in, outer)
        g_out, at_out = gather(ffn_out, outer), 0

    first_weights, moves = hold(first_weights, moves)
    plane = plane_place(moves)
    core_move = swap(plane, 1, devices)
    my_inner, my_outer = lax.axis_index("inner"), lax.axis_index("outer")
    outer_places = jnp.arange(outer, dtype=jnp.int32) ^ my_outer
    inner_order = jnp.array(
        [chip * 2 + core for core in range(2) for chip in range(inner // 2)], jnp.int32
    ) ^ my_inner
    table = jnp.concatenate([inner_order, outer_places])
    seg = segment_ids.reshape(-1)
    hot_seg = seg[:, None] == jnp.arange(directions.shape[1])[None, :]
    token_dir = jnp.sum(jnp.where(hot_seg, directions.reshape(1, -1), 0), axis=-1)
    token_hot = (token_dir[:, None] == jnp.arange(128)[None, :]).astype(bf16)
    token_t = (jnp.arange(langs)[:, None] == token_dir[None, :]).astype(bf16)
    own_column = seg[:, None]

    smalls = first_weights[:, :, at_small:at_small + piece].reshape(devices, rows, piece)[:, :n_small]
    smalls = smalls.transpose(1, 0, 2)
    lang_rows = jnp.pad(smalls[:langs].reshape(langs, model), ((0, 128 - langs), (0, 0)))
    vec = jnp.pad(smalls[langs:langs + 7].reshape(7, model).astype(f32), ((0, 1), (0, 0)))
    in_bias = smalls[langs + 7:].transpose(1, 0, 2).reshape(1, hidden).astype(f32)

    triple, self_entry_t = triple_call(target, token_hot, lang_rows, first_weights, w3, 0)
    triple, core_move = hold(triple, core_move)
    weights = core_place(plane, core_move)
    hg = HEADS // GROUP
    self_mix, self_mix_t, self_levels = attend_call(
        triple, 0, triple, hg, triple, 2 * hg, own_column, segment_ids, True
    )
    pairs, memory_t = pairs_call(memory, weights, w2, 1)
    normed0, rstd0, cross_entry_t, queries = middle_call(
        self_mix, target, token_hot, lang_rows, vec, weights, 0, 1, w1
    )
    cross_mix, cross_mix_t, cross_levels = attend_call(
        queries, 0, pairs, 0, pairs, hg, own_column, memory_segments, False
    )
    (
        layer_output, ffn_entry_t, act, branch_grad_t, pre_grad, residual1, cross_grad,
        cross_mix_grad, sums, bias_sum,
    ) = feed_call(
        cross_mix, normed0, cotangent, vec, in_bias, weights, 2 * w1 + w2, g_in, 0, g_out, at_out, w1
    )

    plain = jnp.concatenate([jnp.arange(inner, dtype=jnp.int32), outer_places])
    hidden_step = pl.BlockSpec((tokens, w4), lambda o, table: (0, o))
    if together:
        ffn_grads = feed_weight_grad(
            feed_out_kernel, plain, branch_grad_t, whole(branch_grad_t.shape), act, hidden_step,
            inner, rows, model, 1, 2 * w4,
        )
        ffn_grads = [feed_weight_grad(
            feed_in_kernel, plain, ffn_entry_t, whole(ffn_entry_t.shape), pre_grad, hidden_step,
            inner, rows, w4, 0, 2 * w4, ffn_grads,
        )]
    else:
        branch_grad = branch_grad_t.T
        ffn_grads = [
            feed_weight_grad(
                feed_in_kernel, plain, ffn_entry_t, whole(ffn_entry_t.shape), pre_grad, hidden_step,
                inner, rows, w4, 0, w4,
            ),
            feed_weight_grad(
                feed_rows_kernel, plain, act, hidden_step, branch_grad, whole(branch_grad.shape),
                inner, ffn_out.shape[0], model, 0, model,
            ),
        ]
    ffn_parts = [inner_scatter(item) for item in ffn_grads]

    cross_mix_grad, _ = hold(cross_mix_grad, ffn_grads)
    queries_grad, pairs_grad = attend_back_call(
        queries, 0, pairs, 0, pairs, hg, cross_mix_grad, cross_levels, own_column, memory_segments, False
    )
    start_grad, self_grad, self_mix_grad, sums0 = middle_back_call(
        residual1, queries_grad, normed0, rstd0, vec, weights, 1, 0, w1
    )
    lefts_a = [memory_t, cross_entry_t, cross_mix_t, self_mix_t]
    rights_a = [pairs_grad, queries_grad, cross_grad, self_grad]
    send_a = half_weight_grads(table, lefts_a, rights_a, inner, inner // 2)
    rights_a, send_a = hold(rights_a, send_a)
    keep_a = half_weight_grads(table, lefts_a, rights_a, inner, 0)
    parts_a = core_stage(keep_a, send_a, devices)
    self_mix_grad, parts_a = hold(self_mix_grad, parts_a)
    (triple_grad,) = attend_back_call(
        triple, 0, triple, hg, triple, 2 * hg, self_mix_grad, self_levels, own_column, segment_ids, True
    )
    parts_a = plane_stage(parts_a, devices)
    triple_grad, parts_a = hold(triple_grad, parts_a)
    send_c = half_weight_grads(table, [self_entry_t], [triple_grad], inner, inner // 2)
    triple_grad, send_c = hold(triple_grad, send_c)
    keep_c = half_weight_grads(table, [self_entry_t], [triple_grad], inner, 0)
    parts_c = core_stage(keep_c, send_c, devices)
    done_a = outer_stage(parts_a, inner, devices)
    triple_grad, parts_c, ffn_parts, done_a = hold(triple_grad, parts_c, ffn_parts, done_a)
    target_grad, memory_grad, lang_sum = entry_back_call(
        start_grad, triple_grad, pairs_grad, first_weights, w3, weights, w2, 1, token_t
    )
    parts_c = plane_stage(parts_c, devices)
    ffn_parts = [outer_half(item, inner, devices) for item in ffn_parts]
    lang_sum, parts_c, ffn_parts = hold(lang_sum, parts_c, ffn_parts)

    stacked = jnp.concatenate(
        [lang_sum, sums0[0:1], sums[3:4], sums[0:1], sums0[1:2], sums[4:5], sums[1:2], sums[2:3]], axis=0
    )
    stacked = stacked.reshape(langs + 7, devices, piece).transpose(1, 0, 2)
    stacked = jnp.concatenate([stacked, bias_sum.reshape(devices, ratio, piece)], axis=1)
    order = inner_order[:, None] + inner * outer_places[None, :]
    stacked = jnp.take(stacked, order.reshape(-1), axis=0, mode="clip")
    stacked = stacked.reshape(2, inner // 2, outer, n_small, piece)
    parts_e = core_stage(stacked[0], stacked[1], devices)
    parts_e = plane_stage(parts_e, devices)
    while ffn_parts[0].shape[0] > 1:
        ffn_parts = [outer_half(item, inner, devices) for item in ffn_parts]
    ffn_done = [item[0] for item in ffn_parts]
    done_c = outer_stage(parts_c, inner, devices)
    parts_e, ffn_done, done_c = hold(parts_e, ffn_done, done_c)
    extra = outer_stage(parts_e, inner, devices)
    if together:
        ffn_in_grad = ffn_done[0][:, :w4]
        ffn_out_grad = ffn_done[0][:, w4:].reshape(rows, model // rows, rows)
        ffn_out_grad = ffn_out_grad.transpose(2, 1, 0).reshape(rows, model)
    else:
        ffn_in_grad, ffn_out_grad = ffn_done
    return (
        layer_output,
        target_grad,
        memory_grad,
        extra[:langs].T,
        done_c,
        done_a[:, w2 + 2 * w1:],
        done_a[:, w2:w2 + w1],
        done_a[:, :w2],
        done_a[:, w2 + w1:w2 + 2 * w1],
        ffn_in_grad,
        extra[langs + 7:].reshape(-1),
        ffn_out_grad,
        extra[langs + 6],
        extra[langs:langs + 3].T,
        extra[langs + 3:langs + 6].T,
    )


def solution(mesh):
    rows, cols, line = P(both, None), P("inner", "outer"), P(both)
    return jax.shard_map(
        per_device,
        mesh=mesh,
        in_specs=(
            rows, rows, rows, rows, rows, rows, rows, cols, cols, cols, cols, cols, cols, line, rows,
            line, rows, rows,
        ),
        out_specs=(
            rows, rows, rows, rows, cols, cols, cols, cols, cols, cols, line, rows, line, rows, rows,
        ),
        check_vma=False,
    )
```

```python
import functools

import jax
import jax.numpy as jnp
from jax import lax
from jax.experimental import pallas as pl
from jax.experimental.pallas import tpu as pltpu
from jax.sharding import PartitionSpec as P

HEADS = 16
HEAD_DIM = 64
GROUP = 4
BLOCK = 256
CHUNK = 128
WINDOWS = (256, 384, 512)

epsilon = 1e-05
masked_score = -1000000000.0
bf16 = jnp.bfloat16
f32 = jnp.float32
both = ("outer", "inner")
MIB = 1 << 20


def mm(left, right):
    return lax.dot_general(left, right, (((1,), (0,)), ((), ())), preferred_element_type=f32)


def mm_nt(left, right):
    return lax.dot_general(left, right, (((1,), (1,)), ((), ())), preferred_element_type=f32)


def params():
    return pltpu.CompilerParams(vmem_limit_bytes=60 * MIB)


def cost(flops, moved, trans=0):
    share = 64
    return pl.CostEstimate(
        flops=int(flops) // share, bytes_accessed=int(moved) // share, transcendentals=int(trans) // share
    )


def whole(shape):
    return pl.BlockSpec(shape, lambda *_: (0,) * len(shape), pipeline_mode=pl.Buffered(1))


def weight_step(model, width, at):
    return pl.BlockSpec((1, model, width), lambda o, *_: (o, 0, at))


def weight_block(packed, width, at):
    outer, model, _ = packed.shape
    return pl.BlockSpec(
        (outer, model, width), lambda *_: (0, 0, at), pipeline_mode=pl.Buffered(1)
    )


def normalise(matrix):
    centred = matrix - jnp.mean(matrix, axis=-1, keepdims=True)
    rstd = lax.rsqrt(jnp.mean(centred * centred, axis=-1, keepdims=True) + epsilon)
    return centred * rstd, rstd


def norm_back(grad, gain, normed, rstd):
    scaled = grad * gain
    mean_scaled = jnp.mean(scaled, axis=-1, keepdims=True)
    mean_product = jnp.mean(scaled * normed, axis=-1, keepdims=True)
    return (scaled - mean_scaled - normed * mean_product) * rstd


def column_sum(matrix):
    return jnp.sum(matrix, axis=0, keepdims=True)


def triple_kernel(target_ref, token_ref, lang_ref, weight_ref, out_ref, entry_t_ref, entry_ref):
    @pl.when(pl.program_id(0) == 0)
    def _():
        start = target_ref[...].astype(f32) + mm(token_ref[...], lang_ref[...])
        entry_ref[...] = start.astype(bf16)
        entry_t_ref[...] = entry_ref[...].T

    out_ref[...] = mm(entry_ref[...], weight_ref[0]).astype(bf16)


def triple_call(target, token_hot, lang_rows, packed, width, at):
    tokens, model = target.shape
    outer = packed.shape[0]
    return pl.pallas_call(
        triple_kernel,
        grid=(outer,),
        in_specs=[
            whole(target.shape), whole(token_hot.shape), whole(lang_rows.shape),
            weight_step(model, width, at),
        ],
        out_specs=[pl.BlockSpec((tokens, width), lambda o: (0, o)), whole((model, tokens))],
        out_shape=[
            jax.ShapeDtypeStruct((tokens, outer * width), bf16),
            jax.ShapeDtypeStruct((model, tokens), bf16),
        ],
        scratch_shapes=[pltpu.VMEM((tokens, model), bf16)],
        compiler_params=params(),
        cost_estimate=cost(2 * tokens * model * outer * width, 16 * MIB),
        name="triple",
    )(target, token_hot, lang_rows, packed)


def pairs_kernel(memory_ref, weight_ref, out_ref, memory_t_ref):
    @pl.when(pl.program_id(0) == 0)
    def _():
        memory_t_ref[...] = memory_ref[...].T

    out_ref[...] = mm(memory_ref[...], weight_ref[0]).astype(bf16)


def pairs_call(memory, packed, width, at):
    tokens, model = memory.shape
    outer = packed.shape[0]
    return pl.pallas_call(
        pairs_kernel,
        grid=(outer,),
        in_specs=[whole(memory.shape), weight_step(model, width, at)],
        out_specs=[pl.BlockSpec((tokens, width), lambda o: (0, o)), whole((model, tokens))],
        out_shape=[
            jax.ShapeDtypeStruct((tokens, outer * width), bf16),
            jax.ShapeDtypeStruct((model, tokens), bf16),
        ],
        compiler_params=params(),
        cost_estimate=cost(2 * tokens * model * outer * width, 8 * MIB),
        name="pairs",
    )(memory, packed)


def mask_bias(own_ref, other_ref, start, window, causal):
    block = own_ref.shape[0]
    allowed = own_ref[...] == other_ref[:, pl.ds(start, window)]
    if causal:
        own_at = pl.program_id(0) * block + lax.broadcasted_iota(jnp.int32, (block, window), 0)
        other_at = start + lax.broadcasted_iota(jnp.int32, (block, window), 1)
        allowed = allowed & (own_at >= other_at)
    return jnp.where(allowed, 0.0, masked_score).astype(f32)


def for_window(table_ref, body):
    block_index = pl.program_id(0)
    start = pl.multiple_of(table_ref[block_index], CHUNK)
    chunks = table_ref[pl.num_programs(0) + block_index]
    for window in WINDOWS:
        @pl.when(chunks == window // CHUNK)
        def _():
            body(start, window)


def self_windows(ids):
    blocks = ids.shape[0] // BLOCK
    below = jnp.sum(ids[None, :] < ids[::BLOCK][:, None], axis=1)
    start = below // CHUNK * CHUNK
    ends = (jnp.arange(blocks) + 1) * BLOCK
    return jnp.concatenate([start, (ends - start) // CHUNK]).astype(jnp.int32)


def cross_windows(ids, others):
    below = jnp.sum(others[None, :] < ids[::BLOCK][:, None], axis=1)
    ends = jnp.sum(others[None, :] <= ids[BLOCK - 1::BLOCK][:, None], axis=1)
    start = below // CHUNK * CHUNK
    chunks = jnp.clip((ends - start + CHUNK - 1) // CHUNK, WINDOWS[0] // CHUNK, WINDOWS[-1] // CHUNK)
    start = jnp.minimum(start, others.shape[0] - chunks * CHUNK)
    return jnp.concatenate([start, chunks]).astype(jnp.int32)


def attend_kernel(
    causal, table_ref, q_ref, k_ref, v_ref, own_ref, other_ref, mix_ref, mix_t_ref, level_ref, bias_ref
):
    group = pl.program_id(1)
    width = q_ref.shape[1]
    owner = lax.broadcasted_iota(jnp.int32, (1, width), 1) // HEAD_DIM
    lane = lax.broadcasted_iota(jnp.int32, (1, 128), 1)

    def body(start, window):
        @pl.when(group == 0)
        def _():
            bias_ref[:, :window] = mask_bias(own_ref, other_ref, start, window, causal)
            level_ref[...] = jnp.zeros_like(level_ref)

        queries = q_ref[...] * bf16(HEAD_DIM ** -0.5)
        keys = k_ref[pl.ds(start, window), :]
        values = v_ref[pl.ds(start, window), :]
        bias = bias_ref[:, :window]
        mix = jnp.zeros(q_ref.shape, f32)
        levels = level_ref[...]
        for head in range(GROUP):
            chosen = owner == head
            scores = mm_nt(queries * chosen.astype(bf16), keys) + bias
            row_max = jnp.max(scores, axis=-1, keepdims=True)
            exps = jnp.exp(scores - row_max)
            total = jnp.sum(exps, axis=-1, keepdims=True)
            probs = (exps * (1.0 / total)).astype(bf16)
            mix = jnp.where(chosen, mm(probs, values), mix)
            levels = jnp.where(lane == group * GROUP + head, row_max + jnp.log(total), levels)
        mix = mix.astype(bf16)
        mix_ref[...] = mix
        mix_t_ref[...] = mix.T
        level_ref[...] = levels

    for_window(table_ref, body)


def attend_call(table, q_array, q_at, k_array, k_at, v_array, v_at, own_column, other_row, causal):
    tokens, others = q_array.shape[0], k_array.shape[0]
    width = GROUP * HEAD_DIM
    model = HEADS * HEAD_DIM
    return pl.pallas_call(
        functools.partial(attend_kernel, causal),
        grid_spec=pltpu.PrefetchScalarGridSpec(
            num_scalar_prefetch=1,
            grid=(tokens // BLOCK, HEADS // GROUP),
            in_specs=[
                pl.BlockSpec((BLOCK, width), lambda b, g, t: (b, q_at + g)),
                pl.BlockSpec((others, width), lambda b, g, t: (0, k_at + g)),
                pl.BlockSpec((others, width), lambda b, g, t: (0, v_at + g)),
                pl.BlockSpec((BLOCK, 1), lambda b, g, t: (b, 0)),
                pl.BlockSpec((1, others), lambda b, g, t: (0, 0)),
            ],
            out_specs=[
                pl.BlockSpec((BLOCK, width), lambda b, g, t: (b, g)),
                pl.BlockSpec((width, BLOCK), lambda b, g, t: (g, b)),
                pl.BlockSpec((BLOCK, 128), lambda b, g, t: (b, 0)),
            ],
            scratch_shapes=[pltpu.VMEM((BLOCK, WINDOWS[-1]), f32)],
        ),
        out_shape=[
            jax.ShapeDtypeStruct((tokens, model), bf16),
            jax.ShapeDtypeStruct((model, tokens), bf16),
            jax.ShapeDtypeStruct((tokens, 128), f32),
        ],
        compiler_params=params(),
        cost_estimate=cost(12e9, 12 * MIB, HEADS * tokens * 384),
        name="attend",
    )(table, q_array, k_array, v_array, own_column, other_row)


def attend_back_kernel(
    causal, table_ref, q_ref, k_ref, v_ref, grad_ref, level_ref, own_ref, other_ref, *rest
):
    if causal:
        out_ref, keys_t, values_t = rest
    else:
        out_ref, pair_ref, keys_t, values_t = rest
    block_index = pl.program_id(0)
    group = pl.program_id(1)
    blocks = pl.num_programs(0)
    width = q_ref.shape[1]
    model = HEADS * HEAD_DIM
    rows = pl.ds(pl.multiple_of(group * width, width), width)
    columns = pl.multiple_of(group * width, width)
    owner = lax.broadcasted_iota(jnp.int32, (1, width), 1) // HEAD_DIM
    lane = lax.broadcasted_iota(jnp.int32, (1, 128), 1)

    @pl.when(block_index == 0)
    def _():
        keys_t[rows, :] = jnp.zeros((width, keys_t.shape[1]), f32)
        values_t[rows, :] = jnp.zeros((width, keys_t.shape[1]), f32)

    def body(start, window):
        bias = mask_bias(own_ref, other_ref, start, window, causal)
        queries = q_ref[...] * bf16(HEAD_DIM ** -0.5)
        grads = grad_ref[...]
        queries_t = queries.T
        grads_t = grads.T
        spot = pl.ds(start, window)
        keys = k_ref[spot, :]
        values = v_ref[spot, :]
        levels = level_ref[...]
        grad_q = jnp.zeros(q_ref.shape, f32)
        for head in range(GROUP):
            chosen = owner == head
            picked = chosen.astype(bf16)
            scores = mm_nt(queries * picked, keys) + bias
            level = jnp.sum(
                jnp.where(lane == group * GROUP + head, levels, 0.0), axis=-1, keepdims=True
            )
            probs = jnp.exp(scores - level)
            grad_probs = mm_nt(grads * picked, values)
            inner = jnp.sum(probs * grad_probs, axis=-1, keepdims=True)
            grad_scores = (probs * (grad_probs - inner)).astype(bf16)
            band = slice(head * HEAD_DIM, (head + 1) * HEAD_DIM)
            target_rows = pl.ds(
                pl.multiple_of(group * width + head * HEAD_DIM, HEAD_DIM), HEAD_DIM
            )
            values_t[target_rows, spot] += mm(grads_t[band, :], probs.astype(bf16))
            keys_t[target_rows, spot] += mm(queries_t[band, :], grad_scores)
            grad_q = jnp.where(chosen, mm(grad_scores, keys), grad_q)
        grad_q = (grad_q * HEAD_DIM ** -0.5).astype(bf16)
        own_rows = pl.ds(pl.multiple_of(block_index * BLOCK, BLOCK), BLOCK)
        out_ref[own_rows, pl.ds(columns, width)] = grad_q

    for_window(table_ref, body)
    pair_out, shift = (out_ref, model) if causal else (pair_ref, 0)

    @pl.when(block_index == blocks - 1)
    def _():
        pair_out[:, pl.ds(columns + shift, width)] = keys_t[rows, :].astype(bf16).T
        pair_out[:, pl.ds(columns + shift + model, width)] = values_t[rows, :].astype(bf16).T


def attend_back_call(
    table, q_array, q_at, k_array, k_at, v_array, v_at, grad_mix, levels, own_column, other_row, causal
):
    tokens, others = q_array.shape[0], k_array.shape[0]
    width = GROUP * HEAD_DIM
    model = HEADS * HEAD_DIM
    if causal:
        out_shape = [jax.ShapeDtypeStruct((tokens, 3 * model), bf16)]
    else:
        out_shape = [
            jax.ShapeDtypeStruct((tokens, model), bf16),
            jax.ShapeDtypeStruct((others, 2 * model), bf16),
        ]
    return pl.pallas_call(
        functools.partial(attend_back_kernel, causal),
        grid_spec=pltpu.PrefetchScalarGridSpec(
            num_scalar_prefetch=1,
            grid=(tokens // BLOCK, HEADS // GROUP),
            in_specs=[
                pl.BlockSpec((BLOCK, width), lambda b, g, t: (b, q_at + g)),
                pl.BlockSpec((others, width), lambda b, g, t: (0, k_at + g)),
                pl.BlockSpec((others, width), lambda b, g, t: (0, v_at + g)),
                pl.BlockSpec((BLOCK, width), lambda b, g, t: (b, g)),
                pl.BlockSpec((BLOCK, 128), lambda b, g, t: (b, 0)),
                pl.BlockSpec((BLOCK, 1), lambda b, g, t: (b, 0)),
                pl.BlockSpec((1, others), lambda b, g, t: (0, 0)),
            ],
            out_specs=[whole(item.shape) for item in out_shape],
            scratch_shapes=[pltpu.VMEM((model, others), f32), pltpu.VMEM((model, others), f32)],
        ),
        out_shape=out_shape,
        compiler_params=params(),
        cost_estimate=cost(30e9, 16 * MIB, HEADS * tokens * 384),
        name="attend_back",
    )(table, q_array, k_array, v_array, grad_mix, levels, own_column, other_row)


def middle_kernel(
    mix_ref, target_ref, token_ref, lang_ref, vec_ref, out_weight_ref, query_weight_ref,
    normed_ref, rstd_ref, entry_t_ref, queries_ref,
):
    outer, _, width = out_weight_ref.shape
    start = target_ref[...].astype(f32) + mm(token_ref[...], lang_ref[...])
    mix = mix_ref[...]
    branch = jnp.concatenate([mm(mix, out_weight_ref[o]) for o in range(outer)], axis=1)
    normed, rstd = normalise(2.0 * start + branch)
    normed_ref[...] = normed
    rstd_ref[...] = rstd
    entry = (normed * vec_ref[0:1, :] + vec_ref[3:4, :]).astype(bf16)
    entry_t_ref[...] = entry.T
    for o in range(outer):
        queries_ref[:, o * width:(o + 1) * width] = mm(entry, query_weight_ref[o]).astype(bf16)


def middle_call(mix, target, token_hot, lang_rows, vec, packed, at_self, at_cross, width):
    tokens, model = target.shape
    row = lambda r: (r, 0)
    return pl.pallas_call(
        middle_kernel,
        grid=(tokens // BLOCK,),
        in_specs=[
            pl.BlockSpec((BLOCK, model), row),
            pl.BlockSpec((BLOCK, model), row),
            pl.BlockSpec((BLOCK, 128), row),
            whole(lang_rows.shape),
            whole(vec.shape),
            weight_block(packed, width, at_self),
            weight_block(packed, width, at_cross),
        ],
        out_specs=[
            pl.BlockSpec((BLOCK, model), row),
            pl.BlockSpec((BLOCK, 1), row),
            pl.BlockSpec((model, BLOCK), lambda r: (0, r)),
            pl.BlockSpec((BLOCK, model), row),
        ],
        out_shape=[
            jax.ShapeDtypeStruct((tokens, model), f32),
            jax.ShapeDtypeStruct((tokens, 1), f32),
            jax.ShapeDtypeStruct((model, tokens), bf16),
            jax.ShapeDtypeStruct((tokens, model), bf16),
        ],
        compiler_params=params(),
        cost_estimate=cost(4 * tokens * model * model, 16 * MIB),
        name="middle",
    )(mix, target, token_hot, lang_rows, vec, packed, packed)


def feed_kernel(
    at_cross, at_in, at_out,
    mix_ref, normed_ref, cot_ref, vec_ref, bias_ref, cross_hbm, in_hbm, out_hbm,
    layer_ref, entry_t_ref, act_ref, branch_grad_t_ref, pre_grad_ref, residual_ref, cross_grad_ref,
    mix_grad_ref, sums_ref, bias_sum_ref,
    cross_weight, in_weight, out_weight, slope, sems,
):
    outer, _, width = cross_weight.shape
    chunk = in_weight.shape[2]
    step = pl.program_id(0)

    def cross_copy():
        return pltpu.make_async_copy(
            cross_hbm.at[:, :, pl.ds(at_cross, width)], cross_weight, sems.at[0]
        )

    def in_copy(o):
        return pltpu.make_async_copy(
            in_hbm.at[o, :, pl.ds(at_in, chunk)], in_weight.at[o], sems.at[1 + o]
        )

    def out_copy(o):
        return pltpu.make_async_copy(
            out_hbm.at[o, :, pl.ds(at_out, out_weight.shape[2])], out_weight.at[o],
            sems.at[1 + outer + o],
        )


    @pl.when(step == 0)
    def _():
        cross_copy().start()
        for o in range(outer):
            in_copy(o).start()
            out_copy(o).start()
        sums_ref[...] = jnp.zeros_like(sums_ref)
        bias_sum_ref[...] = jnp.zeros_like(bias_sum_ref)
        cross_copy().wait()

    gain0, gain1, gain2 = vec_ref[0:1, :], vec_ref[1:2, :], vec_ref[2:3, :]
    shift0, shift1, shift2 = vec_ref[3:4, :], vec_ref[4:5, :], vec_ref[5:6, :]
    first = normed_ref[...] * gain0 + shift0
    mix = mix_ref[...]
    branch = jnp.concatenate([mm(mix, cross_weight[o]) for o in range(outer)], axis=1)
    normed1, rstd1 = normalise(2.0 * first + branch)
    second = normed1 * gain1 + shift1
    entry = second.astype(bf16)
    entry_t_ref[...] = entry.T
    total = 2.0 * second + vec_ref[6:7, :]
    for o in range(outer):
        @pl.when(step == 0)
        def _():
            in_copy(o).wait()
            out_copy(o).wait()

        span = slice(o * chunk, (o + 1) * chunk)
        pre = mm(entry, in_weight[o]) + bias_ref[:, span]
        half = 0.5 + 0.5 * lax.erf(pre * (0.5 ** 0.5))
        slope[:, span] = half + pre * (jnp.exp(-0.5 * pre * pre) * 0.3989422804014327)
        act = (pre * half).astype(bf16)
        act_ref[:, span] = act
        total = total + mm(act, out_weight[o])
    normed2, rstd2 = normalise(total)
    layer_ref[...] = (normed2 * gain2 + shift2).astype(bf16)
    cot = cot_ref[...].astype(f32)
    sums_ref[0:1, :] += column_sum(cot * normed2)
    sums_ref[1:2, :] += column_sum(cot)
    back2 = norm_back(cot, gain2, normed2, rstd2)
    branch_grad = back2.astype(bf16)
    branch_grad_t_ref[...] = branch_grad.T
    sums_ref[2:3, :] += column_sum(branch_grad.astype(f32))
    grad_second = 2.0 * back2
    for o in range(outer):
        span = slice(o * chunk, (o + 1) * chunk)
        pre_grad = (mm_nt(branch_grad, out_weight[o]) * slope[:, span]).astype(bf16)
        pre_grad_ref[:, span] = pre_grad
        bias_sum_ref[:, span] += column_sum(pre_grad.astype(f32))
        grad_second = grad_second + mm_nt(pre_grad, in_weight[o])
    sums_ref[3:4, :] += column_sum(grad_second * normed1)
    sums_ref[4:5, :] += column_sum(grad_second)
    back1 = norm_back(grad_second, gain1, normed1, rstd1)
    residual_ref[...] = back1
    cross_grad = back1.astype(bf16)
    cross_grad_ref[...] = cross_grad
    mix_grad = mm_nt(cross_grad[:, 0:width], cross_weight[0])
    for o in range(1, outer):
        mix_grad = mix_grad + mm_nt(
            cross_grad[:, o * width:(o + 1) * width], cross_weight[o]
        )
    mix_grad_ref[...] = mix_grad.astype(bf16)


def feed_call(mix, normed, cot, vec, bias, packed_cross, at_cross, packed_in, at_in, packed_out, at_out, width):
    tokens, model = mix.shape
    hidden = bias.shape[1]
    outer = packed_cross.shape[0]
    chunk = hidden // outer
    row = lambda r: (r, 0)
    blocked = lambda cols: pl.BlockSpec((BLOCK, cols), row)
    anywhere = pl.BlockSpec(memory_space=pl.ANY)
    turned = pl.BlockSpec((model, BLOCK), lambda r: (0, r))
    turned_shape = jax.ShapeDtypeStruct((model, tokens), bf16)
    out = lambda cols, kind: jax.ShapeDtypeStruct((tokens, cols), kind)
    return pl.pallas_call(
        functools.partial(feed_kernel, at_cross, at_in, at_out),
        grid=(tokens // BLOCK,),
        in_specs=[
            blocked(model), blocked(model), blocked(model),
            whole(vec.shape), whole(bias.shape), anywhere, anywhere, anywhere,
        ],
        out_specs=[
            blocked(model), turned, blocked(hidden), turned, blocked(hidden),
            blocked(model), blocked(model), blocked(model),
            pl.BlockSpec((8, model), lambda r: (0, 0)),
            pl.BlockSpec((1, hidden), lambda r: (0, 0)),
        ],
        out_shape=[
            out(model, bf16), turned_shape, out(hidden, bf16), turned_shape,
            out(hidden, bf16), out(model, f32), out(model, bf16), out(model, bf16),
            jax.ShapeDtypeStruct((8, model), f32),
            jax.ShapeDtypeStruct((1, hidden), f32),
        ],
        scratch_shapes=[
            pltpu.VMEM((outer, model, width), bf16),
            pltpu.VMEM((outer, model, chunk), bf16),
            pltpu.VMEM((outer, chunk, model), bf16),
            pltpu.VMEM((BLOCK, hidden), f32),
            pltpu.SemaphoreType.DMA((1 + 2 * outer,)),
        ],
        compiler_params=params(),
        cost_estimate=cost(36 * tokens * model * model, 60 * MIB, tokens * hidden * 2),
        name="feed",
    )(mix, normed, cot, vec, bias, packed_cross, packed_in, packed_out)


def middle_back_kernel(
    residual_ref, queries_grad_ref, normed_ref, rstd_ref, vec_ref, query_weight_ref, out_weight_ref,
    start_ref, branch_grad_ref, mix_grad_ref, sums_ref,
):
    outer, _, width = out_weight_ref.shape

    @pl.when(pl.program_id(0) == 0)
    def _():
        sums_ref[...] = jnp.zeros_like(sums_ref)

    grad_first = 2.0 * residual_ref[...]
    for o in range(outer):
        grad_first = grad_first + mm_nt(
            queries_grad_ref[:, o * width:(o + 1) * width], query_weight_ref[o]
        )
    normed = normed_ref[...]
    sums_ref[0:1, :] += column_sum(grad_first * normed)
    sums_ref[1:2, :] += column_sum(grad_first)
    back = norm_back(grad_first, vec_ref[0:1, :], normed, rstd_ref[...])
    start_ref[...] = back
    branch_grad = back.astype(bf16)
    branch_grad_ref[...] = branch_grad
    mix_grad = mm_nt(branch_grad[:, 0:width], out_weight_ref[0])
    for o in range(1, outer):
        mix_grad = mix_grad + mm_nt(
            branch_grad[:, o * width:(o + 1) * width], out_weight_ref[o]
        )
    mix_grad_ref[...] = mix_grad.astype(bf16)


def middle_back_call(residual, queries_grad, normed, rstd, vec, packed, at_cross, at_self, width):
    tokens, model = residual.shape
    row = lambda r: (r, 0)
    blocked = pl.BlockSpec((BLOCK, model), row)
    return pl.pallas_call(
        middle_back_kernel,
        grid=(tokens // BLOCK,),
        in_specs=[
            blocked, blocked, blocked,
            pl.BlockSpec((BLOCK, 1), row),
            whole(vec.shape),
            weight_block(packed, width, at_cross),
            weight_block(packed, width, at_self),
        ],
        out_specs=[blocked, blocked, blocked, pl.BlockSpec((8, model), lambda r: (0, 0))],
        out_shape=[
            jax.ShapeDtypeStruct((tokens, model), f32),
            jax.ShapeDtypeStruct((tokens, model), bf16),
            jax.ShapeDtypeStruct((tokens, model), bf16),
            jax.ShapeDtypeStruct((8, model), f32),
        ],
        compiler_params=params(),
        cost_estimate=cost(4 * tokens * model * model, 22 * MIB),
        name="middle_back",
    )(residual, queries_grad, normed, rstd, vec, packed, packed)


def half_kernel(count, first, table_ref, *refs):
    lefts, rights = refs[:count], refs[count:2 * count]
    out_ref, held, sems = refs[2 * count], refs[2 * count + 1:-1], refs[-1]
    part, _, piece, _ = out_ref.shape
    step = pl.program_id(0)

    def copy(at, row):
        source = pl.multiple_of(table_ref[first + row] * piece, piece)
        return pltpu.make_async_copy(
            lefts[at].at[pl.ds(source, piece), :], held[at].at[pl.ds(row * piece, piece), :],
            sems.at[at, row],
        )

    @pl.when(step == 0)
    def _():
        for at in range(count):
            for row in range(part):
                copy(at, row).start()

    lo = 0
    for at in range(count):
        @pl.when(step == 0)
        def _():
            for row in range(part):
                copy(at, row).wait()

        width = rights[at].shape[1]
        product = mm(held[at][...], rights[at][...]).astype(bf16)
        out_ref[:, 0, :, lo:lo + width] = product.reshape(part, piece, width)
        lo += width


def half_weight_grads(table, lefts, rights, inner, first):
    outer = table.shape[0] - inner
    part, piece = inner // 2, lefts[0].shape[0] // inner
    widths = [right.shape[1] // outer for right in rights]
    flops = sum(right.size for right in rights) * part * piece * 2
    return pl.pallas_call(
        functools.partial(half_kernel, len(lefts), first),
        grid_spec=pltpu.PrefetchScalarGridSpec(
            num_scalar_prefetch=1,
            grid=(outer,),
            in_specs=[pl.BlockSpec(memory_space=pl.ANY)] * len(lefts) + [
                pl.BlockSpec((right.shape[0], width), lambda o, table: (0, o))
                for right, width in zip(rights, widths)
            ],
            out_specs=pl.BlockSpec(
                (part, 1, piece, sum(widths)), lambda o, table: (0, table[inner + o], 0, 0)
            ),
            scratch_shapes=[pltpu.VMEM((part * piece, left.shape[1]), bf16) for left in lefts]
            + [pltpu.SemaphoreType.DMA((len(lefts), part))],
        ),
        out_shape=jax.ShapeDtypeStruct((part, outer, piece, sum(widths)), bf16),
        compiler_params=params(),
        cost_estimate=cost(flops, 12 * MIB),
        name="half_weight_grads",
    )(table, *lefts, *rights)


def feed_in_kernel(left_ref, right_ref, *rest):
    out_ref = rest[-1]
    _, inner, piece, width = out_ref.shape
    product = mm(left_ref[...], right_ref[...]).astype(bf16)
    out_ref[0] = product.reshape(inner, piece, width)


def feed_out_kernel(left_ref, right_ref, out_ref):
    _, inner, piece, width = out_ref.shape
    product = mm(left_ref[...], right_ref[...]).astype(bf16)
    for i in range(inner):
        for b in range(width // piece):
            out_ref[0, i, :, b * piece:(b + 1) * piece] = product[
                b * piece:(b + 1) * piece, i * piece:(i + 1) * piece
            ]


def feed_rows_kernel(left_ref, right_ref, out_ref):
    _, inner, piece, width = out_ref.shape
    product = mm(left_ref[...].T, right_ref[...]).astype(bf16)
    out_ref[0] = product.reshape(inner, piece, width)


def feed_weight_grad(
    kernel, left, left_spec, right, right_spec, outer, inner, piece, width, at, total, held=None
):
    operands, specs = [left, right], [left_spec, right_spec]
    if held is not None:
        operands.append(held)
        specs.append(pl.BlockSpec(memory_space=pl.ANY))
    return pl.pallas_call(
        kernel,
        grid=(outer,),
        in_specs=specs,
        out_specs=pl.BlockSpec((1, inner, piece, width), lambda o: (o, 0, 0, at)),
        out_shape=jax.ShapeDtypeStruct((outer, inner, piece, total), bf16),
        input_output_aliases={} if held is None else {2: 0},
        compiler_params=params(),
        cost_estimate=cost(8 * left.shape[1] * 1024 * 1024, 24 * MIB),
        name="feed_weight_grad",
    )(*operands)


def entry_back_kernel(
    start_ref, triple_ref, pairs_ref, weight_ref, pairs_weight_ref, token_t_ref,
    out_ref, memory_ref, lang_ref,
):
    outer, _, width = weight_ref.shape
    pair_width = pairs_weight_ref.shape[2]

    @pl.when(pl.program_id(0) == 0)
    def _():
        lang_ref[...] = jnp.zeros_like(lang_ref)

    grad = 2.0 * start_ref[...]
    for o in range(outer):
        grad = grad + mm_nt(triple_ref[:, o * width:(o + 1) * width], weight_ref[o])
    out_ref[...] = grad
    high = grad.astype(bf16)
    rest = grad - high.astype(f32)
    mid = rest.astype(bf16)
    low = (rest - mid.astype(f32)).astype(bf16)
    token_t = token_t_ref[...]
    lang_ref[...] += mm(token_t, high) + mm(token_t, mid) + mm(token_t, low)
    memory_grad = mm_nt(pairs_ref[:, 0:pair_width], pairs_weight_ref[0])
    for o in range(1, outer):
        memory_grad = memory_grad + mm_nt(
            pairs_ref[:, o * pair_width:(o + 1) * pair_width], pairs_weight_ref[o]
        )
    memory_ref[...] = memory_grad


def entry_back_call(start_grad, triple_grad, pairs_grad, packed, width, pairs_packed, pairs_width, at, token_t):
    tokens, model = start_grad.shape
    outer = packed.shape[0]
    steps = tokens // BLOCK
    memory_block = pairs_grad.shape[0] // steps
    row = lambda r: (r, 0)
    return pl.pallas_call(
        entry_back_kernel,
        grid=(steps,),
        in_specs=[
            pl.BlockSpec((BLOCK, model), row),
            pl.BlockSpec((BLOCK, outer * width), row),
            pl.BlockSpec((memory_block, outer * pairs_width), row),
            weight_block(packed, width, 0),
            weight_block(pairs_packed, pairs_width, at),
            pl.BlockSpec((token_t.shape[0], BLOCK), lambda r: (0, r)),
        ],
        out_specs=[
            pl.BlockSpec((BLOCK, model), row),
            pl.BlockSpec((memory_block, model), row),
            pl.BlockSpec((token_t.shape[0], model), lambda r: (0, 0)),
        ],
        out_shape=[
            jax.ShapeDtypeStruct((tokens, model), f32),
            jax.ShapeDtypeStruct(pairs_grad.shape[:1] + (model,), f32),
            jax.ShapeDtypeStruct((token_t.shape[0], model), f32),
        ],
        compiler_params=params(),
        cost_estimate=cost(2 * tokens * model * outer * (width + pairs_width // 2), 40 * MIB),
        name="entry_back",
    )(start_grad, triple_grad, pairs_grad, packed, pairs_packed, token_t)


def gather(shard, outer):
    full = lax.all_gather(shard, both, axis=0, tiled=True)
    return full.reshape(outer, full.shape[0] // outer, full.shape[1])


def swap(value, distance, devices):
    return lax.ppermute(value, both, [(d, d ^ distance) for d in range(devices)])


def total_of(pieces, kind):
    total = pieces[0].astype(f32)
    for item in pieces[1:]:
        total = total + item.astype(f32)
    return total.astype(kind)


def hold(*values):
    return lax.optimization_barrier(values)


def core_stage(keep, send, devices):
    moved = swap(send, 1, devices)
    return [total_of((keep[k], moved[k]), keep.dtype) for k in range(keep.shape[0])]


def plane_stage(parts, devices):
    moved = [parts[0]] + [swap(parts[k], 2 * k, devices) for k in range(1, len(parts))]
    return [total_of([item[o] for item in moved], parts[0].dtype) for o in range(parts[0].shape[0])]


def outer_stage(parts, inner, devices):
    moved = [parts[0]] + [swap(parts[k], inner * k, devices) for k in range(1, len(parts))]
    return total_of(moved, f32)


def joint_scatter(packed):
    outer, inner, rows, columns = packed.shape
    flat = packed.reshape(outer * inner * rows, columns)
    return lax.psum_scatter(flat, both, scatter_dimension=0, tiled=True).astype(f32)


def core_halves(keep, send, devices):
    moved = swap(send, 1, devices)
    cut = keep.shape[-1] // 256 * 128
    result = []
    for columns, kept, sent in (
        (slice(0, cut), slice(0, None, 2), slice(1, None, 2)),
        (slice(cut, None), slice(0, 2), slice(2, 4)),
    ):
        for rows in (kept, sent):
            result.append(total_of((keep[rows, ..., columns], moved[rows, ..., columns]), keep.dtype))
    return result


def first_halves(parts, devices):
    keep_x, send_x, keep_y, send_y = parts
    result = []
    for keep, send, distance in ((keep_x, send_x, 2), (keep_y, send_y, 4)):
        moved = swap(send, distance, devices)
        result += [total_of((keep[k], moved[k]), keep.dtype) for k in range(2)]
    return result


def second_halves(parts, devices):
    keep_x, send_x, keep_y, send_y = parts
    moved_x, moved_y = swap(send_x, 4, devices), swap(send_y, 2, devices)
    return [
        jnp.concatenate(
            [total_of((keep_x[o], moved_x[o]), keep_x.dtype),
             total_of((keep_y[o], moved_y[o]), keep_y.dtype)], axis=-1,
        )
        for o in range(keep_x.shape[0])
    ]


def chain_stages(chips):
    if chips == 4:
        return core_halves, first_halves, second_halves
    return core_stage, plane_stage, lambda parts, devices: parts


def permuted_column(shard, outer, inner, devices):
    own = lax.axis_index("outer")
    column = jnp.zeros((outer,) + shard.shape, shard.dtype)
    for k in range(outer):
        moved = swap(shard, inner * k, devices) if k else shard
        column = lax.dynamic_update_slice(column, moved[None], (own ^ k, 0, 0))
    return column


def plane_moves(column, inner, devices):
    return [column] + [swap(column, 2 * k, devices) for k in range(1, inner // 2)]


def plane_place(moves):
    chip = lax.axis_index("inner") // 2
    outer, rows, columns = moves[0].shape
    plane = jnp.zeros((outer, len(moves), rows, columns), moves[0].dtype)
    for k, item in enumerate(moves):
        plane = lax.dynamic_update_slice(plane, item[:, None], (0, chip ^ k, 0, 0))
    return plane


def core_place(plane, moved):
    core = lax.rem(lax.axis_index("inner"), 2)
    mine = jnp.arange(2)[None, None, :, None, None] == core
    full = jnp.where(mine, plane[:, :, None], moved[:, :, None])
    outer, chips, _, rows, columns = full.shape
    return full.reshape(outer, chips * 2 * rows, columns)


def per_device(
    target, memory, cotangent, segment_ids, memory_segments, directions, lang_table,
    self_qkv, self_out, cross_q, cross_kv, cross_out, ffn_in, ffn_in_bias, ffn_out, ffn_out_bias,
    norm_gains, norm_biases,
):
    outer = lax.axis_size("outer")
    inner = lax.axis_size("inner")
    devices = outer * inner
    tokens, model = target.shape
    hidden = devices * ffn_in_bias.shape[0]
    langs = lang_table.shape[1]
    piece = model // devices
    rows = model // inner
    w3, w1, w2, w4 = 3 * model // outer, model // outer, 2 * model // outer, hidden // outer
    ratio = hidden // model
    together = ffn_out.shape[0] == rows and model == w4

    small = jnp.concatenate(
        [
            lang_table.T, norm_gains.T, norm_biases.T,
            ffn_out_bias.reshape(1, piece), ffn_in_bias.reshape(ratio, piece),
        ],
        axis=0,
    )
    n_small = small.shape[0]
    small = jnp.pad(small, ((0, rows - n_small), (0, 128 - piece)))
    first_weights = gather(jnp.concatenate([self_qkv, small], axis=1), outer)
    at_small = w3
    column = permuted_column(
        jnp.concatenate([self_out, cross_q, cross_kv, cross_out], axis=1), outer, inner, devices
    )
    moves = plane_moves(column, inner, devices)
    if together:
        shard, _ = hold(jnp.concatenate([ffn_in, ffn_out], axis=1), column)
        g_in = gather(shard, outer)
        g_out, at_out = g_in, w4
    else:
        g_in = gather(ffn_in, outer)
        g_out, at_out = gather(ffn_out, outer), 0

    first_weights, moves = hold(first_weights, moves)
    plane = plane_place(moves)
    core_move = swap(plane, 1, devices)
    my_inner, my_outer = lax.axis_index("inner"), lax.axis_index("outer")
    outer_places = jnp.arange(outer, dtype=jnp.int32) ^ my_outer
    inner_order = jnp.array(
        [chip * 2 + core for core in range(2) for chip in range(inner // 2)], jnp.int32
    ) ^ my_inner
    table = jnp.concatenate([inner_order, outer_places])
    seg = segment_ids.reshape(-1)
    hot_seg = seg[:, None] == jnp.arange(directions.shape[1])[None, :]
    token_dir = jnp.sum(jnp.where(hot_seg, directions.reshape(1, -1), 0), axis=-1)
    token_hot = (token_dir[:, None] == jnp.arange(128)[None, :]).astype(bf16)
    token_t = (jnp.arange(langs)[:, None] == token_dir[None, :]).astype(bf16)
    own_column = seg[:, None]
    self_table = self_windows(seg)
    cross_table = cross_windows(seg, memory_segments.reshape(-1))

    smalls = first_weights[:, :, at_small:at_small + piece].reshape(devices, rows, piece)[:, :n_small]
    smalls = smalls.transpose(1, 0, 2)
    lang_rows = jnp.pad(smalls[:langs].reshape(langs, model), ((0, 128 - langs), (0, 0)))
    vec = jnp.pad(smalls[langs:langs + 7].reshape(7, model).astype(f32), ((0, 1), (0, 0)))
    in_bias = smalls[langs + 7:].transpose(1, 0, 2).reshape(1, hidden).astype(f32)

    triple, self_entry_t = triple_call(target, token_hot, lang_rows, first_weights, w3, 0)
    triple, core_move = hold(triple, core_move)
    weights = core_place(plane, core_move)
    hg = HEADS // GROUP
    self_mix, self_mix_t, self_levels = attend_call(
        self_table, triple, 0, triple, hg, triple, 2 * hg, own_column, segment_ids, True
    )
    pairs, memory_t = pairs_call(memory, weights, w2, 1)
    normed0, rstd0, cross_entry_t, queries = middle_call(
        self_mix, target, token_hot, lang_rows, vec, weights, 0, 1, w1
    )
    cross_mix, cross_mix_t, cross_levels = attend_call(
        cross_table, queries, 0, pairs, 0, pairs, hg, own_column, memory_segments, False
    )
    (
        layer_output, ffn_entry_t, act, branch_grad_t, pre_grad, residual1, cross_grad,
        cross_mix_grad, sums, bias_sum,
    ) = feed_call(
        cross_mix, normed0, cotangent, vec, in_bias, weights, 2 * w1 + w2, g_in, 0, g_out, at_out, w1
    )

    hidden_step = pl.BlockSpec((tokens, w4), lambda o: (0, o))
    if together:
        ffn_grads = feed_weight_grad(
            feed_out_kernel, branch_grad_t, whole(branch_grad_t.shape), act, hidden_step,
            outer, inner, rows, model, 1, 2 * w4,
        )
        ffn_grads = [feed_weight_grad(
            feed_in_kernel, ffn_entry_t, whole(ffn_entry_t.shape), pre_grad, hidden_step,
            outer, inner, rows, w4, 0, 2 * w4, ffn_grads,
        )]
    else:
        branch_grad = branch_grad_t.T
        ffn_grads = [
            feed_weight_grad(
                feed_in_kernel, ffn_entry_t, whole(ffn_entry_t.shape), pre_grad, hidden_step,
                outer, inner, rows, w4, 0, w4,
            ),
            feed_weight_grad(
                feed_rows_kernel, act, hidden_step, branch_grad, whole(branch_grad.shape),
                outer, inner, ffn_out.shape[0], model, 0, model,
            ),
        ]
    ffn_done = [joint_scatter(item) for item in ffn_grads]
    core, first_plane, second_plane = chain_stages(inner // 2)

    cross_mix_grad, _ = hold(cross_mix_grad, ffn_grads)
    queries_grad, pairs_grad = attend_back_call(
        cross_table, queries, 0, pairs, 0, pairs, hg, cross_mix_grad, cross_levels, own_column, memory_segments, False
    )
    start_grad, self_grad, self_mix_grad, sums0 = middle_back_call(
        residual1, queries_grad, normed0, rstd0, vec, weights, 1, 0, w1
    )
    lefts_a = [memory_t, cross_entry_t, cross_mix_t, self_mix_t]
    rights_a = [pairs_grad, queries_grad, cross_grad, self_grad]
    send_a = half_weight_grads(table, lefts_a, rights_a, inner, inner // 2)
    rights_a, send_a = hold(rights_a, send_a)
    keep_a = half_weight_grads(table, lefts_a, rights_a, inner, 0)
    parts_a = core(keep_a, send_a, devices)
    self_mix_grad, parts_a = hold(self_mix_grad, parts_a)
    (triple_grad,) = attend_back_call(
        self_table, triple, 0, triple, hg, triple, 2 * hg, self_mix_grad, self_levels, own_column, segment_ids, True
    )
    parts_a = first_plane(parts_a, devices)
    triple_grad, parts_a = hold(triple_grad, parts_a)
    send_c = half_weight_grads(table, [self_entry_t], [triple_grad], inner, inner // 2)
    triple_grad, send_c = hold(triple_grad, send_c)
    keep_c = half_weight_grads(table, [self_entry_t], [triple_grad], inner, 0)
    parts_c = core(keep_c, send_c, devices)
    parts_a = second_plane(parts_a, devices)
    triple_grad, parts_c, parts_a = hold(triple_grad, parts_c, parts_a)
    target_grad, memory_grad, lang_sum = entry_back_call(
        start_grad, triple_grad, pairs_grad, first_weights, w3, weights, w2, 1, token_t
    )
    parts_c = first_plane(parts_c, devices)
    done_a = outer_stage(parts_a, inner, devices)
    lang_sum, parts_c, done_a = hold(lang_sum, parts_c, done_a)

    stacked = jnp.concatenate(
        [lang_sum, sums0[0:1], sums[3:4], sums[0:1], sums0[1:2], sums[4:5], sums[1:2], sums[2:3]], axis=0
    )
    stacked = stacked.reshape(langs + 7, devices, piece).transpose(1, 0, 2)
    stacked = jnp.concatenate([stacked, bias_sum.reshape(devices, ratio, piece)], axis=1)
    order = inner_order[:, None] + inner * outer_places[None, :]
    stacked = jnp.take(stacked, order.reshape(-1), axis=0, mode="clip")
    stacked = stacked.reshape(2, inner // 2, outer, n_small, piece)
    parts_e = core_stage(stacked[0], stacked[1], devices)
    parts_c = second_plane(parts_c, devices)
    parts_e, parts_c = hold(parts_e, parts_c)
    parts_e = plane_stage(parts_e, devices)
    done_c = outer_stage(parts_c, inner, devices)
    parts_e, done_c = hold(parts_e, done_c)
    extra = outer_stage(parts_e, inner, devices)
    if together:
        ffn_in_grad = ffn_done[0][:, :w4]
        ffn_out_grad = ffn_done[0][:, w4:].reshape(rows, model // rows, rows)
        ffn_out_grad = ffn_out_grad.transpose(2, 1, 0).reshape(rows, model)
    else:
        ffn_in_grad, ffn_out_grad = ffn_done
    return (
        layer_output,
        target_grad,
        memory_grad,
        extra[:langs].T,
        done_c,
        done_a[:, w2 + 2 * w1:],
        done_a[:, w2:w2 + w1],
        done_a[:, :w2],
        done_a[:, w2 + w1:w2 + 2 * w1],
        ffn_in_grad,
        extra[langs + 7:].reshape(-1),
        ffn_out_grad,
        extra[langs + 6],
        extra[langs:langs + 3].T,
        extra[langs + 3:langs + 6].T,
    )


def solution(mesh):
    rows, cols, line = P(both, None), P("inner", "outer"), P(both)
    return jax.shard_map(
        per_device,
        mesh=mesh,
        in_specs=(
            rows, rows, rows, rows, rows, rows, rows, cols, cols, cols, cols, cols, cols, line, rows,
            line, rows, rows,
        ),
        out_specs=(
            rows, rows, rows, rows, cols, cols, cols, cols, cols, cols, line, rows, line, rows, rows,
        ),
        check_vma=False,
    )
```

```python
import functools

import jax
import jax.numpy as jnp
from jax import lax
from jax.experimental import pallas as pl
from jax.experimental.pallas import tpu as pltpu
from jax.sharding import PartitionSpec as P

HEADS = 16
HEAD_DIM = 64
GROUP = 4
BLOCK = 256
CHUNK = 128
WINDOWS = (256, 384, 512)

epsilon = 1e-05
masked_score = -1000000000.0
bf16 = jnp.bfloat16
f32 = jnp.float32
both = ("outer", "inner")
MIB = 1 << 20


def mm(left, right):
    return lax.dot_general(left, right, (((1,), (0,)), ((), ())), preferred_element_type=f32)


def mm_nt(left, right):
    return lax.dot_general(left, right, (((1,), (1,)), ((), ())), preferred_element_type=f32)


def params():
    return pltpu.CompilerParams(vmem_limit_bytes=60 * MIB)


def cost(flops, moved, trans=0):
    share = 64
    return pl.CostEstimate(
        flops=int(flops) // share, bytes_accessed=int(moved) // share, transcendentals=int(trans) // share
    )


def whole(shape):
    return pl.BlockSpec(shape, lambda *_: (0,) * len(shape), pipeline_mode=pl.Buffered(1))


def weight_step(model, width, at):
    return pl.BlockSpec((1, model, width), lambda o, *_: (o, 0, at))


def weight_block(packed, width, at):
    outer, model, _ = packed.shape
    return pl.BlockSpec(
        (outer, model, width), lambda *_: (0, 0, at), pipeline_mode=pl.Buffered(1)
    )


def normalise(matrix):
    centred = matrix - jnp.mean(matrix, axis=-1, keepdims=True)
    rstd = lax.rsqrt(jnp.mean(centred * centred, axis=-1, keepdims=True) + epsilon)
    return centred * rstd, rstd


def norm_back(grad, gain, normed, rstd):
    scaled = grad * gain
    mean_scaled = jnp.mean(scaled, axis=-1, keepdims=True)
    mean_product = jnp.mean(scaled * normed, axis=-1, keepdims=True)
    return (scaled - mean_scaled - normed * mean_product) * rstd


def column_sum(matrix):
    return jnp.sum(matrix, axis=0, keepdims=True)


def triple_kernel(target_ref, token_ref, lang_ref, weight_ref, out_ref, entry_t_ref, entry_ref):
    @pl.when(pl.program_id(0) == 0)
    def _():
        start = target_ref[...].astype(f32) + mm(token_ref[...], lang_ref[...])
        entry_ref[...] = start.astype(bf16)
        entry_t_ref[...] = entry_ref[...].T

    out_ref[...] = mm(entry_ref[...], weight_ref[0]).astype(bf16)


def triple_call(target, token_hot, lang_rows, packed, width, at):
    tokens, model = target.shape
    outer = packed.shape[0]
    return pl.pallas_call(
        triple_kernel,
        grid=(outer,),
        in_specs=[
            whole(target.shape), whole(token_hot.shape), whole(lang_rows.shape),
            weight_step(model, width, at),
        ],
        out_specs=[pl.BlockSpec((tokens, width), lambda o: (0, o)), whole((model, tokens))],
        out_shape=[
            jax.ShapeDtypeStruct((tokens, outer * width), bf16),
            jax.ShapeDtypeStruct((model, tokens), bf16),
        ],
        scratch_shapes=[pltpu.VMEM((tokens, model), bf16)],
        compiler_params=params(),
        cost_estimate=cost(2 * tokens * model * outer * width, 16 * MIB),
        name="triple",
    )(target, token_hot, lang_rows, packed)


def pairs_kernel(memory_ref, weight_ref, out_ref, memory_t_ref):
    @pl.when(pl.program_id(0) == 0)
    def _():
        memory_t_ref[...] = memory_ref[...].T

    out_ref[...] = mm(memory_ref[...], weight_ref[0]).astype(bf16)


def pairs_call(memory, packed, width, at):
    tokens, model = memory.shape
    outer = packed.shape[0]
    return pl.pallas_call(
        pairs_kernel,
        grid=(outer,),
        in_specs=[whole(memory.shape), weight_step(model, width, at)],
        out_specs=[pl.BlockSpec((tokens, width), lambda o: (0, o)), whole((model, tokens))],
        out_shape=[
            jax.ShapeDtypeStruct((tokens, outer * width), bf16),
            jax.ShapeDtypeStruct((model, tokens), bf16),
        ],
        compiler_params=params(),
        cost_estimate=cost(2 * tokens * model * outer * width, 8 * MIB),
        name="pairs",
    )(memory, packed)


def mask_bias(own_ref, other_ref, start, window, causal):
    block = own_ref.shape[0]
    allowed = own_ref[...] == other_ref[:, pl.ds(start, window)]
    if causal:
        own_at = pl.program_id(0) * block + lax.broadcasted_iota(jnp.int32, (block, window), 0)
        other_at = start + lax.broadcasted_iota(jnp.int32, (block, window), 1)
        allowed = allowed & (own_at >= other_at)
    return jnp.where(allowed, 0.0, masked_score).astype(f32)


def for_window(table_ref, body):
    block_index = pl.program_id(0)
    start = pl.multiple_of(table_ref[block_index], CHUNK)
    chunks = table_ref[pl.num_programs(0) + block_index]
    for window in WINDOWS:
        @pl.when(chunks == window // CHUNK)
        def _():
            body(start, window)


def self_windows(ids):
    blocks = ids.shape[0] // BLOCK
    below = jnp.sum(ids[None, :] < ids[::BLOCK][:, None], axis=1)
    start = below // CHUNK * CHUNK
    ends = (jnp.arange(blocks) + 1) * BLOCK
    return jnp.concatenate([start, (ends - start) // CHUNK]).astype(jnp.int32)


def cross_windows(ids, others):
    below = jnp.sum(others[None, :] < ids[::BLOCK][:, None], axis=1)
    ends = jnp.sum(others[None, :] <= ids[BLOCK - 1::BLOCK][:, None], axis=1)
    start = below // CHUNK * CHUNK
    chunks = jnp.clip((ends - start + CHUNK - 1) // CHUNK, WINDOWS[0] // CHUNK, WINDOWS[-1] // CHUNK)
    start = jnp.minimum(start, others.shape[0] - chunks * CHUNK)
    return jnp.concatenate([start, chunks]).astype(jnp.int32)


def attend_kernel(
    causal, table_ref, q_ref, k_ref, v_ref, own_ref, other_ref, mix_ref, mix_t_ref, level_ref, bias_ref
):
    group = pl.program_id(1)
    width = q_ref.shape[1]
    owner = lax.broadcasted_iota(jnp.int32, (1, width), 1) // HEAD_DIM
    lane = lax.broadcasted_iota(jnp.int32, (1, 128), 1)

    def body(start, window):
        @pl.when(group == 0)
        def _():
            bias_ref[:, :window] = mask_bias(own_ref, other_ref, start, window, causal)
            level_ref[...] = jnp.zeros_like(level_ref)

        queries = q_ref[...] * bf16(HEAD_DIM ** -0.5)
        keys = k_ref[pl.ds(start, window), :]
        values = v_ref[pl.ds(start, window), :]
        bias = bias_ref[:, :window]
        mix = jnp.zeros(q_ref.shape, f32)
        levels = level_ref[...]
        for head in range(GROUP):
            chosen = owner == head
            scores = mm_nt(queries * chosen.astype(bf16), keys) + bias
            row_max = jnp.max(scores, axis=-1, keepdims=True)
            exps = jnp.exp(scores - row_max)
            total = jnp.sum(exps, axis=-1, keepdims=True)
            probs = (exps * (1.0 / total)).astype(bf16)
            mix = jnp.where(chosen, mm(probs, values), mix)
            levels = jnp.where(lane == group * GROUP + head, row_max + jnp.log(total), levels)
        mix = mix.astype(bf16)
        mix_ref[...] = mix
        mix_t_ref[...] = mix.T
        level_ref[...] = levels

    for_window(table_ref, body)


def attend_call(table, q_array, q_at, k_array, k_at, v_array, v_at, own_column, other_row, causal):
    tokens, others = q_array.shape[0], k_array.shape[0]
    width = GROUP * HEAD_DIM
    model = HEADS * HEAD_DIM
    return pl.pallas_call(
        functools.partial(attend_kernel, causal),
        grid_spec=pltpu.PrefetchScalarGridSpec(
            num_scalar_prefetch=1,
            grid=(tokens // BLOCK, HEADS // GROUP),
            in_specs=[
                pl.BlockSpec((BLOCK, width), lambda b, g, t: (b, q_at + g)),
                pl.BlockSpec((others, width), lambda b, g, t: (0, k_at + g)),
                pl.BlockSpec((others, width), lambda b, g, t: (0, v_at + g)),
                pl.BlockSpec((BLOCK, 1), lambda b, g, t: (b, 0)),
                pl.BlockSpec((1, others), lambda b, g, t: (0, 0)),
            ],
            out_specs=[
                pl.BlockSpec((BLOCK, width), lambda b, g, t: (b, g)),
                pl.BlockSpec((width, BLOCK), lambda b, g, t: (g, b)),
                pl.BlockSpec((BLOCK, 128), lambda b, g, t: (b, 0)),
            ],
            scratch_shapes=[pltpu.VMEM((BLOCK, WINDOWS[-1]), f32)],
        ),
        out_shape=[
            jax.ShapeDtypeStruct((tokens, model), bf16),
            jax.ShapeDtypeStruct((model, tokens), bf16),
            jax.ShapeDtypeStruct((tokens, 128), f32),
        ],
        compiler_params=params(),
        cost_estimate=cost(12e9, 12 * MIB, HEADS * tokens * 384),
        name="attend",
    )(table, q_array, k_array, v_array, own_column, other_row)


def attend_back_kernel(
    causal, table_ref, q_ref, k_ref, v_ref, grad_ref, level_ref, own_ref, other_ref, *rest
):
    if causal:
        out_ref, keys_t, values_t = rest
    else:
        out_ref, pair_ref, keys_t, values_t = rest
    block_index = pl.program_id(0)
    group = pl.program_id(1)
    blocks = pl.num_programs(0)
    width = q_ref.shape[1]
    model = HEADS * HEAD_DIM
    rows = pl.ds(pl.multiple_of(group * width, width), width)
    columns = pl.multiple_of(group * width, width)
    owner = lax.broadcasted_iota(jnp.int32, (1, width), 1) // HEAD_DIM
    lane = lax.broadcasted_iota(jnp.int32, (1, 128), 1)

    @pl.when(block_index == 0)
    def _():
        keys_t[rows, :] = jnp.zeros((width, keys_t.shape[1]), f32)
        values_t[rows, :] = jnp.zeros((width, keys_t.shape[1]), f32)

    def body(start, window):
        bias = mask_bias(own_ref, other_ref, start, window, causal)
        queries = q_ref[...] * bf16(HEAD_DIM ** -0.5)
        grads = grad_ref[...]
        queries_t = queries.T
        grads_t = grads.T
        spot = pl.ds(start, window)
        keys = k_ref[spot, :]
        values = v_ref[spot, :]
        levels = level_ref[...]
        grad_q = jnp.zeros(q_ref.shape, f32)
        for head in range(GROUP):
            chosen = owner == head
            picked = chosen.astype(bf16)
            scores = mm_nt(queries * picked, keys) + bias
            level = jnp.sum(
                jnp.where(lane == group * GROUP + head, levels, 0.0), axis=-1, keepdims=True
            )
            probs = jnp.exp(scores - level)
            grad_probs = mm_nt(grads * picked, values)
            inner = jnp.sum(probs * grad_probs, axis=-1, keepdims=True)
            grad_scores = (probs * (grad_probs - inner)).astype(bf16)
            band = slice(head * HEAD_DIM, (head + 1) * HEAD_DIM)
            target_rows = pl.ds(
                pl.multiple_of(group * width + head * HEAD_DIM, HEAD_DIM), HEAD_DIM
            )
            values_t[target_rows, spot] += mm(grads_t[band, :], probs.astype(bf16))
            keys_t[target_rows, spot] += mm(queries_t[band, :], grad_scores)
            grad_q = jnp.where(chosen, mm(grad_scores, keys), grad_q)
        grad_q = (grad_q * HEAD_DIM ** -0.5).astype(bf16)
        own_rows = pl.ds(pl.multiple_of(block_index * BLOCK, BLOCK), BLOCK)
        out_ref[own_rows, pl.ds(columns, width)] = grad_q

    for_window(table_ref, body)
    pair_out, shift = (out_ref, model) if causal else (pair_ref, 0)

    @pl.when(block_index == blocks - 1)
    def _():
        pair_out[:, pl.ds(columns + shift, width)] = keys_t[rows, :].astype(bf16).T
        pair_out[:, pl.ds(columns + shift + model, width)] = values_t[rows, :].astype(bf16).T


def attend_back_call(
    table, q_array, q_at, k_array, k_at, v_array, v_at, grad_mix, levels, own_column, other_row, causal
):
    tokens, others = q_array.shape[0], k_array.shape[0]
    width = GROUP * HEAD_DIM
    model = HEADS * HEAD_DIM
    if causal:
        out_shape = [jax.ShapeDtypeStruct((tokens, 3 * model), bf16)]
    else:
        out_shape = [
            jax.ShapeDtypeStruct((tokens, model), bf16),
            jax.ShapeDtypeStruct((others, 2 * model), bf16),
        ]
    return pl.pallas_call(
        functools.partial(attend_back_kernel, causal),
        grid_spec=pltpu.PrefetchScalarGridSpec(
            num_scalar_prefetch=1,
            grid=(tokens // BLOCK, HEADS // GROUP),
            in_specs=[
                pl.BlockSpec((BLOCK, width), lambda b, g, t: (b, q_at + g)),
                pl.BlockSpec((others, width), lambda b, g, t: (0, k_at + g)),
                pl.BlockSpec((others, width), lambda b, g, t: (0, v_at + g)),
                pl.BlockSpec((BLOCK, width), lambda b, g, t: (b, g)),
                pl.BlockSpec((BLOCK, 128), lambda b, g, t: (b, 0)),
                pl.BlockSpec((BLOCK, 1), lambda b, g, t: (b, 0)),
                pl.BlockSpec((1, others), lambda b, g, t: (0, 0)),
            ],
            out_specs=[whole(item.shape) for item in out_shape],
            scratch_shapes=[pltpu.VMEM((model, others), f32), pltpu.VMEM((model, others), f32)],
        ),
        out_shape=out_shape,
        compiler_params=params(),
        cost_estimate=cost(30e9, 16 * MIB, HEADS * tokens * 384),
        name="attend_back",
    )(table, q_array, k_array, v_array, grad_mix, levels, own_column, other_row)


def middle_kernel(
    mix_ref, target_ref, token_ref, lang_ref, vec_ref, out_weight_ref, query_weight_ref,
    normed_ref, rstd_ref, entry_t_ref, queries_ref,
):
    outer, _, width = out_weight_ref.shape
    start = target_ref[...].astype(f32) + mm(token_ref[...], lang_ref[...])
    mix = mix_ref[...]
    branch = jnp.concatenate([mm(mix, out_weight_ref[o]) for o in range(outer)], axis=1)
    normed, rstd = normalise(2.0 * start + branch)
    normed_ref[...] = normed
    rstd_ref[...] = rstd
    entry = (normed * vec_ref[0:1, :] + vec_ref[3:4, :]).astype(bf16)
    entry_t_ref[...] = entry.T
    for o in range(outer):
        queries_ref[:, o * width:(o + 1) * width] = mm(entry, query_weight_ref[o]).astype(bf16)


def middle_call(mix, target, token_hot, lang_rows, vec, packed, at_self, at_cross, width):
    tokens, model = target.shape
    row = lambda r: (r, 0)
    return pl.pallas_call(
        middle_kernel,
        grid=(tokens // BLOCK,),
        in_specs=[
            pl.BlockSpec((BLOCK, model), row),
            pl.BlockSpec((BLOCK, model), row),
            pl.BlockSpec((BLOCK, 128), row),
            whole(lang_rows.shape),
            whole(vec.shape),
            weight_block(packed, width, at_self),
            weight_block(packed, width, at_cross),
        ],
        out_specs=[
            pl.BlockSpec((BLOCK, model), row),
            pl.BlockSpec((BLOCK, 1), row),
            pl.BlockSpec((model, BLOCK), lambda r: (0, r)),
            pl.BlockSpec((BLOCK, model), row),
        ],
        out_shape=[
            jax.ShapeDtypeStruct((tokens, model), f32),
            jax.ShapeDtypeStruct((tokens, 1), f32),
            jax.ShapeDtypeStruct((model, tokens), bf16),
            jax.ShapeDtypeStruct((tokens, model), bf16),
        ],
        compiler_params=params(),
        cost_estimate=cost(4 * tokens * model * model, 16 * MIB),
        name="middle",
    )(mix, target, token_hot, lang_rows, vec, packed, packed)


def feed_kernel(
    at_cross, at_in, at_out,
    mix_ref, normed_ref, cot_ref, vec_ref, bias_ref, cross_hbm, in_hbm, out_hbm,
    layer_ref, entry_t_ref, act_ref, branch_grad_t_ref, pre_grad_ref, residual_ref, cross_grad_ref,
    mix_grad_ref, sums_ref, bias_sum_ref,
    cross_weight, in_weight, out_weight, slope, sems,
):
    outer, _, width = cross_weight.shape
    chunk = in_weight.shape[2]
    step = pl.program_id(0)

    def cross_copy():
        return pltpu.make_async_copy(
            cross_hbm.at[:, :, pl.ds(at_cross, width)], cross_weight, sems.at[0]
        )

    def in_copy(o):
        return pltpu.make_async_copy(
            in_hbm.at[o, :, pl.ds(at_in, chunk)], in_weight.at[o], sems.at[1 + o]
        )

    def out_copy(o):
        return pltpu.make_async_copy(
            out_hbm.at[o, :, pl.ds(at_out, out_weight.shape[2])], out_weight.at[o],
            sems.at[1 + outer + o],
        )


    @pl.when(step == 0)
    def _():
        cross_copy().start()
        for o in range(outer):
            in_copy(o).start()
            out_copy(o).start()
        sums_ref[...] = jnp.zeros_like(sums_ref)
        bias_sum_ref[...] = jnp.zeros_like(bias_sum_ref)
        cross_copy().wait()

    gain0, gain1, gain2 = vec_ref[0:1, :], vec_ref[1:2, :], vec_ref[2:3, :]
    shift0, shift1, shift2 = vec_ref[3:4, :], vec_ref[4:5, :], vec_ref[5:6, :]
    first = normed_ref[...] * gain0 + shift0
    mix = mix_ref[...]
    branch = jnp.concatenate([mm(mix, cross_weight[o]) for o in range(outer)], axis=1)
    normed1, rstd1 = normalise(2.0 * first + branch)
    second = normed1 * gain1 + shift1
    entry = second.astype(bf16)
    entry_t_ref[...] = entry.T
    total = 2.0 * second + vec_ref[6:7, :]
    for o in range(outer):
        @pl.when(step == 0)
        def _():
            in_copy(o).wait()
            out_copy(o).wait()

        span = slice(o * chunk, (o + 1) * chunk)
        pre = mm(entry, in_weight[o]) + bias_ref[:, span]
        half = 0.5 + 0.5 * lax.erf(pre * (0.5 ** 0.5))
        slope[:, span] = half + pre * (jnp.exp(-0.5 * pre * pre) * 0.3989422804014327)
        act = (pre * half).astype(bf16)
        act_ref[:, span] = act
        total = total + mm(act, out_weight[o])
    normed2, rstd2 = normalise(total)
    layer_ref[...] = (normed2 * gain2 + shift2).astype(bf16)
    cot = cot_ref[...].astype(f32)
    sums_ref[0:1, :] += column_sum(cot * normed2)
    sums_ref[1:2, :] += column_sum(cot)
    back2 = norm_back(cot, gain2, normed2, rstd2)
    branch_grad = back2.astype(bf16)
    branch_grad_t_ref[...] = branch_grad.T
    sums_ref[2:3, :] += column_sum(branch_grad.astype(f32))
    grad_second = 2.0 * back2
    for o in range(outer):
        span = slice(o * chunk, (o + 1) * chunk)
        pre_grad = (mm_nt(branch_grad, out_weight[o]) * slope[:, span]).astype(bf16)
        pre_grad_ref[:, span] = pre_grad
        bias_sum_ref[:, span] += column_sum(pre_grad.astype(f32))
        grad_second = grad_second + mm_nt(pre_grad, in_weight[o])
    sums_ref[3:4, :] += column_sum(grad_second * normed1)
    sums_ref[4:5, :] += column_sum(grad_second)
    back1 = norm_back(grad_second, gain1, normed1, rstd1)
    residual_ref[...] = back1
    cross_grad = back1.astype(bf16)
    cross_grad_ref[...] = cross_grad
    mix_grad = mm_nt(cross_grad[:, 0:width], cross_weight[0])
    for o in range(1, outer):
        mix_grad = mix_grad + mm_nt(
            cross_grad[:, o * width:(o + 1) * width], cross_weight[o]
        )
    mix_grad_ref[...] = mix_grad.astype(bf16)


def feed_call(mix, normed, cot, vec, bias, packed_cross, at_cross, packed_in, at_in, packed_out, at_out, width):
    tokens, model = mix.shape
    hidden = bias.shape[1]
    outer = packed_cross.shape[0]
    chunk = hidden // outer
    row = lambda r: (r, 0)
    blocked = lambda cols: pl.BlockSpec((BLOCK, cols), row)
    anywhere = pl.BlockSpec(memory_space=pl.ANY)
    turned = pl.BlockSpec((model, BLOCK), lambda r: (0, r))
    turned_shape = jax.ShapeDtypeStruct((model, tokens), bf16)
    out = lambda cols, kind: jax.ShapeDtypeStruct((tokens, cols), kind)
    return pl.pallas_call(
        functools.partial(feed_kernel, at_cross, at_in, at_out),
        grid=(tokens // BLOCK,),
        in_specs=[
            blocked(model), blocked(model), blocked(model),
            whole(vec.shape), whole(bias.shape), anywhere, anywhere, anywhere,
        ],
        out_specs=[
            blocked(model), turned, blocked(hidden), turned, blocked(hidden),
            blocked(model), blocked(model), blocked(model),
            pl.BlockSpec((8, model), lambda r: (0, 0)),
            pl.BlockSpec((1, hidden), lambda r: (0, 0)),
        ],
        out_shape=[
            out(model, bf16), turned_shape, out(hidden, bf16), turned_shape,
            out(hidden, bf16), out(model, f32), out(model, bf16), out(model, bf16),
            jax.ShapeDtypeStruct((8, model), f32),
            jax.ShapeDtypeStruct((1, hidden), f32),
        ],
        scratch_shapes=[
            pltpu.VMEM((outer, model, width), bf16),
            pltpu.VMEM((outer, model, chunk), bf16),
            pltpu.VMEM((outer, chunk, model), bf16),
            pltpu.VMEM((BLOCK, hidden), f32),
            pltpu.SemaphoreType.DMA((1 + 2 * outer,)),
        ],
        compiler_params=params(),
        cost_estimate=cost(36 * tokens * model * model, 60 * MIB, tokens * hidden * 2),
        name="feed",
    )(mix, normed, cot, vec, bias, packed_cross, packed_in, packed_out)


def middle_back_kernel(
    residual_ref, queries_grad_ref, normed_ref, rstd_ref, vec_ref, query_weight_ref, out_weight_ref,
    start_ref, branch_grad_ref, mix_grad_ref, sums_ref,
):
    outer, _, width = out_weight_ref.shape

    @pl.when(pl.program_id(0) == 0)
    def _():
        sums_ref[...] = jnp.zeros_like(sums_ref)

    grad_first = 2.0 * residual_ref[...]
    for o in range(outer):
        grad_first = grad_first + mm_nt(
            queries_grad_ref[:, o * width:(o + 1) * width], query_weight_ref[o]
        )
    normed = normed_ref[...]
    sums_ref[0:1, :] += column_sum(grad_first * normed)
    sums_ref[1:2, :] += column_sum(grad_first)
    back = norm_back(grad_first, vec_ref[0:1, :], normed, rstd_ref[...])
    start_ref[...] = back
    branch_grad = back.astype(bf16)
    branch_grad_ref[...] = branch_grad
    mix_grad = mm_nt(branch_grad[:, 0:width], out_weight_ref[0])
    for o in range(1, outer):
        mix_grad = mix_grad + mm_nt(
            branch_grad[:, o * width:(o + 1) * width], out_weight_ref[o]
        )
    mix_grad_ref[...] = mix_grad.astype(bf16)


def middle_back_call(residual, queries_grad, normed, rstd, vec, packed, at_cross, at_self, width):
    tokens, model = residual.shape
    row = lambda r: (r, 0)
    blocked = pl.BlockSpec((BLOCK, model), row)
    return pl.pallas_call(
        middle_back_kernel,
        grid=(tokens // BLOCK,),
        in_specs=[
            blocked, blocked, blocked,
            pl.BlockSpec((BLOCK, 1), row),
            whole(vec.shape),
            weight_block(packed, width, at_cross),
            weight_block(packed, width, at_self),
        ],
        out_specs=[blocked, blocked, blocked, pl.BlockSpec((8, model), lambda r: (0, 0))],
        out_shape=[
            jax.ShapeDtypeStruct((tokens, model), f32),
            jax.ShapeDtypeStruct((tokens, model), bf16),
            jax.ShapeDtypeStruct((tokens, model), bf16),
            jax.ShapeDtypeStruct((8, model), f32),
        ],
        compiler_params=params(),
        cost_estimate=cost(4 * tokens * model * model, 22 * MIB),
        name="middle_back",
    )(residual, queries_grad, normed, rstd, vec, packed, packed)


def half_kernel(count, first, table_ref, *refs):
    lefts, rights = refs[:count], refs[count:2 * count]
    out_ref, held, sems = refs[2 * count], refs[2 * count + 1:-1], refs[-1]
    part, _, piece, _ = out_ref.shape
    step = pl.program_id(0)

    def copy(at, row):
        source = pl.multiple_of(table_ref[first + row] * piece, piece)
        return pltpu.make_async_copy(
            lefts[at].at[pl.ds(source, piece), :], held[at].at[pl.ds(row * piece, piece), :],
            sems.at[at, row],
        )

    @pl.when(step == 0)
    def _():
        for at in range(count):
            for row in range(part):
                copy(at, row).start()

    lo = 0
    for at in range(count):
        @pl.when(step == 0)
        def _():
            for row in range(part):
                copy(at, row).wait()

        width = rights[at].shape[1]
        product = mm(held[at][...], rights[at][...]).astype(bf16)
        out_ref[:, 0, :, lo:lo + width] = product.reshape(part, piece, width)
        lo += width


def half_weight_grads(table, lefts, rights, inner, first):
    outer = table.shape[0] - inner
    part, piece = inner // 2, lefts[0].shape[0] // inner
    widths = [right.shape[1] // outer for right in rights]
    flops = sum(right.size for right in rights) * part * piece * 2
    return pl.pallas_call(
        functools.partial(half_kernel, len(lefts), first),
        grid_spec=pltpu.PrefetchScalarGridSpec(
            num_scalar_prefetch=1,
            grid=(outer,),
            in_specs=[pl.BlockSpec(memory_space=pl.ANY)] * len(lefts) + [
                pl.BlockSpec((right.shape[0], width), lambda o, table: (0, o))
                for right, width in zip(rights, widths)
            ],
            out_specs=pl.BlockSpec(
                (part, 1, piece, sum(widths)), lambda o, table: (0, table[inner + o], 0, 0)
            ),
            scratch_shapes=[pltpu.VMEM((part * piece, left.shape[1]), bf16) for left in lefts]
            + [pltpu.SemaphoreType.DMA((len(lefts), part))],
        ),
        out_shape=jax.ShapeDtypeStruct((part, outer, piece, sum(widths)), bf16),
        compiler_params=params(),
        cost_estimate=cost(flops, 12 * MIB),
        name="half_weight_grads",
    )(table, *lefts, *rights)


def feed_out_half_kernel(first, table_ref, left_ref, right_ref, out_ref, held):
    part, _, piece, width = out_ref.shape
    for row in range(part):
        column = pl.multiple_of(table_ref[first + row] * piece, piece)
        held[:, row * piece:(row + 1) * piece] = right_ref[:, pl.ds(column, piece)]
    product = mm(left_ref[...], held[...]).astype(bf16)
    for row in range(part):
        for b in range(width // piece):
            out_ref[row, 0, :, b * piece:(b + 1) * piece] = product[
                b * piece:(b + 1) * piece, row * piece:(row + 1) * piece
            ]


def feed_out_half(table, left, right, inner, first):
    outer = table.shape[0] - inner
    model, tokens = left.shape
    width = right.shape[1] // outer
    part, piece = inner // 2, width // inner
    return pl.pallas_call(
        functools.partial(feed_out_half_kernel, first),
        grid_spec=pltpu.PrefetchScalarGridSpec(
            num_scalar_prefetch=1,
            grid=(outer,),
            in_specs=[
                whole(left.shape), pl.BlockSpec((tokens, width), lambda o, table: (0, o)),
            ],
            out_specs=pl.BlockSpec(
                (part, 1, piece, model), lambda o, table: (0, table[inner + o], 0, 0)
            ),
            scratch_shapes=[pltpu.VMEM((tokens, part * piece), bf16)],
        ),
        out_shape=jax.ShapeDtypeStruct((part, outer, piece, model), bf16),
        compiler_params=params(),
        cost_estimate=cost(right.size * model, 16 * MIB),
        name="feed_out_half",
    )(table, left, right)


def feed_in_kernel(left_ref, right_ref, out_ref):
    _, inner, piece, width = out_ref.shape
    product = mm(left_ref[...], right_ref[...]).astype(bf16)
    out_ref[0] = product.reshape(inner, piece, width)


def feed_rows_kernel(left_ref, right_ref, out_ref):
    _, inner, piece, width = out_ref.shape
    product = mm(left_ref[...].T, right_ref[...]).astype(bf16)
    out_ref[0] = product.reshape(inner, piece, width)


def feed_weight_grad(kernel, left, left_spec, right, right_spec, outer, inner, piece, width):
    return pl.pallas_call(
        kernel,
        grid=(outer,),
        in_specs=[left_spec, right_spec],
        out_specs=pl.BlockSpec((1, inner, piece, width), lambda o: (o, 0, 0, 0)),
        out_shape=jax.ShapeDtypeStruct((outer, inner, piece, width), bf16),
        compiler_params=params(),
        cost_estimate=cost(8 * left.shape[1] * 1024 * 1024, 24 * MIB),
        name="feed_weight_grad",
    )(left, right)


def entry_back_kernel(
    start_ref, triple_ref, pairs_ref, weight_ref, pairs_weight_ref, token_t_ref,
    out_ref, memory_ref, lang_ref,
):
    outer, _, width = weight_ref.shape
    pair_width = pairs_weight_ref.shape[2]

    @pl.when(pl.program_id(0) == 0)
    def _():
        lang_ref[...] = jnp.zeros_like(lang_ref)

    grad = 2.0 * start_ref[...]
    for o in range(outer):
        grad = grad + mm_nt(triple_ref[:, o * width:(o + 1) * width], weight_ref[o])
    out_ref[...] = grad
    high = grad.astype(bf16)
    rest = grad - high.astype(f32)
    mid = rest.astype(bf16)
    low = (rest - mid.astype(f32)).astype(bf16)
    token_t = token_t_ref[...]
    lang_ref[...] += mm(token_t, high) + mm(token_t, mid) + mm(token_t, low)
    memory_grad = mm_nt(pairs_ref[:, 0:pair_width], pairs_weight_ref[0])
    for o in range(1, outer):
        memory_grad = memory_grad + mm_nt(
            pairs_ref[:, o * pair_width:(o + 1) * pair_width], pairs_weight_ref[o]
        )
    memory_ref[...] = memory_grad


def entry_back_call(start_grad, triple_grad, pairs_grad, packed, width, pairs_packed, pairs_width, at, token_t):
    tokens, model = start_grad.shape
    outer = packed.shape[0]
    steps = tokens // BLOCK
    memory_block = pairs_grad.shape[0] // steps
    row = lambda r: (r, 0)
    return pl.pallas_call(
        entry_back_kernel,
        grid=(steps,),
        in_specs=[
            pl.BlockSpec((BLOCK, model), row),
            pl.BlockSpec((BLOCK, outer * width), row),
            pl.BlockSpec((memory_block, outer * pairs_width), row),
            weight_block(packed, width, 0),
            weight_block(pairs_packed, pairs_width, at),
            pl.BlockSpec((token_t.shape[0], BLOCK), lambda r: (0, r)),
        ],
        out_specs=[
            pl.BlockSpec((BLOCK, model), row),
            pl.BlockSpec((memory_block, model), row),
            pl.BlockSpec((token_t.shape[0], model), lambda r: (0, 0)),
        ],
        out_shape=[
            jax.ShapeDtypeStruct((tokens, model), f32),
            jax.ShapeDtypeStruct(pairs_grad.shape[:1] + (model,), f32),
            jax.ShapeDtypeStruct((token_t.shape[0], model), f32),
        ],
        compiler_params=params(),
        cost_estimate=cost(2 * tokens * model * outer * (width + pairs_width // 2), 40 * MIB),
        name="entry_back",
    )(start_grad, triple_grad, pairs_grad, packed, pairs_packed, token_t)


def gather(shard, outer):
    full = lax.all_gather(shard, both, axis=0, tiled=True)
    return full.reshape(outer, full.shape[0] // outer, full.shape[1])


def swap(value, distance, devices):
    return lax.ppermute(value, both, [(d, d ^ distance) for d in range(devices)])


def total_of(pieces, kind):
    total = pieces[0].astype(f32)
    for item in pieces[1:]:
        total = total + item.astype(f32)
    return total.astype(kind)


def hold(*values):
    return lax.optimization_barrier(values)


def core_stage(keep, send, devices):
    moved = swap(send, 1, devices)
    return [total_of((keep[k], moved[k]), keep.dtype) for k in range(keep.shape[0])]


def plane_stage(parts, devices):
    moved = [parts[0]] + [swap(parts[k], 2 * k, devices) for k in range(1, len(parts))]
    return [total_of([item[o] for item in moved], parts[0].dtype) for o in range(parts[0].shape[0])]


def outer_stage(parts, inner, devices):
    moved = [parts[0]] + [swap(parts[k], inner * k, devices) for k in range(1, len(parts))]
    return total_of(moved, f32)


def joint_scatter(packed):
    outer, inner, rows, columns = packed.shape
    flat = packed.reshape(outer * inner * rows, columns)
    return lax.psum_scatter(flat, both, scatter_dimension=0, tiled=True).astype(f32)


def halves_of(keep, moved, along_x, columns=slice(None)):
    kept, sent = (slice(0, None, 2), slice(1, None, 2)) if along_x else (slice(0, 2), slice(2, 4))
    return [
        total_of((keep[rows, ..., columns], moved[rows, ..., columns]), keep.dtype)
        for rows in (kept, sent)
    ]


def core_halves(keep, send, devices):
    moved = swap(send, 1, devices)
    cut = keep.shape[-1] // 256 * 128
    return halves_of(keep, moved, True, slice(0, cut)) + halves_of(keep, moved, False, slice(cut, None))


def core_pair(keep_x, send_x, keep_y, send_y, devices):
    moved_x, moved_y = swap(send_x, 1, devices), swap(send_y, 1, devices)
    return halves_of(keep_x, moved_x, True) + halves_of(keep_y, moved_y, False)


def first_halves(parts, devices):
    keep_x, send_x, keep_y, send_y = parts
    result = []
    for keep, send, distance in ((keep_x, send_x, 2), (keep_y, send_y, 4)):
        moved = swap(send, distance, devices)
        result += [total_of((keep[k], moved[k]), keep.dtype) for k in range(2)]
    return result


def second_halves(parts, devices):
    keep_x, send_x, keep_y, send_y = parts
    moved_x, moved_y = swap(send_x, 4, devices), swap(send_y, 2, devices)
    return [
        jnp.concatenate(
            [total_of((keep_x[o], moved_x[o]), keep_x.dtype),
             total_of((keep_y[o], moved_y[o]), keep_y.dtype)], axis=-1,
        )
        for o in range(keep_x.shape[0])
    ]


def outer_steps(parts):
    return jnp.stack(parts[0::2]), jnp.stack(parts[1::2])


def outer_step(keep, send, distance, devices):
    moved = swap(send, distance, devices)
    if keep.shape[0] == 1:
        return keep[0].astype(f32) + moved[0].astype(f32)
    totals = [total_of((keep[k], moved[k]), keep.dtype) for k in range(keep.shape[0])]
    return outer_steps(totals)


def chain_stages(chips):
    if chips == 4:
        return core_halves, first_halves, second_halves
    return core_stage, plane_stage, lambda parts, devices: parts


def permuted_column(shard, outer, inner, devices):
    own = lax.axis_index("outer")
    column = jnp.zeros((outer,) + shard.shape, shard.dtype)
    for k in range(outer):
        moved = swap(shard, inner * k, devices) if k else shard
        column = lax.dynamic_update_slice(column, moved[None], (own ^ k, 0, 0))
    return column


def plane_moves(column, inner, devices):
    return [column] + [swap(column, 2 * k, devices) for k in range(1, inner // 2)]


def plane_place(moves):
    chip = lax.axis_index("inner") // 2
    outer, rows, columns = moves[0].shape
    plane = jnp.zeros((outer, len(moves), rows, columns), moves[0].dtype)
    for k, item in enumerate(moves):
        plane = lax.dynamic_update_slice(plane, item[:, None], (0, chip ^ k, 0, 0))
    return plane


def core_place(plane, moved):
    core = lax.rem(lax.axis_index("inner"), 2)
    mine = jnp.arange(2)[None, None, :, None, None] == core
    full = jnp.where(mine, plane[:, :, None], moved[:, :, None])
    outer, chips, _, rows, columns = full.shape
    return full.reshape(outer, chips * 2 * rows, columns)


def per_device(
    target, memory, cotangent, segment_ids, memory_segments, directions, lang_table,
    self_qkv, self_out, cross_q, cross_kv, cross_out, ffn_in, ffn_in_bias, ffn_out, ffn_out_bias,
    norm_gains, norm_biases,
):
    outer = lax.axis_size("outer")
    inner = lax.axis_size("inner")
    devices = outer * inner
    tokens, model = target.shape
    hidden = devices * ffn_in_bias.shape[0]
    langs = lang_table.shape[1]
    piece = model // devices
    rows = model // inner
    w3, w1, w2, w4 = 3 * model // outer, model // outer, 2 * model // outer, hidden // outer
    ratio = hidden // model
    together = ffn_out.shape[0] == rows and model == w4

    small = jnp.concatenate(
        [
            lang_table.T, norm_gains.T, norm_biases.T,
            ffn_out_bias.reshape(1, piece), ffn_in_bias.reshape(ratio, piece),
        ],
        axis=0,
    )
    n_small = small.shape[0]
    small = jnp.pad(small, ((0, rows - n_small), (0, 128 - piece)))
    first_weights = gather(jnp.concatenate([self_qkv, small], axis=1), outer)
    at_small = w3
    column = permuted_column(
        jnp.concatenate([self_out, cross_q, cross_kv, cross_out], axis=1), outer, inner, devices
    )
    moves = plane_moves(column, inner, devices)
    if together:
        shard, _ = hold(jnp.concatenate([ffn_in, ffn_out], axis=1), column)
        g_in = gather(shard, outer)
        g_out, at_out = g_in, w4
    else:
        g_in = gather(ffn_in, outer)
        g_out, at_out = gather(ffn_out, outer), 0

    first_weights, moves = hold(first_weights, moves)
    plane = plane_place(moves)
    core_move = swap(plane, 1, devices)
    my_inner, my_outer = lax.axis_index("inner"), lax.axis_index("outer")
    outer_places = jnp.arange(outer, dtype=jnp.int32) ^ my_outer
    inner_order = jnp.array(
        [chip * 2 + core for core in range(2) for chip in range(inner // 2)], jnp.int32
    ) ^ my_inner
    table = jnp.concatenate([inner_order, outer_places])
    seg = segment_ids.reshape(-1)
    hot_seg = seg[:, None] == jnp.arange(directions.shape[1])[None, :]
    token_dir = jnp.sum(jnp.where(hot_seg, directions.reshape(1, -1), 0), axis=-1)
    token_hot = (token_dir[:, None] == jnp.arange(128)[None, :]).astype(bf16)
    token_t = (jnp.arange(langs)[:, None] == token_dir[None, :]).astype(bf16)
    own_column = seg[:, None]
    self_table = self_windows(seg)
    cross_table = cross_windows(seg, memory_segments.reshape(-1))

    smalls = first_weights[:, :, at_small:at_small + piece].reshape(devices, rows, piece)[:, :n_small]
    smalls = smalls.transpose(1, 0, 2)
    lang_rows = jnp.pad(smalls[:langs].reshape(langs, model), ((0, 128 - langs), (0, 0)))
    vec = jnp.pad(smalls[langs:langs + 7].reshape(7, model).astype(f32), ((0, 1), (0, 0)))
    in_bias = smalls[langs + 7:].transpose(1, 0, 2).reshape(1, hidden).astype(f32)

    triple, self_entry_t = triple_call(target, token_hot, lang_rows, first_weights, w3, 0)
    triple, core_move = hold(triple, core_move)
    weights = core_place(plane, core_move)
    hg = HEADS // GROUP
    self_mix, self_mix_t, self_levels = attend_call(
        self_table, triple, 0, triple, hg, triple, 2 * hg, own_column, segment_ids, True
    )
    pairs, memory_t = pairs_call(memory, weights, w2, 1)
    normed0, rstd0, cross_entry_t, queries = middle_call(
        self_mix, target, token_hot, lang_rows, vec, weights, 0, 1, w1
    )
    cross_mix, cross_mix_t, cross_levels = attend_call(
        cross_table, queries, 0, pairs, 0, pairs, hg, own_column, memory_segments, False
    )
    (
        layer_output, ffn_entry_t, act, branch_grad_t, pre_grad, residual1, cross_grad,
        cross_mix_grad, sums, bias_sum,
    ) = feed_call(
        cross_mix, normed0, cotangent, vec, in_bias, weights, 2 * w1 + w2, g_in, 0, g_out, at_out, w1
    )

    core, first_plane, second_plane = chain_stages(inner // 2)
    chained = together and inner == 8
    if chained:
        half = inner // 2
        send_in = half_weight_grads(table, [ffn_entry_t], [pre_grad], inner, half)
        act, send_in = hold(act, send_in)
        send_out = feed_out_half(table, branch_grad_t, act, inner, half)
        pre_grad, send_out = hold(pre_grad, send_out)
        keep_in = half_weight_grads(table, [ffn_entry_t], [pre_grad], inner, 0)
        act, keep_in = hold(act, keep_in)
        keep_out = feed_out_half(table, branch_grad_t, act, inner, 0)
        parts_f = core_pair(keep_in, send_in, keep_out, send_out, devices)
    else:
        hidden_step = pl.BlockSpec((tokens, w4), lambda o: (0, o))
        branch_grad = branch_grad_t.T
        ffn_grads = [
            feed_weight_grad(
                feed_in_kernel, ffn_entry_t, whole(ffn_entry_t.shape), pre_grad, hidden_step,
                outer, inner, rows, w4,
            ),
            feed_weight_grad(
                feed_rows_kernel, act, hidden_step, branch_grad, whole(branch_grad.shape),
                outer, inner, ffn_out.shape[0], model,
            ),
        ]
        parts_f = ffn_done = [joint_scatter(item) for item in ffn_grads]
    cross_mix_grad, parts_f = hold(cross_mix_grad, parts_f)
    queries_grad, pairs_grad = attend_back_call(
        cross_table, queries, 0, pairs, 0, pairs, hg, cross_mix_grad, cross_levels, own_column, memory_segments, False
    )
    if chained:
        parts_f = first_halves(parts_f, devices)
    queries_grad, parts_f = hold(queries_grad, parts_f)
    start_grad, self_grad, self_mix_grad, sums0 = middle_back_call(
        residual1, queries_grad, normed0, rstd0, vec, weights, 1, 0, w1
    )
    lefts_a = [memory_t, cross_entry_t, cross_mix_t, self_mix_t]
    rights_a = [pairs_grad, queries_grad, cross_grad, self_grad]
    send_a = half_weight_grads(table, lefts_a, rights_a, inner, inner // 2)
    if chained:
        parts_f = outer_steps(second_halves(parts_f, devices))
    rights_a, send_a, parts_f = hold(rights_a, send_a, parts_f)
    keep_a = half_weight_grads(table, lefts_a, rights_a, inner, 0)
    parts_a = core(keep_a, send_a, devices)
    distance = inner
    if chained:
        parts_f = outer_step(*parts_f, distance, devices)
    self_mix_grad, parts_a, parts_f = hold(self_mix_grad, parts_a, parts_f)
    (triple_grad,) = attend_back_call(
        self_table, triple, 0, triple, hg, triple, 2 * hg, self_mix_grad, self_levels, own_column, segment_ids, True
    )
    parts_a = first_plane(parts_a, devices)
    while chained and isinstance(parts_f, (tuple, list)):
        distance *= 2
        parts_f = outer_step(*parts_f, distance, devices)
    done_f = parts_f
    triple_grad, parts_a, done_f = hold(triple_grad, parts_a, done_f)
    send_c = half_weight_grads(table, [self_entry_t], [triple_grad], inner, inner // 2)
    triple_grad, send_c = hold(triple_grad, send_c)
    keep_c = half_weight_grads(table, [self_entry_t], [triple_grad], inner, 0)
    parts_c = core(keep_c, send_c, devices)
    parts_a = second_plane(parts_a, devices)
    triple_grad, parts_c, parts_a = hold(triple_grad, parts_c, parts_a)
    target_grad, memory_grad, lang_sum = entry_back_call(
        start_grad, triple_grad, pairs_grad, first_weights, w3, weights, w2, 1, token_t
    )
    parts_c = first_plane(parts_c, devices)
    done_a = outer_stage(parts_a, inner, devices)
    lang_sum, parts_c, done_a = hold(lang_sum, parts_c, done_a)

    stacked = jnp.concatenate(
        [lang_sum, sums0[0:1], sums[3:4], sums[0:1], sums0[1:2], sums[4:5], sums[1:2], sums[2:3]], axis=0
    )
    stacked = stacked.reshape(langs + 7, devices, piece).transpose(1, 0, 2)
    stacked = jnp.concatenate([stacked, bias_sum.reshape(devices, ratio, piece)], axis=1)
    order = inner_order[:, None] + inner * outer_places[None, :]
    stacked = jnp.take(stacked, order.reshape(-1), axis=0, mode="clip")
    stacked = stacked.reshape(2, inner // 2, outer, n_small, piece)
    parts_e = core_stage(stacked[0], stacked[1], devices)
    parts_c = second_plane(parts_c, devices)
    parts_e, parts_c = hold(parts_e, parts_c)
    parts_e = plane_stage(parts_e, devices)
    done_c = outer_stage(parts_c, inner, devices)
    parts_e, done_c = hold(parts_e, done_c)
    extra = outer_stage(parts_e, inner, devices)
    if chained:
        ffn_in_grad = done_f[:, :w4]
        ffn_out_grad = done_f[:, w4:].reshape(rows, model // rows, rows)
        ffn_out_grad = ffn_out_grad.transpose(2, 1, 0).reshape(rows, model)
    else:
        ffn_in_grad, ffn_out_grad = ffn_done
    return (
        layer_output,
        target_grad,
        memory_grad,
        extra[:langs].T,
        done_c,
        done_a[:, w2 + 2 * w1:],
        done_a[:, w2:w2 + w1],
        done_a[:, :w2],
        done_a[:, w2 + w1:w2 + 2 * w1],
        ffn_in_grad,
        extra[langs + 7:].reshape(-1),
        ffn_out_grad,
        extra[langs + 6],
        extra[langs:langs + 3].T,
        extra[langs + 3:langs + 6].T,
    )


def solution(mesh):
    rows, cols, line = P(both, None), P("inner", "outer"), P(both)
    return jax.shard_map(
        per_device,
        mesh=mesh,
        in_specs=(
            rows, rows, rows, rows, rows, rows, rows, cols, cols, cols, cols, cols, cols, line, rows,
            line, rows, rows,
        ),
        out_specs=(
            rows, rows, rows, rows, cols, cols, cols, cols, cols, cols, line, rows, line, rows, rows,
        ),
        check_vma=False,
    )
```

```python
import functools

import jax
import jax.numpy as jnp
from jax import lax
from jax.experimental import pallas as pl
from jax.experimental.pallas import tpu as pltpu
from jax.sharding import PartitionSpec as P

HEADS = 16
HEAD_DIM = 64
GROUP = 4
BLOCK = 256
CHUNK = 128
WINDOWS = (256, 384, 512)

epsilon = 1e-05
masked_score = -1000000000.0
bf16 = jnp.bfloat16
f32 = jnp.float32
both = ("outer", "inner")
MIB = 1 << 20


def mm(left, right):
    return lax.dot_general(left, right, (((1,), (0,)), ((), ())), preferred_element_type=f32)


def mm_nt(left, right):
    return lax.dot_general(left, right, (((1,), (1,)), ((), ())), preferred_element_type=f32)


def params():
    return pltpu.CompilerParams(vmem_limit_bytes=60 * MIB)


def cost(flops, moved, trans=0):
    share = 64
    return pl.CostEstimate(
        flops=int(flops) // share, bytes_accessed=int(moved) // share, transcendentals=int(trans) // share
    )


def whole(shape):
    return pl.BlockSpec(shape, lambda *_: (0,) * len(shape), pipeline_mode=pl.Buffered(1))


def weight_step(model, width, at):
    return pl.BlockSpec((1, model, width), lambda o, *_: (o, 0, at))


def weight_slices(packed, width, at):
    outer, model, _ = packed.shape
    return [
        pl.BlockSpec((1, model, width), lambda *_, o=o: (o, 0, at), pipeline_mode=pl.Buffered(1))
        for o in range(outer)
    ]


def weight_block(packed, width, at):
    outer, model, _ = packed.shape
    return pl.BlockSpec(
        (outer, model, width), lambda *_: (0, 0, at), pipeline_mode=pl.Buffered(1)
    )


def normalise(matrix):
    centred = matrix - jnp.mean(matrix, axis=-1, keepdims=True)
    rstd = lax.rsqrt(jnp.mean(centred * centred, axis=-1, keepdims=True) + epsilon)
    return centred * rstd, rstd


def norm_back(grad, gain, normed, rstd):
    scaled = grad * gain
    mean_scaled = jnp.mean(scaled, axis=-1, keepdims=True)
    mean_product = jnp.mean(scaled * normed, axis=-1, keepdims=True)
    return (scaled - mean_scaled - normed * mean_product) * rstd


def column_sum(matrix):
    return jnp.sum(matrix, axis=0, keepdims=True)


def triple_kernel(target_ref, token_ref, lang_ref, weight_ref, out_ref, entry_t_ref, entry_ref):
    @pl.when(pl.program_id(0) == 0)
    def _():
        start = target_ref[...].astype(f32) + mm(token_ref[...], lang_ref[...])
        entry_ref[...] = start.astype(bf16)
        entry_t_ref[...] = entry_ref[...].T

    out_ref[...] = mm(entry_ref[...], weight_ref[0]).astype(bf16)


def triple_call(target, token_hot, lang_rows, packed, width, at):
    tokens, model = target.shape
    outer = packed.shape[0]
    return pl.pallas_call(
        triple_kernel,
        grid=(outer,),
        in_specs=[
            whole(target.shape), whole(token_hot.shape), whole(lang_rows.shape),
            weight_step(model, width, at),
        ],
        out_specs=[pl.BlockSpec((tokens, width), lambda o: (0, o)), whole((model, tokens))],
        out_shape=[
            jax.ShapeDtypeStruct((tokens, outer * width), bf16),
            jax.ShapeDtypeStruct((model, tokens), bf16),
        ],
        scratch_shapes=[pltpu.VMEM((tokens, model), bf16)],
        compiler_params=params(),
        cost_estimate=cost(2 * tokens * model * outer * width, 16 * MIB),
        name="triple",
    )(target, token_hot, lang_rows, packed)


def pairs_kernel(memory_ref, weight_ref, out_ref, memory_t_ref):
    @pl.when(pl.program_id(0) == 0)
    def _():
        memory_t_ref[...] = memory_ref[...].T

    out_ref[...] = mm(memory_ref[...], weight_ref[0]).astype(bf16)


def pairs_call(memory, packed, width, at):
    tokens, model = memory.shape
    outer = packed.shape[0]
    return pl.pallas_call(
        pairs_kernel,
        grid=(outer,),
        in_specs=[whole(memory.shape), weight_step(model, width, at)],
        out_specs=[pl.BlockSpec((tokens, width), lambda o: (0, o)), whole((model, tokens))],
        out_shape=[
            jax.ShapeDtypeStruct((tokens, outer * width), bf16),
            jax.ShapeDtypeStruct((model, tokens), bf16),
        ],
        compiler_params=params(),
        cost_estimate=cost(2 * tokens * model * outer * width, 8 * MIB),
        name="pairs",
    )(memory, packed)


def mask_bias(own_ref, other_ref, start, window, causal):
    block = own_ref.shape[0]
    allowed = own_ref[...] == other_ref[:, pl.ds(start, window)]
    if causal:
        own_at = pl.program_id(0) * block + lax.broadcasted_iota(jnp.int32, (block, window), 0)
        other_at = start + lax.broadcasted_iota(jnp.int32, (block, window), 1)
        allowed = allowed & (own_at >= other_at)
    return jnp.where(allowed, 0.0, masked_score).astype(f32)


def for_window(table_ref, body):
    block_index = pl.program_id(0)
    start = pl.multiple_of(table_ref[block_index], CHUNK)
    chunks = table_ref[pl.num_programs(0) + block_index]
    for window in WINDOWS:
        @pl.when(chunks == window // CHUNK)
        def _():
            body(start, window)


def self_windows(ids):
    blocks = ids.shape[0] // BLOCK
    below = jnp.sum(ids[None, :] < ids[::BLOCK][:, None], axis=1)
    start = below // CHUNK * CHUNK
    ends = (jnp.arange(blocks) + 1) * BLOCK
    return jnp.concatenate([start, (ends - start) // CHUNK]).astype(jnp.int32)


def cross_windows(ids, others):
    below = jnp.sum(others[None, :] < ids[::BLOCK][:, None], axis=1)
    ends = jnp.sum(others[None, :] <= ids[BLOCK - 1::BLOCK][:, None], axis=1)
    start = below // CHUNK * CHUNK
    chunks = jnp.clip((ends - start + CHUNK - 1) // CHUNK, WINDOWS[0] // CHUNK, WINDOWS[-1] // CHUNK)
    start = jnp.minimum(start, others.shape[0] - chunks * CHUNK)
    return jnp.concatenate([start, chunks]).astype(jnp.int32)


def attend_kernel(
    causal, table_ref, q_ref, k_ref, v_ref, own_ref, other_ref, mix_ref, mix_t_ref, level_ref, bias_ref
):
    group = pl.program_id(1)
    width = q_ref.shape[1]
    owner = lax.broadcasted_iota(jnp.int32, (1, width), 1) // HEAD_DIM
    lane = lax.broadcasted_iota(jnp.int32, (1, 128), 1)

    def body(start, window):
        @pl.when(group == 0)
        def _():
            bias_ref[:, :window] = mask_bias(own_ref, other_ref, start, window, causal)
            level_ref[...] = jnp.zeros_like(level_ref)

        queries = q_ref[...] * bf16(HEAD_DIM ** -0.5)
        keys = k_ref[pl.ds(start, window), :]
        values = v_ref[pl.ds(start, window), :]
        bias = bias_ref[:, :window]
        mix = jnp.zeros(q_ref.shape, f32)
        levels = level_ref[...]
        for head in range(GROUP):
            chosen = owner == head
            scores = mm_nt(queries * chosen.astype(bf16), keys) + bias
            row_max = jnp.max(scores, axis=-1, keepdims=True)
            exps = jnp.exp(scores - row_max)
            total = jnp.sum(exps, axis=-1, keepdims=True)
            probs = (exps * (1.0 / total)).astype(bf16)
            mix = jnp.where(chosen, mm(probs, values), mix)
            levels = jnp.where(lane == group * GROUP + head, row_max + jnp.log(total), levels)
        mix = mix.astype(bf16)
        mix_ref[...] = mix
        mix_t_ref[...] = mix.T
        level_ref[...] = levels

    for_window(table_ref, body)


def attend_call(table, q_array, q_at, k_array, k_at, v_array, v_at, own_column, other_row, causal):
    tokens, others = q_array.shape[0], k_array.shape[0]
    width = GROUP * HEAD_DIM
    model = HEADS * HEAD_DIM
    return pl.pallas_call(
        functools.partial(attend_kernel, causal),
        grid_spec=pltpu.PrefetchScalarGridSpec(
            num_scalar_prefetch=1,
            grid=(tokens // BLOCK, HEADS // GROUP),
            in_specs=[
                pl.BlockSpec((BLOCK, width), lambda b, g, t: (b, q_at + g)),
                pl.BlockSpec((others, width), lambda b, g, t: (0, k_at + g)),
                pl.BlockSpec((others, width), lambda b, g, t: (0, v_at + g)),
                pl.BlockSpec((BLOCK, 1), lambda b, g, t: (b, 0)),
                pl.BlockSpec((1, others), lambda b, g, t: (0, 0)),
            ],
            out_specs=[
                pl.BlockSpec((BLOCK, width), lambda b, g, t: (b, g)),
                pl.BlockSpec((width, BLOCK), lambda b, g, t: (g, b)),
                pl.BlockSpec((BLOCK, 128), lambda b, g, t: (b, 0)),
            ],
            scratch_shapes=[pltpu.VMEM((BLOCK, WINDOWS[-1]), f32)],
        ),
        out_shape=[
            jax.ShapeDtypeStruct((tokens, model), bf16),
            jax.ShapeDtypeStruct((model, tokens), bf16),
            jax.ShapeDtypeStruct((tokens, 128), f32),
        ],
        compiler_params=params(),
        cost_estimate=cost(12e9, 12 * MIB, HEADS * tokens * 384),
        name="attend",
    )(table, q_array, k_array, v_array, own_column, other_row)


def attend_back_kernel(
    causal, table_ref, q_ref, k_ref, v_ref, grad_ref, level_ref, own_ref, other_ref, *rest
):
    if causal:
        out_hbm, out_ref, keys_t, values_t, sems, pair_sems = rest
        pair_hbm, pair_ref, shift = out_hbm, out_ref, HEADS * HEAD_DIM
    else:
        out_hbm, pair_hbm, out_ref, pair_ref, keys_t, values_t, sems, pair_sems = rest
        shift = 0
    block_index = pl.program_id(0)
    group = pl.program_id(1)
    blocks = pl.num_programs(0)
    width = q_ref.shape[1]
    model = HEADS * HEAD_DIM
    rows = pl.ds(pl.multiple_of(group * width, width), width)
    columns = pl.multiple_of(group * width, width)
    owner = lax.broadcasted_iota(jnp.int32, (1, width), 1) // HEAD_DIM
    lane = lax.broadcasted_iota(jnp.int32, (1, 128), 1)

    @pl.when(block_index == 0)
    def _():
        keys_t[rows, :] = jnp.zeros((width, keys_t.shape[1]), f32)
        values_t[rows, :] = jnp.zeros((width, keys_t.shape[1]), f32)

    def body(start, window):
        bias = mask_bias(own_ref, other_ref, start, window, causal)
        queries = q_ref[...] * bf16(HEAD_DIM ** -0.5)
        grads = grad_ref[...]
        queries_t = queries.T
        grads_t = grads.T
        spot = pl.ds(start, window)
        keys = k_ref[spot, :]
        values = v_ref[spot, :]
        levels = level_ref[...]
        grad_q = jnp.zeros(q_ref.shape, f32)
        for head in range(GROUP):
            chosen = owner == head
            picked = chosen.astype(bf16)
            scores = mm_nt(queries * picked, keys) + bias
            level = jnp.sum(
                jnp.where(lane == group * GROUP + head, levels, 0.0), axis=-1, keepdims=True
            )
            probs = jnp.exp(scores - level)
            grad_probs = mm_nt(grads * picked, values)
            inner = jnp.sum(probs * grad_probs, axis=-1, keepdims=True)
            grad_scores = (probs * (grad_probs - inner)).astype(bf16)
            band = slice(head * HEAD_DIM, (head + 1) * HEAD_DIM)
            target_rows = pl.ds(
                pl.multiple_of(group * width + head * HEAD_DIM, HEAD_DIM), HEAD_DIM
            )
            values_t[target_rows, spot] += mm(grads_t[band, :], probs.astype(bf16))
            keys_t[target_rows, spot] += mm(queries_t[band, :], grad_scores)
            grad_q = jnp.where(chosen, mm(grad_scores, keys), grad_q)
        grad_q = (grad_q * HEAD_DIM ** -0.5).astype(bf16)
        own_rows = pl.ds(pl.multiple_of(block_index * BLOCK, BLOCK), BLOCK)
        out_ref[own_rows, pl.ds(columns, width)] = grad_q

    def query_copy(b, g):
        spot = (
            pl.ds(pl.multiple_of(b * BLOCK, BLOCK), BLOCK), pl.ds(pl.multiple_of(g * width, width), width)
        )
        return pltpu.make_async_copy(out_ref.at[spot], out_hbm.at[spot], sems.at[b, g])

    def pair_copy(g, at):
        spot = (
            slice(None), pl.ds(pl.multiple_of(g * width + (shift + at * model), width), width)
        )
        return pltpu.make_async_copy(pair_ref.at[spot], pair_hbm.at[spot], pair_sems.at[g, at])

    for_window(table_ref, body)
    query_copy(block_index, group).start()

    @pl.when(block_index == blocks - 1)
    def _():
        pair_ref[:, pl.ds(columns + shift, width)] = keys_t[rows, :].astype(bf16).T
        pair_ref[:, pl.ds(columns + shift + model, width)] = values_t[rows, :].astype(bf16).T
        pair_copy(group, 0).start()
        pair_copy(group, 1).start()

    @pl.when((block_index == blocks - 1) & (group == pl.num_programs(1) - 1))
    def _():
        for g in range(model // width):
            for b in range(out_ref.shape[0] // BLOCK):
                query_copy(b, g).wait()
            pair_copy(g, 0).wait()
            pair_copy(g, 1).wait()


def attend_back_call(
    table, q_array, q_at, k_array, k_at, v_array, v_at, grad_mix, levels, own_column, other_row, causal
):
    tokens, others = q_array.shape[0], k_array.shape[0]
    width = GROUP * HEAD_DIM
    model = HEADS * HEAD_DIM
    if causal:
        out_shape = [jax.ShapeDtypeStruct((tokens, 3 * model), bf16)]
    else:
        out_shape = [
            jax.ShapeDtypeStruct((tokens, model), bf16),
            jax.ShapeDtypeStruct((others, 2 * model), bf16),
        ]
    return pl.pallas_call(
        functools.partial(attend_back_kernel, causal),
        grid_spec=pltpu.PrefetchScalarGridSpec(
            num_scalar_prefetch=1,
            grid=(tokens // BLOCK, HEADS // GROUP),
            in_specs=[
                pl.BlockSpec((BLOCK, width), lambda b, g, t: (b, q_at + g)),
                pl.BlockSpec((others, width), lambda b, g, t: (0, k_at + g)),
                pl.BlockSpec((others, width), lambda b, g, t: (0, v_at + g)),
                pl.BlockSpec((BLOCK, width), lambda b, g, t: (b, g)),
                pl.BlockSpec((BLOCK, 128), lambda b, g, t: (b, 0)),
                pl.BlockSpec((BLOCK, 1), lambda b, g, t: (b, 0)),
                pl.BlockSpec((1, others), lambda b, g, t: (0, 0)),
            ],
            out_specs=[pl.BlockSpec(memory_space=pl.ANY)] * len(out_shape),
            scratch_shapes=[pltpu.VMEM(item.shape, bf16) for item in out_shape]
            + [pltpu.VMEM((model, others), f32), pltpu.VMEM((model, others), f32)]
            + [pltpu.SemaphoreType.DMA((tokens // BLOCK, HEADS // GROUP)),
               pltpu.SemaphoreType.DMA((HEADS // GROUP, 2))],
        ),
        out_shape=out_shape,
        compiler_params=params(),
        cost_estimate=cost(30e9, 16 * MIB, HEADS * tokens * 384),
        name="attend_back",
    )(table, q_array, k_array, v_array, grad_mix, levels, own_column, other_row)


def middle_kernel(
    mix_ref, target_ref, token_ref, lang_ref, vec_ref, out_weight_ref, query_weight_ref,
    normed_ref, rstd_ref, entry_t_ref, queries_ref,
):
    outer, _, width = out_weight_ref.shape
    start = target_ref[...].astype(f32) + mm(token_ref[...], lang_ref[...])
    mix = mix_ref[...]
    branch = jnp.concatenate([mm(mix, out_weight_ref[o]) for o in range(outer)], axis=1)
    normed, rstd = normalise(2.0 * start + branch)
    normed_ref[...] = normed
    rstd_ref[...] = rstd
    entry = (normed * vec_ref[0:1, :] + vec_ref[3:4, :]).astype(bf16)
    entry_t_ref[...] = entry.T
    for o in range(outer):
        queries_ref[:, o * width:(o + 1) * width] = mm(entry, query_weight_ref[o]).astype(bf16)


def middle_call(mix, target, token_hot, lang_rows, vec, packed, at_self, at_cross, width):
    tokens, model = target.shape
    row = lambda r: (r, 0)
    return pl.pallas_call(
        middle_kernel,
        grid=(tokens // BLOCK,),
        in_specs=[
            pl.BlockSpec((BLOCK, model), row),
            pl.BlockSpec((BLOCK, model), row),
            pl.BlockSpec((BLOCK, 128), row),
            whole(lang_rows.shape),
            whole(vec.shape),
            weight_block(packed, width, at_self),
            weight_block(packed, width, at_cross),
        ],
        out_specs=[
            pl.BlockSpec((BLOCK, model), row),
            pl.BlockSpec((BLOCK, 1), row),
            pl.BlockSpec((model, BLOCK), lambda r: (0, r)),
            pl.BlockSpec((BLOCK, model), row),
        ],
        out_shape=[
            jax.ShapeDtypeStruct((tokens, model), f32),
            jax.ShapeDtypeStruct((tokens, 1), f32),
            jax.ShapeDtypeStruct((model, tokens), bf16),
            jax.ShapeDtypeStruct((tokens, model), bf16),
        ],
        compiler_params=params(),
        cost_estimate=cost(4 * tokens * model * model, 16 * MIB),
        name="middle",
    )(mix, target, token_hot, lang_rows, vec, packed, packed)


def feed_kernel(
    at_cross, at_in, at_out,
    mix_ref, normed_ref, cot_ref, vec_ref, bias_ref, cross_hbm, in_hbm, out_hbm,
    layer_ref, entry_t_ref, act_ref, branch_grad_t_ref, pre_grad_ref, residual_ref, cross_grad_ref,
    mix_grad_ref, sums_ref, bias_sum_ref,
    cross_weight, in_weight, out_weight, slope, sems,
):
    outer, _, width = cross_weight.shape
    chunk = in_weight.shape[2]
    step = pl.program_id(0)

    def cross_copy():
        return pltpu.make_async_copy(
            cross_hbm.at[:, :, pl.ds(at_cross, width)], cross_weight, sems.at[0]
        )

    def in_copy(o):
        return pltpu.make_async_copy(
            in_hbm.at[o, :, pl.ds(at_in, chunk)], in_weight.at[o], sems.at[1 + o]
        )

    def out_copy(o):
        return pltpu.make_async_copy(
            out_hbm.at[o, :, pl.ds(at_out, out_weight.shape[2])], out_weight.at[o],
            sems.at[1 + outer + o],
        )


    @pl.when(step == 0)
    def _():
        cross_copy().start()
        for o in range(outer):
            in_copy(o).start()
            out_copy(o).start()
        sums_ref[...] = jnp.zeros_like(sums_ref)
        bias_sum_ref[...] = jnp.zeros_like(bias_sum_ref)
        cross_copy().wait()

    gain0, gain1, gain2 = vec_ref[0:1, :], vec_ref[1:2, :], vec_ref[2:3, :]
    shift0, shift1, shift2 = vec_ref[3:4, :], vec_ref[4:5, :], vec_ref[5:6, :]
    first = normed_ref[...] * gain0 + shift0
    mix = mix_ref[...]
    branch = jnp.concatenate([mm(mix, cross_weight[o]) for o in range(outer)], axis=1)
    normed1, rstd1 = normalise(2.0 * first + branch)
    second = normed1 * gain1 + shift1
    entry = second.astype(bf16)
    entry_t_ref[...] = entry.T
    total = 2.0 * second + vec_ref[6:7, :]
    for o in range(outer):
        @pl.when(step == 0)
        def _():
            in_copy(o).wait()
            out_copy(o).wait()

        span = slice(o * chunk, (o + 1) * chunk)
        pre = mm(entry, in_weight[o]) + bias_ref[:, span]
        half = 0.5 + 0.5 * lax.erf(pre * (0.5 ** 0.5))
        slope[:, span] = half + pre * (jnp.exp(-0.5 * pre * pre) * 0.3989422804014327)
        act = (pre * half).astype(bf16)
        act_ref[:, span] = act
        total = total + mm(act, out_weight[o])
    normed2, rstd2 = normalise(total)
    layer_ref[...] = (normed2 * gain2 + shift2).astype(bf16)
    cot = cot_ref[...].astype(f32)
    sums_ref[0:1, :] += column_sum(cot * normed2)
    sums_ref[1:2, :] += column_sum(cot)
    back2 = norm_back(cot, gain2, normed2, rstd2)
    branch_grad = back2.astype(bf16)
    branch_grad_t_ref[...] = branch_grad.T
    sums_ref[2:3, :] += column_sum(branch_grad.astype(f32))
    grad_second = 2.0 * back2
    for o in range(outer):
        span = slice(o * chunk, (o + 1) * chunk)
        pre_grad = (mm_nt(branch_grad, out_weight[o]) * slope[:, span]).astype(bf16)
        pre_grad_ref[:, span] = pre_grad
        bias_sum_ref[:, span] += column_sum(pre_grad.astype(f32))
        grad_second = grad_second + mm_nt(pre_grad, in_weight[o])
    sums_ref[3:4, :] += column_sum(grad_second * normed1)
    sums_ref[4:5, :] += column_sum(grad_second)
    back1 = norm_back(grad_second, gain1, normed1, rstd1)
    residual_ref[...] = back1
    cross_grad = back1.astype(bf16)
    cross_grad_ref[...] = cross_grad
    mix_grad = mm_nt(cross_grad[:, 0:width], cross_weight[0])
    for o in range(1, outer):
        mix_grad = mix_grad + mm_nt(
            cross_grad[:, o * width:(o + 1) * width], cross_weight[o]
        )
    mix_grad_ref[...] = mix_grad.astype(bf16)


def feed_call(mix, normed, cot, vec, bias, packed_cross, at_cross, packed_in, at_in, packed_out, at_out, width):
    tokens, model = mix.shape
    hidden = bias.shape[1]
    outer = packed_cross.shape[0]
    chunk = hidden // outer
    row = lambda r: (r, 0)
    blocked = lambda cols: pl.BlockSpec((BLOCK, cols), row)
    anywhere = pl.BlockSpec(memory_space=pl.ANY)
    turned = pl.BlockSpec((model, BLOCK), lambda r: (0, r))
    turned_shape = jax.ShapeDtypeStruct((model, tokens), bf16)
    out = lambda cols, kind: jax.ShapeDtypeStruct((tokens, cols), kind)
    return pl.pallas_call(
        functools.partial(feed_kernel, at_cross, at_in, at_out),
        grid=(tokens // BLOCK,),
        in_specs=[
            blocked(model), blocked(model), blocked(model),
            whole(vec.shape), whole(bias.shape), anywhere, anywhere, anywhere,
        ],
        out_specs=[
            blocked(model), turned, blocked(hidden), turned, blocked(hidden),
            blocked(model), blocked(model), blocked(model),
            pl.BlockSpec((8, model), lambda r: (0, 0)),
            pl.BlockSpec((1, hidden), lambda r: (0, 0)),
        ],
        out_shape=[
            out(model, bf16), turned_shape, out(hidden, bf16), turned_shape,
            out(hidden, bf16), out(model, f32), out(model, bf16), out(model, bf16),
            jax.ShapeDtypeStruct((8, model), f32),
            jax.ShapeDtypeStruct((1, hidden), f32),
        ],
        scratch_shapes=[
            pltpu.VMEM((outer, model, width), bf16),
            pltpu.VMEM((outer, model, chunk), bf16),
            pltpu.VMEM((outer, chunk, model), bf16),
            pltpu.VMEM((BLOCK, hidden), f32),
            pltpu.SemaphoreType.DMA((1 + 2 * outer,)),
        ],
        compiler_params=params(),
        cost_estimate=cost(36 * tokens * model * model, 60 * MIB, tokens * hidden * 2),
        name="feed",
    )(mix, normed, cot, vec, bias, packed_cross, packed_in, packed_out)


def middle_back_kernel(
    outer, residual_ref, queries_grad_ref, normed_ref, rstd_ref, vec_ref, *rest
):
    query_weights, out_weights = rest[:outer], rest[outer:2 * outer]
    start_ref, branch_grad_ref, mix_grad_ref, sums_ref = rest[2 * outer:]
    width = out_weights[0].shape[2]

    @pl.when(pl.program_id(0) == 0)
    def _():
        sums_ref[...] = jnp.zeros_like(sums_ref)

    grad_first = 2.0 * residual_ref[...]
    for o in range(outer):
        grad_first = grad_first + mm_nt(
            queries_grad_ref[:, o * width:(o + 1) * width], query_weights[o][0]
        )
    normed = normed_ref[...]
    sums_ref[0:1, :] += column_sum(grad_first * normed)
    sums_ref[1:2, :] += column_sum(grad_first)
    back = norm_back(grad_first, vec_ref[0:1, :], normed, rstd_ref[...])
    start_ref[...] = back
    branch_grad = back.astype(bf16)
    branch_grad_ref[...] = branch_grad
    mix_grad = mm_nt(branch_grad[:, 0:width], out_weights[0][0])
    for o in range(1, outer):
        mix_grad = mix_grad + mm_nt(
            branch_grad[:, o * width:(o + 1) * width], out_weights[o][0]
        )
    mix_grad_ref[...] = mix_grad.astype(bf16)


def middle_back_call(residual, queries_grad, normed, rstd, vec, packed, at_cross, at_self, width):
    tokens, model = residual.shape
    row = lambda r: (r, 0)
    blocked = pl.BlockSpec((BLOCK, model), row)
    outer = packed.shape[0]
    return pl.pallas_call(
        functools.partial(middle_back_kernel, outer),
        grid=(tokens // BLOCK,),
        in_specs=[
            blocked, blocked, blocked,
            pl.BlockSpec((BLOCK, 1), row),
            whole(vec.shape),
            *weight_slices(packed, width, at_cross),
            *weight_slices(packed, width, at_self),
        ],
        out_specs=[blocked, blocked, blocked, pl.BlockSpec((8, model), lambda r: (0, 0))],
        out_shape=[
            jax.ShapeDtypeStruct((tokens, model), f32),
            jax.ShapeDtypeStruct((tokens, model), bf16),
            jax.ShapeDtypeStruct((tokens, model), bf16),
            jax.ShapeDtypeStruct((8, model), f32),
        ],
        compiler_params=params(),
        cost_estimate=cost(4 * tokens * model * model, 22 * MIB),
        name="middle_back",
    )(residual, queries_grad, normed, rstd, vec, *[packed] * (2 * outer))


def column_copy(source, held, sems, at):
    width = held.shape[2]
    columns = pl.ds(pl.multiple_of(at * width, width), width)
    return pltpu.make_async_copy(source.at[:, columns], held.at[at], sems.at[at])


def half_kernel(count, first, table_ref, *refs):
    lefts, rights = refs[:count], refs[count:2 * count]
    out_ref, held = refs[2 * count], refs[2 * count + 1:3 * count + 1]
    held_rights = refs[3 * count + 1:4 * count + 1]
    sems, right_sems = refs[4 * count + 1], refs[4 * count + 2:]
    part, _, piece, _ = out_ref.shape
    step = pl.program_id(0)

    def copy(at, row):
        source = pl.multiple_of(table_ref[first + row] * piece, piece)
        return pltpu.make_async_copy(
            lefts[at].at[pl.ds(source, piece), :], held[at].at[pl.ds(row * piece, piece), :],
            sems.at[at, row],
        )

    @pl.when(step == 0)
    def _():
        for at in range(count):
            for row in range(part):
                copy(at, row).start()
            column_copy(rights[at], held_rights[at], right_sems[at], 0).start()
        for o in range(1, held_rights[0].shape[0]):
            for at in range(count):
                column_copy(rights[at], held_rights[at], right_sems[at], o).start()

    lo = 0
    for at in range(count):
        @pl.when(step == 0)
        def _():
            for row in range(part):
                copy(at, row).wait()

        column_copy(rights[at], held_rights[at], right_sems[at], step).wait()
        width = held_rights[at].shape[2]
        product = mm(held[at][...], held_rights[at][step]).astype(bf16)
        out_ref[:, 0, :, lo:lo + width] = product.reshape(part, piece, width)
        lo += width


def half_weight_grads(table, lefts, rights, inner, first):
    outer = table.shape[0] - inner
    part, piece = inner // 2, lefts[0].shape[0] // inner
    widths = [right.shape[1] // outer for right in rights]
    flops = sum(right.size for right in rights) * part * piece * 2
    return pl.pallas_call(
        functools.partial(half_kernel, len(lefts), first),
        grid_spec=pltpu.PrefetchScalarGridSpec(
            num_scalar_prefetch=1,
            grid=(outer,),
            in_specs=[pl.BlockSpec(memory_space=pl.ANY)] * (len(lefts) + len(rights)),
            out_specs=pl.BlockSpec(
                (part, 1, piece, sum(widths)), lambda o, table: (0, table[inner + o], 0, 0)
            ),
            scratch_shapes=[pltpu.VMEM((part * piece, left.shape[1]), bf16) for left in lefts]
            + [pltpu.VMEM((outer, right.shape[0], width), bf16) for right, width in zip(rights, widths)]
            + [pltpu.SemaphoreType.DMA((len(lefts), part))]
            + [pltpu.SemaphoreType.DMA((outer,))] * len(rights),
        ),
        out_shape=jax.ShapeDtypeStruct((part, outer, piece, sum(widths)), bf16),
        compiler_params=params(),
        cost_estimate=cost(flops, 12 * MIB),
        name="half_weight_grads",
    )(table, *lefts, *rights)


def next_columns(right_hbm, held, sems):
    step = pl.program_id(0)

    @pl.when(step == 0)
    def _():
        for o in range(held.shape[0]):
            column_copy(right_hbm, held, sems, o).start()

    column_copy(right_hbm, held, sems, step).wait()
    return held[step]


def feed_in_kernel(left_ref, right_hbm, *rest):
    out_ref, held, sems = rest[-3:]
    _, inner, piece, width = out_ref.shape
    product = mm(left_ref[...], next_columns(right_hbm, held, sems)).astype(bf16)
    out_ref[0] = product.reshape(inner, piece, width)


def feed_out_kernel(left_ref, right_hbm, out_ref, held, sems):
    _, inner, piece, width = out_ref.shape
    product = mm(left_ref[...], next_columns(right_hbm, held, sems)).astype(bf16)
    for i in range(inner):
        for b in range(width // piece):
            out_ref[0, i, :, b * piece:(b + 1) * piece] = product[
                b * piece:(b + 1) * piece, i * piece:(i + 1) * piece
            ]


in_place = pl.BlockSpec(memory_space=pl.ANY)


def feed_rows_kernel(left_ref, right_ref, out_ref):
    _, inner, piece, width = out_ref.shape
    product = mm(left_ref[...].T, right_ref[...]).astype(bf16)
    out_ref[0] = product.reshape(inner, piece, width)


def feed_weight_grad(
    kernel, left, left_spec, right, right_spec, outer, inner, piece, width, at, total, held=None
):
    operands, specs = [left, right], [left_spec, right_spec]
    if held is not None:
        operands.append(held)
        specs.append(pl.BlockSpec(memory_space=pl.ANY))
    return pl.pallas_call(
        kernel,
        grid=(outer,),
        scratch_shapes=[
            pltpu.VMEM((outer, right.shape[0], right.shape[1] // outer), bf16),
            pltpu.SemaphoreType.DMA((outer,)),
        ] if right_spec is in_place else [],
        in_specs=specs,
        out_specs=pl.BlockSpec((1, inner, piece, width), lambda o: (o, 0, 0, at)),
        out_shape=jax.ShapeDtypeStruct((outer, inner, piece, total), bf16),
        input_output_aliases={} if held is None else {2: 0},
        compiler_params=params(),
        cost_estimate=cost(8 * left.shape[1] * 1024 * 1024, 24 * MIB),
        name="feed_weight_grad",
    )(*operands)


def entry_back_kernel(
    outer, start_ref, triple_ref, pairs_ref, token_t_ref, *rest
):
    weights, pairs_weights = rest[:outer], rest[outer:2 * outer]
    out_ref, memory_ref, lang_ref = rest[2 * outer:]
    width, pair_width = weights[0].shape[2], pairs_weights[0].shape[2]

    @pl.when(pl.program_id(0) == 0)
    def _():
        lang_ref[...] = jnp.zeros_like(lang_ref)

    grad = 2.0 * start_ref[...]
    for o in range(outer):
        grad = grad + mm_nt(triple_ref[:, o * width:(o + 1) * width], weights[o][0])
    out_ref[...] = grad
    high = grad.astype(bf16)
    rest = grad - high.astype(f32)
    mid = rest.astype(bf16)
    low = (rest - mid.astype(f32)).astype(bf16)
    token_t = token_t_ref[...]
    lang_ref[...] += mm(token_t, high) + mm(token_t, mid) + mm(token_t, low)
    memory_grad = mm_nt(pairs_ref[:, 0:pair_width], pairs_weights[0][0])
    for o in range(1, outer):
        memory_grad = memory_grad + mm_nt(
            pairs_ref[:, o * pair_width:(o + 1) * pair_width], pairs_weights[o][0]
        )
    memory_ref[...] = memory_grad


def entry_back_call(start_grad, triple_grad, pairs_grad, packed, width, pairs_packed, pairs_width, at, token_t):
    tokens, model = start_grad.shape
    outer = packed.shape[0]
    steps = tokens // BLOCK
    memory_block = pairs_grad.shape[0] // steps
    row = lambda r: (r, 0)
    return pl.pallas_call(
        functools.partial(entry_back_kernel, outer),
        grid=(steps,),
        in_specs=[
            pl.BlockSpec((BLOCK, model), row),
            pl.BlockSpec((BLOCK, outer * width), row),
            pl.BlockSpec((memory_block, outer * pairs_width), row),
            pl.BlockSpec((token_t.shape[0], BLOCK), lambda r: (0, r)),
            *weight_slices(packed, width, 0),
            *weight_slices(pairs_packed, pairs_width, at),
        ],
        out_specs=[
            pl.BlockSpec((BLOCK, model), row),
            pl.BlockSpec((memory_block, model), row),
            pl.BlockSpec((token_t.shape[0], model), lambda r: (0, 0)),
        ],
        out_shape=[
            jax.ShapeDtypeStruct((tokens, model), f32),
            jax.ShapeDtypeStruct(pairs_grad.shape[:1] + (model,), f32),
            jax.ShapeDtypeStruct((token_t.shape[0], model), f32),
        ],
        compiler_params=params(),
        cost_estimate=cost(2 * tokens * model * outer * (width + pairs_width // 2), 40 * MIB),
        name="entry_back",
    )(start_grad, triple_grad, pairs_grad, token_t, *[packed] * outer, *[pairs_packed] * outer)


def gather(shard, outer):
    full = lax.all_gather(shard, both, axis=0, tiled=True)
    return full.reshape(outer, full.shape[0] // outer, full.shape[1])


def swap(value, distance, devices):
    return lax.ppermute(value, both, [(d, d ^ distance) for d in range(devices)])


def total_of(pieces, kind):
    total = pieces[0].astype(f32)
    for item in pieces[1:]:
        total = total + item.astype(f32)
    return total.astype(kind)


def hold(*values):
    return lax.optimization_barrier(values)


def core_stage(keep, send, devices):
    moved = swap(send, 1, devices)
    return [total_of((keep[k], moved[k]), keep.dtype) for k in range(keep.shape[0])]


def plane_stage(parts, devices):
    moved = [parts[0]] + [swap(parts[k], 2 * k, devices) for k in range(1, len(parts))]
    return [total_of([item[o] for item in moved], parts[0].dtype) for o in range(parts[0].shape[0])]


def outer_stage(parts, inner, devices):
    moved = [parts[0]] + [swap(parts[k], inner * k, devices) for k in range(1, len(parts))]
    return total_of(moved, f32)


def joint_scatter(packed):
    outer, inner, rows, columns = packed.shape
    flat = packed.reshape(outer * inner * rows, columns)
    return lax.psum_scatter(flat, both, scatter_dimension=0, tiled=True).astype(f32)


def core_halves(keep, send, devices):
    moved = swap(send, 1, devices)
    cut = keep.shape[-1] // 256 * 128
    result = []
    for columns, kept, sent in (
        (slice(0, cut), slice(0, None, 2), slice(1, None, 2)),
        (slice(cut, None), slice(0, 2), slice(2, 4)),
    ):
        for rows in (kept, sent):
            result.append(total_of((keep[rows, ..., columns], moved[rows, ..., columns]), keep.dtype))
    return result


def first_halves(parts, devices):
    keep_x, send_x, keep_y, send_y = parts
    result = []
    for keep, send, distance in ((keep_x, send_x, 2), (keep_y, send_y, 4)):
        moved = swap(send, distance, devices)
        result += [total_of((keep[k], moved[k]), keep.dtype) for k in range(2)]
    return result


def second_halves(parts, devices):
    keep_x, send_x, keep_y, send_y = parts
    moved_x, moved_y = swap(send_x, 4, devices), swap(send_y, 2, devices)
    return [
        jnp.concatenate(
            [total_of((keep_x[o], moved_x[o]), keep_x.dtype),
             total_of((keep_y[o], moved_y[o]), keep_y.dtype)], axis=-1,
        )
        for o in range(keep_x.shape[0])
    ]


def chain_stages(chips):
    if chips == 4:
        return core_halves, first_halves, second_halves
    return core_stage, plane_stage, lambda parts, devices: parts


def permuted_column(shard, outer, inner, devices):
    own = lax.axis_index("outer")
    column = jnp.zeros((outer,) + shard.shape, shard.dtype)
    for k in range(outer):
        moved = swap(shard, inner * k, devices) if k else shard
        column = lax.dynamic_update_slice(column, moved[None], (own ^ k, 0, 0))
    return column


def plane_moves(column, inner, devices):
    return [column] + [swap(column, 2 * k, devices) for k in range(1, inner // 2)]


def plane_place(moves):
    chip = lax.axis_index("inner") // 2
    outer, rows, columns = moves[0].shape
    plane = jnp.zeros((outer, len(moves), rows, columns), moves[0].dtype)
    for k, item in enumerate(moves):
        plane = lax.dynamic_update_slice(plane, item[:, None], (0, chip ^ k, 0, 0))
    return plane


def core_place(plane, moved):
    core = lax.rem(lax.axis_index("inner"), 2)
    mine = jnp.arange(2)[None, None, :, None, None] == core
    full = jnp.where(mine, plane[:, :, None], moved[:, :, None])
    outer, chips, _, rows, columns = full.shape
    return full.reshape(outer, chips * 2 * rows, columns)


def per_device(
    target, memory, cotangent, segment_ids, memory_segments, directions, lang_table,
    self_qkv, self_out, cross_q, cross_kv, cross_out, ffn_in, ffn_in_bias, ffn_out, ffn_out_bias,
    norm_gains, norm_biases,
):
    outer = lax.axis_size("outer")
    inner = lax.axis_size("inner")
    devices = outer * inner
    tokens, model = target.shape
    hidden = devices * ffn_in_bias.shape[0]
    langs = lang_table.shape[1]
    piece = model // devices
    rows = model // inner
    w3, w1, w2, w4 = 3 * model // outer, model // outer, 2 * model // outer, hidden // outer
    ratio = hidden // model
    together = ffn_out.shape[0] == rows and model == w4

    small = jnp.concatenate(
        [
            lang_table.T, norm_gains.T, norm_biases.T,
            ffn_out_bias.reshape(1, piece), ffn_in_bias.reshape(ratio, piece),
        ],
        axis=0,
    )
    n_small = small.shape[0]
    small = jnp.pad(small, ((0, rows - n_small), (0, 128 - piece)))
    first_weights = gather(jnp.concatenate([self_qkv, small], axis=1), outer)
    at_small = w3
    column = permuted_column(
        jnp.concatenate([self_out, cross_q, cross_kv, cross_out], axis=1), outer, inner, devices
    )
    moves = plane_moves(column, inner, devices)
    if together:
        shard, _ = hold(jnp.concatenate([ffn_in, ffn_out], axis=1), column)
        g_in = gather(shard, outer)
        g_out, at_out = g_in, w4
    else:
        g_in = gather(ffn_in, outer)
        g_out, at_out = gather(ffn_out, outer), 0

    first_weights, moves = hold(first_weights, moves)
    plane = plane_place(moves)
    core_move = swap(plane, 1, devices)
    my_inner, my_outer = lax.axis_index("inner"), lax.axis_index("outer")
    outer_places = jnp.arange(outer, dtype=jnp.int32) ^ my_outer
    inner_order = jnp.array(
        [chip * 2 + core for core in range(2) for chip in range(inner // 2)], jnp.int32
    ) ^ my_inner
    table = jnp.concatenate([inner_order, outer_places])
    seg = segment_ids.reshape(-1)
    hot_seg = seg[:, None] == jnp.arange(directions.shape[1])[None, :]
    token_dir = jnp.sum(jnp.where(hot_seg, directions.reshape(1, -1), 0), axis=-1)
    token_hot = (token_dir[:, None] == jnp.arange(128)[None, :]).astype(bf16)
    token_t = (jnp.arange(langs)[:, None] == token_dir[None, :]).astype(bf16)
    own_column = seg[:, None]
    self_table = self_windows(seg)
    cross_table = cross_windows(seg, memory_segments.reshape(-1))

    smalls = first_weights[:, :, at_small:at_small + piece].reshape(devices, rows, piece)[:, :n_small]
    smalls = smalls.transpose(1, 0, 2)
    lang_rows = jnp.pad(smalls[:langs].reshape(langs, model), ((0, 128 - langs), (0, 0)))
    vec = jnp.pad(smalls[langs:langs + 7].reshape(7, model).astype(f32), ((0, 1), (0, 0)))
    in_bias = smalls[langs + 7:].transpose(1, 0, 2).reshape(1, hidden).astype(f32)

    triple, self_entry_t = triple_call(target, token_hot, lang_rows, first_weights, w3, 0)
    triple, core_move = hold(triple, core_move)
    weights = core_place(plane, core_move)
    hg = HEADS // GROUP
    self_mix, self_mix_t, self_levels = attend_call(
        self_table, triple, 0, triple, hg, triple, 2 * hg, own_column, segment_ids, True
    )
    pairs, memory_t = pairs_call(memory, weights, w2, 1)
    normed0, rstd0, cross_entry_t, queries = middle_call(
        self_mix, target, token_hot, lang_rows, vec, weights, 0, 1, w1
    )
    cross_mix, cross_mix_t, cross_levels = attend_call(
        cross_table, queries, 0, pairs, 0, pairs, hg, own_column, memory_segments, False
    )
    (
        layer_output, ffn_entry_t, act, branch_grad_t, pre_grad, residual1, cross_grad,
        cross_mix_grad, sums, bias_sum,
    ) = feed_call(
        cross_mix, normed0, cotangent, vec, in_bias, weights, 2 * w1 + w2, g_in, 0, g_out, at_out, w1
    )

    hidden_step = pl.BlockSpec((tokens, w4), lambda o: (0, o))
    if together:
        ffn_grads = feed_weight_grad(
            feed_out_kernel, branch_grad_t, whole(branch_grad_t.shape), act, in_place,
            outer, inner, rows, model, 1, 2 * w4,
        )
        ffn_grads = [feed_weight_grad(
            feed_in_kernel, ffn_entry_t, whole(ffn_entry_t.shape), pre_grad, in_place,
            outer, inner, rows, w4, 0, 2 * w4, ffn_grads,
        )]
    else:
        branch_grad = branch_grad_t.T
        ffn_grads = [
            feed_weight_grad(
                feed_in_kernel, ffn_entry_t, whole(ffn_entry_t.shape), pre_grad, in_place,
                outer, inner, rows, w4, 0, w4,
            ),
            feed_weight_grad(
                feed_rows_kernel, act, hidden_step, branch_grad, whole(branch_grad.shape),
                outer, inner, ffn_out.shape[0], model, 0, model,
            ),
        ]
    ffn_done = [joint_scatter(item) for item in ffn_grads]
    core, first_plane, second_plane = chain_stages(inner // 2)

    cross_mix_grad, _ = hold(cross_mix_grad, ffn_grads)
    queries_grad, pairs_grad = attend_back_call(
        cross_table, queries, 0, pairs, 0, pairs, hg, cross_mix_grad, cross_levels, own_column, memory_segments, False
    )
    start_grad, self_grad, self_mix_grad, sums0 = middle_back_call(
        residual1, queries_grad, normed0, rstd0, vec, weights, 1, 0, w1
    )
    lefts_a = [memory_t, cross_entry_t, cross_mix_t, self_mix_t]
    rights_a = [pairs_grad, queries_grad, cross_grad, self_grad]
    send_a = half_weight_grads(table, lefts_a, rights_a, inner, inner // 2)
    rights_a, send_a = hold(rights_a, send_a)
    keep_a = half_weight_grads(table, lefts_a, rights_a, inner, 0)
    parts_a = core(keep_a, send_a, devices)
    self_mix_grad, parts_a = hold(self_mix_grad, parts_a)
    (triple_grad,) = attend_back_call(
        self_table, triple, 0, triple, hg, triple, 2 * hg, self_mix_grad, self_levels, own_column, segment_ids, True
    )
    parts_a = first_plane(parts_a, devices)
    triple_grad, parts_a = hold(triple_grad, parts_a)
    send_c = half_weight_grads(table, [self_entry_t], [triple_grad], inner, inner // 2)
    triple_grad, send_c = hold(triple_grad, send_c)
    keep_c = half_weight_grads(table, [self_entry_t], [triple_grad], inner, 0)
    parts_c = core(keep_c, send_c, devices)
    parts_a = second_plane(parts_a, devices)
    triple_grad, parts_c, parts_a = hold(triple_grad, parts_c, parts_a)
    target_grad, memory_grad, lang_sum = entry_back_call(
        start_grad, triple_grad, pairs_grad, first_weights, w3, weights, w2, 1, token_t
    )
    parts_c = first_plane(parts_c, devices)
    done_a = outer_stage(parts_a, inner, devices)
    lang_sum, parts_c, done_a = hold(lang_sum, parts_c, done_a)

    stacked = jnp.concatenate(
        [lang_sum, sums0[0:1], sums[3:4], sums[0:1], sums0[1:2], sums[4:5], sums[1:2], sums[2:3]], axis=0
    )
    stacked = stacked.reshape(langs + 7, devices, piece).transpose(1, 0, 2)
    stacked = jnp.concatenate([stacked, bias_sum.reshape(devices, ratio, piece)], axis=1)
    order = inner_order[:, None] + inner * outer_places[None, :]
    stacked = jnp.take(stacked, order.reshape(-1), axis=0, mode="clip")
    stacked = stacked.reshape(2, inner // 2, outer, n_small, piece)
    parts_e = core_stage(stacked[0], stacked[1], devices)
    parts_c = second_plane(parts_c, devices)
    parts_e, parts_c = hold(parts_e, parts_c)
    parts_e = plane_stage(parts_e, devices)
    done_c = outer_stage(parts_c, inner, devices)
    parts_e, done_c = hold(parts_e, done_c)
    extra = outer_stage(parts_e, inner, devices)
    if together:
        ffn_in_grad = ffn_done[0][:, :w4]
        ffn_out_grad = ffn_done[0][:, w4:].reshape(rows, model // rows, rows)
        ffn_out_grad = ffn_out_grad.transpose(2, 1, 0).reshape(rows, model)
    else:
        ffn_in_grad, ffn_out_grad = ffn_done
    return (
        layer_output,
        target_grad,
        memory_grad,
        extra[:langs].T,
        done_c,
        done_a[:, w2 + 2 * w1:],
        done_a[:, w2:w2 + w1],
        done_a[:, :w2],
        done_a[:, w2 + w1:w2 + 2 * w1],
        ffn_in_grad,
        extra[langs + 7:].reshape(-1),
        ffn_out_grad,
        extra[langs + 6],
        extra[langs:langs + 3].T,
        extra[langs + 3:langs + 6].T,
    )


def solution(mesh):
    rows, cols, line = P(both, None), P("inner", "outer"), P(both)
    return jax.shard_map(
        per_device,
        mesh=mesh,
        in_specs=(
            rows, rows, rows, rows, rows, rows, rows, cols, cols, cols, cols, cols, cols, line, rows,
            line, rows, rows,
        ),
        out_specs=(
            rows, rows, rows, rows, cols, cols, cols, cols, cols, cols, line, rows, line, rows, rows,
        ),
        check_vma=False,
    )
```
